128 devices in a mesh: blk: 16 (over y, z_hi, core), uly: 8 (over z_lo, x).
Axes of the slice: x: 4, y: 4, z: 4 (z_hi: 2, z_lo: 2; z = z_hi * 2 + z_lo), core: 2. Of those that a mesh axis runs over, the one named last changes fastest.
Arguments:
- queries: bfloat16 [16384, 8192], P(('blk', 'uly')), may hold values from -4 to 4, as said below
- key_rows: bfloat16 [16384, 1024], P(('blk', 'uly')), may hold values from -4 to 4, as said below
- value_rows: bfloat16 [16384, 1024], P(('blk', 'uly')), may hold values from -6 to 6
- grad_out: bfloat16 [16384, 8192], P(('blk', 'uly')), may hold values from -6 to 6
- attn_out: bfloat16 [16384, 8192], P(('blk', 'uly')), may hold values from -1.796875 to 1.796875
- log_norm: float32 [16384, 64], P(('blk', 'uly')), may hold values from 5.5 to 8.5
- doc_ids: int32 [16384], replicated, may hold values from 0 to 7, never falling along the last dimension, each value on 1 to 16128 neighbouring positions
Outputs:
- grad_queries: bfloat16 [16384, 8192], P(('blk', 'uly'))
- grad_keys: bfloat16 [16384, 1024], P(('blk', 'uly'))
- grad_values: bfloat16 [16384, 1024], P(('blk', 'uly'))
The draws below stay inside these ranges and needn't reach their ends.
Inputs may be any that keep to these rules, and one draw needn't show every extreme that they name: `queries`: entries of order one. `key_rows`: entries of order one. `doc_ids`: document numbers never fall along positions; a document holds 1 to 16128 positions.
All inputs are finite; a program needn't handle non-finite values.
Results may differ from the reference program's by a relative error of at most 0.0051.
Values may be sent and summed in bfloat16 or wider, within the bound.
No kernel may reach another device: no remote copies, remote signals or barrier semaphores. Data moves between devices by JAX's collectives and lax.ppermute only.
A program may use at most 192 MiB of HBM per device.

```python
import math
import jax
import jax.numpy as jnp
import numpy as np
from jax import lax

NH = 64
KVH = 8
HD = 128
STEPS = 4
GROUPS = 16
GROUP_ROWS = 1024
HALF = 512
SEQ = 16384
NDOCS = 8
MOST_DOC = 16128


def draw_queries(key, part):
    key = jax.random.fold_in(key, 11)
    values = jnp.clip(jax.random.normal(key, (SEQ, NH * HD), jnp.float32), -4.0, 4.0)
    return values.astype(jnp.bfloat16)


def draw_key_rows(key, part):
    key = jax.random.fold_in(key, 12)
    values = jnp.clip(jax.random.normal(key, (SEQ, KVH * HD), jnp.float32), -4.0, 4.0)
    return values.astype(jnp.bfloat16)


def block_levels(rng, extent, pieces, least, top_value):
    loudness = 1.0
    for dim, parts in pieces:
        draws = jax.random.uniform(jax.random.fold_in(jax.random.fold_in(rng, 6), dim), (parts,), jnp.float32, least / len(pieces), top_value / len(pieces))
        loudness = loudness * jnp.repeat(jnp.exp(draws), extent[dim] // parts).reshape((-1,) + (1,) * (len(extent) - 1 - dim))
    return loudness


def profile(amount, total, reach, skew):
    portions = [(1 << 20) // math.isqrt(standing ** skew) + 1 for standing in range(2, amount + 1)]
    surplus, holding = total - reach - (amount - 1), [1] * (amount - 1)
    while surplus > 0:
        movable = [i for i in range(amount - 1) if holding[i] < reach]
        mass, budget = sum([portions[i] for i in movable]), surplus
        for i in movable:
            extra = min(reach - holding[i], max(1, budget * portions[i] // mass), surplus)
            holding[i] = holding[i] + extra
            surplus = surplus - extra
    return np.array([reach] + holding)


def ragged_sizes(stream_key, number_of, total, reach, slope):
    if number_of == 2:
        one = jax.random.randint(stream_key, (), max(1, total - reach), min(reach, total - 1) + 1)
        return jnp.stack([one, total - one])
    sizes = jnp.asarray(profile(number_of, total, reach, slope), jnp.int32)
    pairs = (number_of - 1) // 2
    donor, receiver = sizes[1:1 + 2 * pairs:2], sizes[2:2 + 2 * pairs:2]
    margin = jnp.minimum(donor - 1, reach - receiver)
    passed = jax.random.randint(jax.random.fold_in(stream_key, 1), (pairs,), 0, 1 << 20) % (margin + 1)
    sizes = sizes.at[1:1 + 2 * pairs:2].set(donor - passed).at[2:2 + 2 * pairs:2].set(receiver + passed)
    return sizes[jax.random.permutation(jax.random.fold_in(stream_key, 2), number_of)]


def centred(own_key, dims, spread, limit, shards=(), kind=jnp.bfloat16):
    factor_of = block_levels(own_key, dims, shards, -0.22, 0.18) if shards else 1.0
    result = jax.random.normal(own_key, dims, jnp.float32) * spread * factor_of
    return jnp.minimum(jnp.maximum(result, -limit), limit).astype(kind)


def setup_inputs(seed: int = 0) -> dict:
    streams_of = jax.random.split(jax.random.key(seed), 8)
    queries = draw_queries(jax.random.fold_in(streams_of[7], 71), 0)
    key_rows = draw_key_rows(jax.random.fold_in(streams_of[7], 71), 0)
    value_rows = centred(streams_of[2], (SEQ, KVH * HD), 1.0, 6.0, ((0, 128),))
    grad_out = centred(streams_of[3], (SEQ, NH * HD), 1.0, 6.0, ((0, 128),))
    attn_out = centred(streams_of[4], (SEQ, NH * HD), 0.3, 1.796875, ((0, 128),))
    log_norm = jnp.clip(5.5 + 3.0 * jax.random.uniform(streams_of[5], (SEQ, NH), jnp.float32) ** block_levels(streams_of[5], (SEQ, NH), ((0, 128),), -0.2, 0.2), 5.5, 8.5)
    doc_ids = jnp.searchsorted(jnp.cumsum(ragged_sizes(streams_of[6], NDOCS, SEQ, MOST_DOC, 1)), jnp.arange(SEQ), side="right").astype(jnp.int32)
    return dict(queries=queries, key_rows=key_rows, value_rows=value_rows, grad_out=grad_out, attn_out=attn_out, log_norm=log_norm, doc_ids=doc_ids)


def block_layout(group_index, doc_ids):
    offsets = jnp.arange(HALF, dtype=jnp.int32)
    positions = jnp.concatenate([group_index * HALF + offsets, (2 * GROUPS - 1 - group_index) * HALF + offsets])
    return positions, jnp.take(doc_ids, positions)


def pick_block(blocks, group_index):
    return lax.dynamic_index_in_dim(blocks, group_index, 0, False)


def reference(queries, key_rows, value_rows, grad_out, attn_out, log_norm, doc_ids):
    group_size = NH // KVH
    softmax_scale = HD ** -0.5
    delta = jnp.sum(grad_out.astype(jnp.float32).reshape(SEQ, NH, HD) * attn_out.astype(jnp.float32).reshape(SEQ, NH, HD), axis=-1)
    query_blocks = queries.reshape(GROUPS, GROUP_ROWS, KVH, group_size, HD)
    grad_blocks = grad_out.reshape(GROUPS, GROUP_ROWS, KVH, group_size, HD)
    key_blocks = key_rows.reshape(GROUPS, GROUP_ROWS, KVH, HD)
    value_blocks = value_rows.reshape(GROUPS, GROUP_ROWS, KVH, HD)
    norm_blocks = log_norm.reshape(GROUPS, GROUP_ROWS, KVH, group_size)
    delta_blocks = delta.reshape(GROUPS, GROUP_ROWS, KVH, group_size)

    def one_group(carry, group_index):
        grad_keys, grad_values = carry
        query_g = pick_block(query_blocks, group_index).astype(jnp.float32)
        grad_g = pick_block(grad_blocks, group_index).astype(jnp.float32)
        norm_g = jnp.transpose(pick_block(norm_blocks, group_index), (1, 2, 0))[..., None]
        delta_g = jnp.transpose(pick_block(delta_blocks, group_index), (1, 2, 0))[..., None]
        query_spots, query_docs = block_layout(group_index, doc_ids)
        grad_query = jnp.zeros((GROUP_ROWS, KVH, group_size, HD), jnp.float32)
        for visit_step in range(STEPS):
            key_group = ((group_index - visit_step) % GROUPS).astype(jnp.int32)
            key_g = pick_block(key_blocks, key_group).astype(jnp.float32)
            value_g = pick_block(value_blocks, key_group).astype(jnp.float32)
            key_spots, key_docs = block_layout(key_group, doc_ids)
            allowed = (query_spots[:, None] >= key_spots[None, :]) & (query_docs[:, None] == key_docs[None, :])
            scores = jnp.einsum("qcgh,kch->cgqk", query_g, key_g) * softmax_scale
            attn_prob = jnp.where(allowed, jnp.exp(scores - norm_g), 0.0)
            prob_round = lax.optimization_barrier(attn_prob.astype(jnp.bfloat16)).astype(jnp.float32)
            value_part = jnp.einsum("cgqk,qcgh->kch", prob_round, grad_g)
            grad_prob = jnp.einsum("qcgh,kch->cgqk", grad_g, value_g)
            score_round = lax.optimization_barrier((attn_prob * (grad_prob - delta_g)).astype(jnp.bfloat16)).astype(jnp.float32)
            grad_query = grad_query + softmax_scale * jnp.einsum("cgqk,kch->qcgh", score_round, key_g)
            key_part = softmax_scale * jnp.einsum("cgqk,qcgh->kch", score_round, query_g)
            grad_keys = grad_keys.at[key_group].add(key_part)
            grad_values = grad_values.at[key_group].add(value_part)
        return (grad_keys, grad_values), grad_query.astype(jnp.bfloat16)

    empty = jnp.zeros((GROUPS, GROUP_ROWS, KVH, HD), jnp.float32)
    sums, grad_query = lax.scan(one_group, (empty, empty), jnp.arange(GROUPS, dtype=jnp.int32))
    grad_keys, grad_values = sums
    return (grad_query.reshape(SEQ, NH * HD), grad_keys.astype(jnp.bfloat16).reshape(SEQ, KVH * HD), grad_values.astype(jnp.bfloat16).reshape(SEQ, KVH * HD))
```

```python
import functools
import math

import jax
import jax.numpy as jnp
from jax import lax
from jax.experimental import pallas as pl
from jax.experimental.pallas import tpu as pltpu
from jax.sharding import PartitionSpec as P

HD = 128
STEPS = 4
DOCS = 8
TOK = 128
HEADS_DEV = 8
HALF = 512
CHUNKS = (4, 4)
PARTS = 3
FAR = 32768.0
SCALE = HD ** (-0.5)
EXP2_SCALE = SCALE * math.log2(math.e)
NORM_SCALE = HD ** 0.5
BF = jnp.bfloat16
F32 = jnp.float32
VMEM_LIMIT = 60 * 1024 * 1024

NN = (((1,), (0,)), ((), ()))
NT = (((1,), (1,)), ((), ()))


def dot(a, b, dims=NN):
    return lax.dot_general(a, b, dims, preferred_element_type=F32)


def three_parts(x, first, second):
    high = x.astype(BF).astype(F32)
    rest = x - high
    mid = rest.astype(BF).astype(F32)
    low = rest - mid
    return jnp.where(first, high, jnp.where(second, mid, low))


def pack_kernel(q_ref, do_ref, o_ref, k_ref, v_ref, ln_ref, doc_ref, kvs_ref, *qd_refs):
    u = pl.program_id(0)
    lane = lax.broadcasted_iota(jnp.int32, (TOK, 128), 1)
    ln_lane = lax.broadcasted_iota(jnp.int32, (TOK, ln_ref.shape[1]), 1)
    norm = ln_ref[...] * NORM_SCALE
    block = jnp.zeros((TOK, 128), F32)
    for h in range(HEADS_DEV):
        cols = slice(h * HD, (h + 1) * HD)
        delta = jnp.sum(
            do_ref[:, cols].astype(F32) * o_ref[:, cols].astype(F32), axis=1, keepdims=True
        )
        norm_h = jnp.sum(
            jnp.where(ln_lane == u * HEADS_DEV + h, norm, 0.0), axis=1, keepdims=True
        )
        mine = lane % HEADS_DEV == h
        block = jnp.where(mine & (lane < 24), norm_h, block)
        block = jnp.where(mine & (lane >= 24) & (lane < 48), delta, block)
    part = (lane // HEADS_DEV) % PARTS
    block = three_parts(block, part == 0, part == 1)
    kvs_ref[0, 0] = k_ref[...].T
    kvs_ref[0, 1] = v_ref[...].T
    kvs_ref[0, 2] = jnp.where(lane < 48, block, doc_ref[...]).astype(BF)
    h = 0
    for ref in qd_refs:
        count = ref.shape[1] // 2
        for i in range(count):
            cols = slice(h * HD, (h + 1) * HD)
            ref[0, i] = q_ref[:, cols]
            ref[0, count + i] = do_ref[:, cols]
            h += 1


def pack(queries, grad_out, attn_out, key_rows, value_rows, log_norm, doc_block):
    width = HEADS_DEV * HD
    wide = pl.BlockSpec((TOK, width), lambda u: (0, u))
    thin = pl.BlockSpec((TOK, HD), lambda u: (0, u))
    shapes = [(8, 3, TOK, HD)] + [(8, 2 * c, TOK, HD) for c in CHUNKS]
    return pl.pallas_call(
        pack_kernel,
        grid=(8,),
        in_specs=[
            wide,
            wide,
            wide,
            thin,
            thin,
            pl.BlockSpec(log_norm.shape, lambda u: (0, 0)),
            pl.BlockSpec(doc_block.shape, lambda u: (0, 0)),
        ],
        out_specs=[pl.BlockSpec((1,) + s[1:], lambda u: (u, 0, 0, 0)) for s in shapes],
        out_shape=[jax.ShapeDtypeStruct(s, BF) for s in shapes],
        compiler_params=pltpu.CompilerParams(vmem_limit_bytes=VMEM_LIMIT),
        cost_estimate=pl.CostEstimate(flops=0, bytes_accessed=11 << 20, transcendentals=0),
        name="pack",
    )(queries, grad_out, attn_out, key_rows, value_rows, log_norm, doc_block)


def attend_kernel(first_head, count, has_sum, *refs):
    second_ref, qd_ref, kvs_ref, kv1_ref, kv2_ref, kv3_ref, kdoc_ref = refs[:7]
    refs = refs[7:]
    if has_sum:
        sum_ref, refs = refs[0], refs[1:]
    dq_ref, dkv_ref, qt_ref, dot_ref, dqt_ref, sel_ref = refs
    kv_refs = (kvs_ref, kv1_ref, kv2_ref, kv3_ref)

    row = lax.broadcasted_iota(jnp.int32, (48, HALF), 0)
    for h in range(count):
        mine = row % HEADS_DEV == first_head + h
        sel_ref[h] = jnp.where(mine & (row < 24), -1.0, 0.0).astype(BF)
        sel_ref[count + h] = jnp.where(mine & (row >= 24), -1.0, 0.0).astype(BF)
    for half in range(2):
        for h in range(count):
            for i in range(4):
                cols = slice(i * TOK, (i + 1) * TOK)
                qt_ref[half, h, :, cols] = qd_ref[half * 4 + i, h].T
                dot_ref[half, h, :, cols] = qd_ref[half * 4 + i, count + h].T
    dqt_ref[...] = jnp.zeros_like(dqt_ref)
    if has_sum:
        dkv_ref[...] = sum_ref[...]
    else:
        dkv_ref[...] = jnp.zeros_like(dkv_ref)

    def rows_of(qhalf, index, q0, qn):
        block = qd_ref[pl.ds(qhalf * 4 + q0 // TOK, qn // TOK), index]
        return block.reshape(qn, HD)

    def tile(step, qhalf, khalf, pieces):
        kv_ref = kv_refs[step]
        kt_all = jnp.concatenate([kv_ref[khalf * 4 + i, 0] for i in range(4)], axis=1)
        vt_all = jnp.concatenate([kv_ref[khalf * 4 + i, 1] for i in range(4)], axis=1)
        docs_all = kdoc_ref[step, khalf]
        for q0, qn, kn, diagonal in pieces:
            kt, vt, docs = kt_all[:, :kn], vt_all[:, :kn], docs_all[:, :kn]
            stats = kvs_ref[pl.ds(qhalf * 4 + q0 // TOK, qn // TOK), 2].reshape(qn, HD)
            dk_sum = jnp.zeros((HD, kn), F32)
            dv_sum = jnp.zeros((HD, kn), F32)
            for h in range(count):
                k_ext = jnp.concatenate(
                    [kt, sel_ref[h, :, :kn], docs, jnp.zeros((64, kn), BF)], axis=0
                )
                v_ext = jnp.concatenate(
                    [vt, sel_ref[count + h, :, :kn], jnp.zeros((80, kn), BF)], axis=0
                )
                q_ext = jnp.concatenate([rows_of(qhalf, h, q0, qn), stats], axis=1)
                do_ext = jnp.concatenate([rows_of(qhalf, count + h, q0, qn), stats], axis=1)
                prob = jnp.exp2(dot(q_ext, k_ext) * EXP2_SCALE)
                if diagonal:
                    qi = lax.broadcasted_iota(jnp.int32, (qn, kn), 0) + q0
                    ki = lax.broadcasted_iota(jnp.int32, (qn, kn), 1)
                    prob = jnp.where(qi >= ki, prob, 0.0)
                dscore = (prob * dot(do_ext, v_ext)).astype(BF)
                prob = prob.astype(BF)
                span = slice(q0, q0 + qn)
                dv_sum += dot(dot_ref[qhalf, h, :, span], prob)
                dk_sum += dot(qt_ref[qhalf, h, :, span], dscore)
                dqt_ref[qhalf, h, :, span] += dot(kt, dscore, NT)
            dkv_ref[step, 0, khalf, :, :kn] += dk_sum
            dkv_ref[step, 1, khalf, :, :kn] += dv_sum

    full = ((0, HALF, HALF, False),)
    corner = ((0, HALF // 2, HALF // 2, True), (HALF // 2, HALF // 2, HALF, True))

    def diagonal(half, carry):
        tile(0, half, half, corner)
        return carry

    lax.fori_loop(0, 2, diagonal, 0)
    tile(0, 1, 0, full)
    for step in range(1, STEPS):

        def both(index, carry, step=step):
            second = second_ref[step]
            tile(step, jnp.where(index == 0, 1, second), jnp.where(index == 0, 0, second), full)
            return carry

        lax.fori_loop(0, 2, both, 0)

    for half in range(2):
        for h in range(count):
            for i in range(4):
                piece = dqt_ref[half, h, :, i * TOK : (i + 1) * TOK]
                dq_ref[half * 4 + i, h] = (piece * SCALE).T.astype(BF)


def attend(first_head, second, qd, kvs, kvs_others, kdoc, dkv):
    count = qd.shape[1] // 2
    has_sum = dkv is not None
    operands = [second, qd, kvs, *kvs_others, kdoc] + ([dkv] if has_sum else [])
    vmem = pl.BlockSpec(memory_space=pltpu.VMEM)
    flops = 9 * 5 * 2 * HALF * HALF * HD * count
    return pl.pallas_call(
        functools.partial(attend_kernel, first_head, count, has_sum),
        in_specs=[pl.BlockSpec(memory_space=pltpu.SMEM)] + [vmem] * (len(operands) - 1),
        out_specs=[vmem, vmem],
        out_shape=[
            jax.ShapeDtypeStruct((8, count, TOK, HD), BF),
            jax.ShapeDtypeStruct((STEPS, 2, 2, HD, HALF), F32),
        ],
        scratch_shapes=[
            pltpu.VMEM((2, count, HD, HALF), BF),
            pltpu.VMEM((2, count, HD, HALF), BF),
            pltpu.VMEM((2, count, HD, HALF), F32),
            pltpu.VMEM((2 * count, 48, HALF), BF),
        ],
        compiler_params=pltpu.CompilerParams(vmem_limit_bytes=VMEM_LIMIT),
        cost_estimate=pl.CostEstimate(
            flops=2 * flops, bytes_accessed=8 << 20, transcendentals=9 * HALF * HALF * count
        ),
        name="attend",
    )(*operands)


def split_kernel(dkv_ref, own_ref, one_ref, two_ref, three_ref):
    for step, ref in ((1, one_ref), (2, two_ref), (3, three_ref)):
        ref[0] = (dkv_ref[step, 0] * SCALE).astype(BF)
        ref[1] = dkv_ref[step, 1].astype(BF)
    own_ref[0] = dkv_ref[0, 0] * SCALE
    own_ref[1] = dkv_ref[0, 1]


def split(dkv):
    shape = (2, 2, HD, HALF)
    return pl.pallas_call(
        split_kernel,
        out_shape=[jax.ShapeDtypeStruct(shape, F32)] + [jax.ShapeDtypeStruct(shape, BF)] * 3,
        compiler_params=pltpu.CompilerParams(vmem_limit_bytes=VMEM_LIMIT),
        name="split",
    )(dkv)


def total_kernel(own_ref, one_ref, two_ref, three_ref, out_ref):
    for pair in range(2):
        for half in range(2):
            total = (
                own_ref[pair, half]
                + one_ref[pair, half].astype(F32)
                + two_ref[pair, half].astype(F32)
                + three_ref[pair, half].astype(F32)
            )
            for i in range(4):
                out_ref[half * 4 + i, pair] = total[:, i * TOK : (i + 1) * TOK].T.astype(BF)


def total(own, one, two, three):
    return pl.pallas_call(
        total_kernel,
        out_shape=jax.ShapeDtypeStruct((8, 2, TOK, HD), BF),
        compiler_params=pltpu.CompilerParams(vmem_limit_bytes=VMEM_LIMIT),
        name="total",
    )(own, one, two, three)


def unpack_q_kernel(*refs):
    out_ref = refs[-1]
    h = 0
    for ref in refs[:-1]:
        for i in range(ref.shape[1]):
            out_ref[:, h * HD : (h + 1) * HD] = ref[0, i]
            h += 1


def unpack_q(parts):
    return pl.pallas_call(
        unpack_q_kernel,
        grid=(8,),
        in_specs=[pl.BlockSpec((1,) + p.shape[1:], lambda u: (u, 0, 0, 0)) for p in parts],
        out_specs=pl.BlockSpec((TOK, HEADS_DEV * HD), lambda u: (0, u)),
        out_shape=jax.ShapeDtypeStruct((TOK, 8 * HEADS_DEV * HD), BF),
        compiler_params=pltpu.CompilerParams(vmem_limit_bytes=VMEM_LIMIT),
        name="unpack_q",
    )(*parts)


def unpack_kv_kernel(pair_ref, k_ref, v_ref):
    for u in range(8):
        k_ref[:, u * HD : (u + 1) * HD] = pair_ref[u, 0]
        v_ref[:, u * HD : (u + 1) * HD] = pair_ref[u, 1]


def unpack_kv(pair):
    shape = jax.ShapeDtypeStruct((TOK, 8 * HD), BF)
    return pl.pallas_call(
        unpack_kv_kernel,
        out_shape=[shape, shape],
        compiler_params=pltpu.CompilerParams(vmem_limit_bytes=VMEM_LIMIT),
        name="unpack_kv",
    )(pair)


def shift(value, axis, steps):
    count = lax.axis_size(axis)
    pairs = [(source, (source + steps) % count) for source in range(count)]
    return lax.ppermute(value, axis, pairs)


def exchange(value):
    return lax.all_to_all(value, "uly", split_axis=0, concat_axis=0, tiled=True)


def local(queries, key_rows, value_rows, grad_out, attn_out, log_norm, doc_ids):
    groups = lax.axis_size("blk")
    group = lax.axis_index("blk")
    member = lax.axis_index("uly")

    first = jnp.where(
        member < 4, group * HALF + member * TOK, (2 * groups - 1 - group) * HALF + (member - 4) * TOK
    )
    my_docs = lax.dynamic_slice_in_dim(doc_ids, first, TOK)
    lane = jnp.arange(128, dtype=jnp.int32)[None, :]
    doc_block = jnp.where(
        (lane >= 48) & (lane < 48 + DOCS) & (my_docs[:, None] != lane - 48), FAR, 0.0
    ).astype(F32)

    kdocs = []
    for step in range(STEPS):
        owner = (group - step) % groups
        low = lax.dynamic_slice_in_dim(doc_ids, owner * HALF, HALF)
        high = lax.dynamic_slice_in_dim(doc_ids, (2 * groups - 1 - owner) * HALF, HALF)
        kdocs.append(jnp.stack([low, high]))
    kdocs = jnp.stack(kdocs)
    kdoc = jnp.where(
        kdocs[:, :, None, :] == jnp.arange(16, dtype=jnp.int32)[None, None, :, None], -1.0, 0.0
    ).astype(BF)
    second = jnp.where(group >= jnp.arange(STEPS), 0, 1).astype(jnp.int32)

    kvs, *qds = pack(queries, grad_out, attn_out, key_rows, value_rows, log_norm, doc_block)
    kvs = exchange(kvs)
    visiting = kvs[:, :2]
    others = []
    for _ in range(1, STEPS):
        visiting = shift(visiting, "blk", 1)
        others.append(visiting)

    dkv = None
    head = 0
    dqs = []
    for qd in qds:
        qd = exchange(qd)
        dq, dkv = attend(head, second, qd, kvs, others, kdoc, dkv)
        head += qd.shape[1] // 2
        dqs.append(exchange(dq))

    own, *sends = split(dkv)
    back = [shift(part, "blk", -step) for step, part in enumerate(sends, start=1)]
    pair = exchange(total(own, *back))
    grad_keys, grad_values = unpack_kv(pair)
    return unpack_q(dqs), grad_keys, grad_values


def solution(mesh):
    rows = P(("blk", "uly"), None)
    return jax.shard_map(
        local,
        mesh=mesh,
        in_specs=(rows, rows, rows, rows, rows, rows, P()),
        out_specs=(rows, rows, rows),
        check_vma=False,
    )
```

```python
import functools
import math

import jax
import jax.numpy as jnp
from jax import lax
from jax.experimental import pallas as pl
from jax.experimental.pallas import tpu as pltpu
from jax.sharding import PartitionSpec as P

HD = 128
STEPS = 4
DOCS = 8
TOK = 128
HEADS_DEV = 8
HALF = 512
CHUNKS = (3, 3, 2)
PARTS = 3
FAR = 32768.0
SCALE = HD ** (-0.5)
EXP2_SCALE = SCALE * math.log2(math.e)
NORM_SCALE = HD ** 0.5
BF = jnp.bfloat16
F32 = jnp.float32
BM, BN, PIPE = 256, 256, True
BM, BN = 256, 256
PACK_PER = 4
VMEM_LIMIT = 60 * 1024 * 1024

NN = (((1,), (0,)), ((), ()))
NT = (((1,), (1,)), ((), ()))


def dot(a, b, dims=NN):
    return lax.dot_general(a, b, dims, preferred_element_type=F32)


def parts_of(x):
    high = x.astype(BF)
    rest = x - high.astype(F32)
    mid = rest.astype(BF)
    low = (rest - mid.astype(F32)).astype(BF)
    return high, mid, low


def pack_kv_kernel(k_ref, v_ref, kv_ref):
    for u in range(8):
        kv_ref[u, 0] = k_ref[:, u * HD : (u + 1) * HD].T
        kv_ref[u, 1] = v_ref[:, u * HD : (u + 1) * HD].T


def pack_kv(key_rows, value_rows):
    return pl.pallas_call(
        pack_kv_kernel,
        out_shape=jax.ShapeDtypeStruct((8, 2, HD, TOK), BF),
        compiler_params=pltpu.CompilerParams(vmem_limit_bytes=VMEM_LIMIT),
        cost_estimate=pl.CostEstimate(flops=0, bytes_accessed=1 << 20, transcendentals=0),
        name="pack_kv",
    )(key_rows, value_rows)


def pack_q_kernel(per, q_ref, do_ref, o_ref, ln_ref, doc_ref, _, *refs):
    *qd_refs, pick_ref = refs
    step = pl.program_id(0)
    heads = ln_ref.shape[1]
    width = HEADS_DEV * HD

    @pl.when(step == 0)
    def _():
        head = lax.broadcasted_iota(jnp.int32, pick_ref.shape, 0) // HD
        col = lax.broadcasted_iota(jnp.int32, pick_ref.shape, 1)
        pick = (col >= 24) & (col < 48) & (head == col % HEADS_DEV)
        pick_ref[...] = jnp.where(pick, 1.0, 0.0).astype(BF)

    head = lax.broadcasted_iota(jnp.int32, (heads, 128), 0)
    col = lax.broadcasted_iota(jnp.int32, (heads, 128), 1)
    lane = lax.broadcasted_iota(jnp.int32, (TOK, 128), 1)
    norm_parts = parts_of(ln_ref[...] * NORM_SCALE)
    for i in range(per):
        first = i * width
        norm = jnp.zeros((TOK, 128), F32)
        for j, part in enumerate(norm_parts):
            mine = head == (step * per + i) * HEADS_DEV + col % HEADS_DEV
            pick = (col // HEADS_DEV == j) & mine
            norm += dot(part, jnp.where(pick, 1.0, 0.0).astype(BF))
        cols = slice(first, first + width)
        high, low, _ = parts_of(do_ref[:, cols].astype(F32) * o_ref[:, cols].astype(F32))
        delta = dot(high, pick_ref[...]) + dot(low, pick_ref[...])
        high, mid, low = parts_of(delta)
        delta = jnp.where(lane < 32, high, jnp.where(lane < 40, mid, low))
        stats = jnp.where(lane < 24, norm.astype(BF), jnp.where(lane < 48, delta, doc_ref[...]))
        h = 0
        for index, ref in enumerate(qd_refs):
            count = ref.shape[1] // 2
            for c in range(count):
                cols = slice(first + h * HD, first + (h + 1) * HD)
                ref[i, c] = q_ref[:, cols]
                ref[i, count + c] = do_ref[:, cols]
                h += 1
            if index == 0:
                ref[i, 2 * count] = stats


def pack_q(queries, grad_out, attn_out, log_norm, doc_block, after):
    per = PACK_PER
    wide = pl.BlockSpec((TOK, per * HEADS_DEV * HD), lambda u: (0, u))
    shapes = [(8, 2 * c + (i == 0), TOK, HD) for i, c in enumerate(CHUNKS)]
    return pl.pallas_call(
        functools.partial(pack_q_kernel, per),
        grid=(8 // per,),
        in_specs=[
            wide,
            wide,
            wide,
            pl.BlockSpec(log_norm.shape, lambda u: (0, 0)),
            pl.BlockSpec(doc_block.shape, lambda u: (0, 0)),
            pl.BlockSpec(memory_space=pl.ANY),
        ],
        out_specs=[pl.BlockSpec((per,) + s[1:], lambda u: (u, 0, 0, 0)) for s in shapes],
        out_shape=[jax.ShapeDtypeStruct(s, BF) for s in shapes],
        scratch_shapes=[pltpu.VMEM((HEADS_DEV * HD, 128), BF)],
        compiler_params=pltpu.CompilerParams(vmem_limit_bytes=VMEM_LIMIT),
        cost_estimate=pl.CostEstimate(flops=0, bytes_accessed=11 << 20, transcendentals=0),
        name="pack_q",
    )(queries, grad_out, attn_out, log_norm, doc_block, after)


def attend_kernel(steps, count, first_head, kv_counts, has_dkv, has_dq, afters, last_dq, last_dkv, *refs):
    refs = list(refs)

    def take(n):
        head = refs[:n]
        del refs[:n]
        return head

    second_ref, qd_ref, stat_ref = take(3)
    kv_refs = [take(n) for n in kv_counts]
    (kdoc_ref,) = take(1)
    dkv_in = take(len(steps)) if has_dkv else None
    (dq_in,) = take(1) if has_dq else (None,)
    take(afters)
    (dq_ref,) = take(1)
    dkv_refs = take(len(steps))
    qt_ref, dot_ref, sel_ref, kv_ref, p_ref, ds_ref = take(6)
    (dqt_ref,) = take(1) if last_dq else (dq_ref,)
    sum_refs = take(len(steps)) if last_dkv else dkv_refs

    row = lax.broadcasted_iota(jnp.int32, (48, HALF), 0)
    for h in range(count):
        mine = row % HEADS_DEV == first_head + h
        sel_ref[h] = jnp.where(mine & (row < 24), -1.0, 0.0).astype(BF)
        sel_ref[count + h] = jnp.where(mine & (row >= 24), -1.0, 0.0).astype(BF)
    for half in range(2):
        for i in range(4):
            cols = slice(i * TOK, (i + 1) * TOK)
            for index, sources in enumerate(kv_refs):
                for pair in range(2):
                    block = sources[0][half * 4 + i, pair]
                    for other in sources[1:]:
                        block = block + other[half * 4 + i, pair]
                    kv_ref[index, pair, half, :, cols] = block
    if has_dq:
        dqt_ref[...] = dq_in[...]
    else:
        dqt_ref[...] = jnp.zeros_like(dqt_ref)
    for index in range(len(steps)):
        if has_dkv:
            sum_refs[index][...] = dkv_in[index][...]
        else:
            sum_refs[index][...] = jnp.zeros_like(sum_refs[index])

    def turn_rows(half):
        for i in range(4):
            cols = slice(i * TOK, (i + 1) * TOK)
            for h in range(count):
                qt_ref[half, h, :, cols] = qd_ref[half * 4 + i, h].T
                dot_ref[half, h, :, cols] = qd_ref[half * 4 + i, count + h].T

    def rows_of(qhalf, index, q0, qn):
        block = qd_ref[pl.ds(qhalf * 4 + q0 // TOK, qn // TOK), index]
        return block.reshape(qn, HD)

    def scores(index, qhalf, khalf, h, slot, q0, k0, bm, bn, diagonal):
        kcols = slice(k0, k0 + bn)
        k_ext = jnp.concatenate(
            [
                kv_ref[index, 0, khalf, :, kcols],
                sel_ref[h, :, kcols],
                kdoc_ref[steps[index], khalf, :, kcols],
                jnp.zeros((64, bn), BF),
            ],
            axis=0,
        )
        v_ext = jnp.concatenate(
            [kv_ref[index, 1, khalf, :, kcols], sel_ref[count + h, :, kcols], jnp.zeros((80, bn), BF)],
            axis=0,
        )
        stats = stat_ref[pl.ds(qhalf * 4 + q0 // TOK, bm // TOK), 0].reshape(bm, HD)
        q_ext = jnp.concatenate([rows_of(qhalf, h, q0, bm), stats], axis=1)
        do_ext = jnp.concatenate([rows_of(qhalf, count + h, q0, bm), stats], axis=1)
        prob = jnp.exp2(dot(q_ext, k_ext) * EXP2_SCALE)
        if diagonal:
            qi = lax.broadcasted_iota(jnp.int32, (bm, bn), 0) + q0
            ki = lax.broadcasted_iota(jnp.int32, (bm, bn), 1) + k0
            prob = jnp.where(qi >= ki, prob, 0.0)
        rows = slice(q0, q0 + bm)
        ds_ref[slot, rows, kcols] = (prob * dot(do_ext, v_ext)).astype(BF)
        p_ref[slot, rows, kcols] = prob.astype(BF)

    def grads(index, qhalf, khalf, h, slot, diagonal):
        for k0, kn, q0 in ((0, 256, 0), (256, 256, 256)) if diagonal else ((0, HALF, 0),):
            span = slice(q0, HALF)
            cols = slice(k0, k0 + kn)
            sum_refs[index][1, khalf, :, cols] += dot(dot_ref[qhalf, h, :, span], p_ref[slot, span, cols])
            sum_refs[index][0, khalf, :, cols] += dot(qt_ref[qhalf, h, :, span], ds_ref[slot, span, cols])
        for q0, qn, kn in ((0, 256, 256), (256, 256, 512)) if diagonal else ((0, HALF, HALF),):
            span = slice(q0, q0 + qn)
            dqt_ref[qhalf, h, :, span] += dot(kv_ref[index, 0, khalf, :, :kn], ds_ref[slot, span, :kn], NT)

    def tile(index, qhalf, khalf, diagonal):
        for h in range(count):
            for k0 in range(0, HALF, BN):
                for q0 in range(0, HALF, BM):
                    if diagonal and q0 + BM <= k0:
                        if q0 >= k0 // 256 * 256:
                            ds_ref[h % 2, q0 : q0 + BM, k0 : k0 + BN] = jnp.zeros((BM, BN), BF)
                            p_ref[h % 2, q0 : q0 + BM, k0 : k0 + BN] = jnp.zeros((BM, BN), BF)
                        continue
                    scores(index, qhalf, khalf, h, h % 2, q0, k0, BM, BN, diagonal and q0 < k0 + BN)
            if PIPE and h > 0:
                grads(index, qhalf, khalf, h - 1, (h - 1) % 2, diagonal)
            if not PIPE:
                grads(index, qhalf, khalf, h, h % 2, diagonal)
        if PIPE:
            grads(index, qhalf, khalf, count - 1, (count - 1) % 2, diagonal)

    for index, step in enumerate(steps):
        if step == 0:

            def diagonal(half, carry, index=index):
                if index == 0:
                    turn_rows(half)
                tile(index, half, half, True)
                return carry

            lax.fori_loop(0, 2, diagonal, 0)
            tile(index, 1, 0, False)
        else:

            def both(turn, carry, index=index, step=step):
                second = second_ref[step]
                if index == 0:
                    turn_rows(1 - turn)
                tile(index, jnp.where(turn == 0, 1, second), jnp.where(turn == 0, 0, second), False)
                return carry

            lax.fori_loop(0, 2, both, 0)

    if last_dq:
        for half in range(2):
            for h in range(count):
                for i in range(4):
                    piece = dqt_ref[half, h, :, i * TOK : (i + 1) * TOK]
                    dq_ref[half * 4 + i, h] = (piece * SCALE).astype(BF).T
    if last_dkv:
        for total_ref, sum_ref in zip(dkv_refs, sum_refs):
            total_ref[0] = (sum_ref[0] * SCALE).astype(total_ref.dtype)
            total_ref[1] = sum_ref[1].astype(total_ref.dtype)


def attend(steps, chunk, second, qd, stats, kvs, kdoc, dkv, dq, last_dq, dkv_type, afters=()):
    first_head, count = sum(CHUNKS[:chunk]), CHUNKS[chunk]
    operands = [second, qd, stats]
    kvs = [kvs[step] for step in steps]
    for sources in kvs:
        operands += sources
    operands.append(kdoc)
    operands += [] if dkv is None else [dkv[step] for step in steps]
    operands += [] if dq is None else [dq]
    vmem = pl.BlockSpec(memory_space=pltpu.VMEM)
    stat_index = stats.shape[1] - 1
    stat_spec = pl.BlockSpec((8, 1, TOK, HD), lambda i: (0, stat_index, 0, 0))
    tiles = sum(2.5 if step == 0 else 2 for step in steps)
    flops = int(tiles * 5 * 2 * HALF * HALF * HD * count)
    partial_dq = (2, count, HD, HALF)
    sums = (2, 2, HD, HALF)
    kernel = functools.partial(
        attend_kernel,
        steps,
        count,
        first_head,
        [len(sources) for sources in kvs],
        dkv is not None,
        dq is not None,
        len(afters),
        last_dq,
        dkv_type is not None,
    )
    dq, *dkv = pl.pallas_call(
        kernel,
        grid=(1,),
        in_specs=[pl.BlockSpec(memory_space=pltpu.SMEM), vmem, stat_spec]
        + [vmem] * (len(operands) - 3)
        + [pl.BlockSpec(memory_space=pl.ANY)] * len(afters),
        out_specs=[vmem] * (1 + len(steps)),
        out_shape=[
            jax.ShapeDtypeStruct((8, count, TOK, HD) if last_dq else partial_dq, BF if last_dq else F32),
        ]
        + [jax.ShapeDtypeStruct(sums, dkv_type or F32)] * len(steps),
        scratch_shapes=[
            pltpu.VMEM((2, count, HD, HALF), BF),
            pltpu.VMEM((2, count, HD, HALF), BF),
            pltpu.VMEM((2 * count, 48, HALF), BF),
            pltpu.VMEM((len(steps), 2, 2, HD, HALF), BF),
            pltpu.VMEM((2, HALF, HALF), BF),
            pltpu.VMEM((2, HALF, HALF), BF),
        ]
        + ([pltpu.VMEM(partial_dq, F32)] if last_dq else [])
        + ([pltpu.VMEM(sums, F32)] * len(steps) if dkv_type is not None else []),
        compiler_params=pltpu.CompilerParams(vmem_limit_bytes=VMEM_LIMIT),
        cost_estimate=pl.CostEstimate(
            flops=2 * flops, bytes_accessed=8 << 20, transcendentals=int(tiles) * HALF * HALF * count
        ),
        name="attend",
    )(*operands, *afters)
    return dq, dict(zip(steps, dkv))


def join_kernel(one_ref, two_ref, inner_two_ref, inner_three_ref, to_one_ref, to_two_ref):
    to_one_ref[...] = (one_ref[...].astype(F32) + inner_two_ref[...].astype(F32)).astype(BF)
    to_two_ref[...] = (two_ref[...].astype(F32) + inner_three_ref[...].astype(F32)).astype(BF)


def join(*parts):
    shape = jax.ShapeDtypeStruct((2, 2, HD, HALF), BF)
    return pl.pallas_call(
        join_kernel,
        out_shape=[shape, shape],
        compiler_params=pltpu.CompilerParams(vmem_limit_bytes=VMEM_LIMIT),
        cost_estimate=pl.CostEstimate(flops=0, bytes_accessed=3 << 20, transcendentals=0),
        name="join",
    )(*parts)


def total_kernel(own_ref, *refs):
    *part_refs, out_ref = refs
    for pair in range(2):
        for half in range(2):
            total = own_ref[pair, half]
            for ref in part_refs:
                total += ref[pair, half].astype(F32)
            for i in range(4):
                out_ref[half * 4 + i, pair] = total[:, i * TOK : (i + 1) * TOK].astype(BF).T


def total(*parts):
    return pl.pallas_call(
        total_kernel,
        out_shape=jax.ShapeDtypeStruct((8, 2, TOK, HD), BF),
        compiler_params=pltpu.CompilerParams(vmem_limit_bytes=VMEM_LIMIT),
        cost_estimate=pl.CostEstimate(flops=0, bytes_accessed=4 << 20, transcendentals=0),
        name="total",
    )(*parts)


def unpack_q_kernel(per, *refs):
    out_ref = refs[-1]
    for u in range(per):
        h = u * HEADS_DEV
        for ref in refs[:-1]:
            for i in range(ref.shape[1]):
                out_ref[:, h * HD : (h + 1) * HD] = ref[u, i]
                h += 1


def unpack_q(parts):
    per = PACK_PER
    return pl.pallas_call(
        functools.partial(unpack_q_kernel, per),
        grid=(8 // per,),
        in_specs=[pl.BlockSpec((per,) + p.shape[1:], lambda u: (u, 0, 0, 0)) for p in parts],
        out_specs=pl.BlockSpec((TOK, per * HEADS_DEV * HD), lambda u: (0, u)),
        out_shape=jax.ShapeDtypeStruct((TOK, 8 * HEADS_DEV * HD), BF),
        compiler_params=pltpu.CompilerParams(vmem_limit_bytes=VMEM_LIMIT),
        cost_estimate=pl.CostEstimate(flops=0, bytes_accessed=4 << 20, transcendentals=0),
        name="unpack_q",
    )(*parts)


def unpack_kv_kernel(pair_ref, k_ref, v_ref):
    for u in range(8):
        k_ref[:, u * HD : (u + 1) * HD] = pair_ref[u, 0]
        v_ref[:, u * HD : (u + 1) * HD] = pair_ref[u, 1]


def unpack_kv(pair):
    shape = jax.ShapeDtypeStruct((TOK, 8 * HD), BF)
    return pl.pallas_call(
        unpack_kv_kernel,
        out_shape=[shape, shape],
        compiler_params=pltpu.CompilerParams(vmem_limit_bytes=VMEM_LIMIT),
        name="unpack_kv",
    )(pair)


def move(value, pairs):
    return lax.ppermute(value, "blk", pairs)


def exchange(value):
    return lax.all_to_all(value, "uly", split_axis=0, concat_axis=0, tiled=True)


def local(queries, key_rows, value_rows, grad_out, attn_out, log_norm, doc_ids):
    groups = lax.axis_size("blk")
    group = lax.axis_index("blk")
    member = lax.axis_index("uly")

    first = jnp.where(
        member < 4, group * HALF + member * TOK, (2 * groups - 1 - group) * HALF + (member - 4) * TOK
    )
    my_docs = lax.dynamic_slice_in_dim(doc_ids, first, TOK)
    lane = jnp.arange(128, dtype=jnp.int32)[None, :]
    doc_block = jnp.where(
        (lane >= 48) & (lane < 48 + DOCS) & (my_docs[:, None] != lane - 48), FAR, 0.0
    ).astype(BF)

    kdocs = []
    for step in range(STEPS):
        owner = (group - step) % groups
        low = lax.dynamic_slice_in_dim(doc_ids, owner * HALF, HALF)
        high = lax.dynamic_slice_in_dim(doc_ids, (2 * groups - 1 - owner) * HALF, HALF)
        kdocs.append(jnp.stack([low, high]))
    kdocs = jnp.stack(kdocs)
    kdoc = jnp.where(
        kdocs[:, :, None, :] == jnp.arange(16, dtype=jnp.int32)[None, None, :, None], -1.0, 0.0
    ).astype(BF)
    second = jnp.where(group >= jnp.arange(STEPS), 0, 1).astype(jnp.int32)

    chips = range(groups // 2)
    up = [(i, (i + 1) % groups) for i in range(groups)]
    inner_up = [(2 * m, 2 * m + 1) for m in chips]
    inner_down = [(2 * m + 1, 2 * m) for m in chips]
    down = [[(2 * m, (2 * m - step) % groups) for m in chips] for step in range(STEPS)]

    kv = exchange(pack_kv(key_rows, value_rows))
    one = move(kv, up)
    two, three = (move(kv, [(b, a) for a, b in down[step]]) for step in (2, 3))
    two_inner, three_inner = (move(part, inner_up) for part in (one, two))
    kvs = [[kv], [one], [two, two_inner], [three, three_inner]]

    qds = pack_q(queries, grad_out, attn_out, log_norm, doc_block, kv)
    qds = [exchange(qd) for qd in qds]
    stats = qds[0]
    dkv = None
    dqs = []
    for chunk in range(len(CHUNKS) - 1):
        dq, dkv = attend(
            (0, 1, 2, 3), chunk, second, qds[chunk], stats, kvs, kdoc, dkv, None, True, None
        )
        dqs.append(exchange(dq))
    args = (len(CHUNKS) - 1, second, qds[-1], stats, kvs, kdoc, dkv)
    dq, far = attend((2, 3), *args, None, False, BF)
    inner_two, inner_three = (move(far[step], inner_down) for step in (2, 3))
    from_three = move(far[3], down[3])
    dq, near = attend((1,), *args, dq, False, BF, dqs[:1])
    inner_one = move(near[1], inner_down)
    to_one, to_two = join(near[1], far[2], inner_two, inner_three)
    from_one, from_two = move(to_one, down[1]), move(to_two, down[2])
    dq, own = attend((0,), *args, dq, True, F32, (to_one,))
    dqs.append(exchange(dq))
    pair = exchange(total(own[0], inner_one, from_one, from_two, from_three))
    grad_keys, grad_values = unpack_kv(pair)
    return unpack_q(dqs), grad_keys, grad_values


def solution(mesh):
    rows = P(("blk", "uly"), None)
    return jax.shard_map(
        local,
        mesh=mesh,
        in_specs=(rows, rows, rows, rows, rows, rows, P()),
        out_specs=(rows, rows, rows),
        check_vma=False,
    )
```

```python
import functools
import math

import jax
import jax.numpy as jnp
from jax import lax
from jax.experimental import pallas as pl
from jax.experimental.pallas import tpu as pltpu
from jax.sharding import PartitionSpec as P

HD = 128
STEPS = 4
DOCS = 8
TOK = 128
HEADS_DEV = 8
HALF = 512
CHUNKS = (4, 4)
PARTS = 3
FAR = 32768.0
SCALE = HD ** (-0.5)
EXP2_SCALE = SCALE * math.log2(math.e)
NORM_SCALE = HD ** 0.5
BF = jnp.bfloat16
F32 = jnp.float32
BM, BN, PIPE = 256, 256, True
BM, BN = 256, 256
PACK_PER = 4
VMEM_LIMIT = 60 * 1024 * 1024

NN = (((1,), (0,)), ((), ()))
NT = (((1,), (1,)), ((), ()))


def dot(a, b, dims=NN):
    return lax.dot_general(a, b, dims, preferred_element_type=F32)


def parts_of(x):
    high = x.astype(BF)
    rest = x - high.astype(F32)
    mid = rest.astype(BF)
    low = (rest - mid.astype(F32)).astype(BF)
    return high, mid, low


def pack_kv_kernel(k_ref, v_ref, kv_ref):
    for u in range(8):
        kv_ref[u, 0] = k_ref[:, u * HD : (u + 1) * HD].T
        kv_ref[u, 1] = v_ref[:, u * HD : (u + 1) * HD].T


def pack_kv(key_rows, value_rows):
    return pl.pallas_call(
        pack_kv_kernel,
        out_shape=jax.ShapeDtypeStruct((8, 2, HD, TOK), BF),
        compiler_params=pltpu.CompilerParams(vmem_limit_bytes=VMEM_LIMIT),
        cost_estimate=pl.CostEstimate(flops=0, bytes_accessed=1 << 20, transcendentals=0),
        name="pack_kv",
    )(key_rows, value_rows)


def pack_q_kernel(per, q_ref, do_ref, o_ref, ln_ref, doc_ref, _, *refs):
    *qd_refs, pick_ref = refs
    step = pl.program_id(0)
    heads = ln_ref.shape[1]
    width = HEADS_DEV * HD

    @pl.when(step == 0)
    def _():
        head = lax.broadcasted_iota(jnp.int32, pick_ref.shape, 0) // HD
        col = lax.broadcasted_iota(jnp.int32, pick_ref.shape, 1)
        pick = (col >= 24) & (col < 48) & (head == col % HEADS_DEV)
        pick_ref[...] = jnp.where(pick, 1.0, 0.0).astype(BF)

    head = lax.broadcasted_iota(jnp.int32, (heads, 128), 0)
    col = lax.broadcasted_iota(jnp.int32, (heads, 128), 1)
    lane = lax.broadcasted_iota(jnp.int32, (TOK, 128), 1)
    norm_parts = parts_of(ln_ref[...] * NORM_SCALE)
    for i in range(per):
        first = i * width
        norm = jnp.zeros((TOK, 128), F32)
        for j, part in enumerate(norm_parts):
            mine = head == (step * per + i) * HEADS_DEV + col % HEADS_DEV
            pick = (col // HEADS_DEV == j) & mine
            norm += dot(part, jnp.where(pick, 1.0, 0.0).astype(BF))
        cols = slice(first, first + width)
        high, low, _ = parts_of(do_ref[:, cols].astype(F32) * o_ref[:, cols].astype(F32))
        delta = dot(high, pick_ref[...]) + dot(low, pick_ref[...])
        high, mid, low = parts_of(delta)
        delta = jnp.where(lane < 32, high, jnp.where(lane < 40, mid, low))
        stats = jnp.where(lane < 24, norm.astype(BF), jnp.where(lane < 48, delta, doc_ref[...]))
        h = 0
        for index, ref in enumerate(qd_refs):
            count = ref.shape[1] // 2
            for c in range(count):
                cols = slice(first + h * HD, first + (h + 1) * HD)
                ref[i, c] = q_ref[:, cols]
                ref[i, count + c] = do_ref[:, cols]
                h += 1
            if index == 0:
                ref[i, 2 * count] = stats


def pack_q(queries, grad_out, attn_out, log_norm, doc_block, after):
    per = PACK_PER
    wide = pl.BlockSpec((TOK, per * HEADS_DEV * HD), lambda u: (0, u))
    shapes = [(8, 2 * c + (i == 0), TOK, HD) for i, c in enumerate(CHUNKS)]
    return pl.pallas_call(
        functools.partial(pack_q_kernel, per),
        grid=(8 // per,),
        in_specs=[
            wide,
            wide,
            wide,
            pl.BlockSpec(log_norm.shape, lambda u: (0, 0)),
            pl.BlockSpec(doc_block.shape, lambda u: (0, 0)),
            pl.BlockSpec(memory_space=pl.ANY),
        ],
        out_specs=[pl.BlockSpec((per,) + s[1:], lambda u: (u, 0, 0, 0)) for s in shapes],
        out_shape=[jax.ShapeDtypeStruct(s, BF) for s in shapes],
        scratch_shapes=[pltpu.VMEM((HEADS_DEV * HD, 128), BF)],
        compiler_params=pltpu.CompilerParams(vmem_limit_bytes=VMEM_LIMIT),
        cost_estimate=pl.CostEstimate(flops=0, bytes_accessed=11 << 20, transcendentals=0),
        name="pack_q",
    )(queries, grad_out, attn_out, log_norm, doc_block, after)


def attend_kernel(steps, count, first_head, kv_counts, has_dkv, has_dq, afters, last_dq, last_dkv, *refs):
    refs = list(refs)

    def take(n):
        head = refs[:n]
        del refs[:n]
        return head

    second_ref, qd_ref, stat_ref = take(3)
    kv_refs = [take(n) for n in kv_counts]
    (kdoc_ref,) = take(1)
    dkv_in = take(len(steps)) if has_dkv else None
    (dq_in,) = take(1) if has_dq else (None,)
    take(afters)
    (dq_ref,) = take(1)
    dkv_refs = take(len(steps))
    qt_ref, dot_ref, sel_ref, kv_ref, p_ref, ds_ref = take(6)
    (dqt_ref,) = take(1) if last_dq else (dq_ref,)
    sum_refs = take(len(steps)) if last_dkv else dkv_refs

    row = lax.broadcasted_iota(jnp.int32, (48, HALF), 0)
    for h in range(count):
        mine = row % HEADS_DEV == first_head + h
        sel_ref[h] = jnp.where(mine & (row < 24), -1.0, 0.0).astype(BF)
        sel_ref[count + h] = jnp.where(mine & (row >= 24), -1.0, 0.0).astype(BF)
    for half in range(2):
        for i in range(4):
            cols = slice(i * TOK, (i + 1) * TOK)
            for index, sources in enumerate(kv_refs):
                for pair in range(2):
                    block = sources[0][half * 4 + i, pair]
                    for other in sources[1:]:
                        block = block + other[half * 4 + i, pair]
                    kv_ref[index, pair, half, :, cols] = block
    if has_dq:
        dqt_ref[...] = dq_in[...]
    else:
        dqt_ref[...] = jnp.zeros_like(dqt_ref)
    for index in range(len(steps)):
        if has_dkv:
            sum_refs[index][...] = dkv_in[index][...]
        else:
            sum_refs[index][...] = jnp.zeros_like(sum_refs[index])

    def turn_rows(half):
        for i in range(4):
            cols = slice(i * TOK, (i + 1) * TOK)
            for h in range(count):
                qt_ref[half, h, :, cols] = qd_ref[half * 4 + i, h].T
                dot_ref[half, h, :, cols] = qd_ref[half * 4 + i, count + h].T

    def rows_of(qhalf, index, q0, qn):
        block = qd_ref[pl.ds(qhalf * 4 + q0 // TOK, qn // TOK), index]
        return block.reshape(qn, HD)

    def scores(index, qhalf, khalf, h, slot, q0, k0, bm, bn, diagonal):
        kcols = slice(k0, k0 + bn)
        k_ext = jnp.concatenate(
            [
                kv_ref[index, 0, khalf, :, kcols],
                sel_ref[h, :, kcols],
                kdoc_ref[steps[index], khalf, :, kcols],
                jnp.zeros((64, bn), BF),
            ],
            axis=0,
        )
        v_ext = jnp.concatenate(
            [kv_ref[index, 1, khalf, :, kcols], sel_ref[count + h, :, kcols], jnp.zeros((80, bn), BF)],
            axis=0,
        )
        stats = stat_ref[pl.ds(qhalf * 4 + q0 // TOK, bm // TOK), 0].reshape(bm, HD)
        q_ext = jnp.concatenate([rows_of(qhalf, h, q0, bm), stats], axis=1)
        do_ext = jnp.concatenate([rows_of(qhalf, count + h, q0, bm), stats], axis=1)
        prob = jnp.exp2(dot(q_ext, k_ext) * EXP2_SCALE)
        if diagonal:
            qi = lax.broadcasted_iota(jnp.int32, (bm, bn), 0) + q0
            ki = lax.broadcasted_iota(jnp.int32, (bm, bn), 1) + k0
            prob = jnp.where(qi >= ki, prob, 0.0)
        rows = slice(q0, q0 + bm)
        ds_ref[slot, rows, kcols] = (prob * dot(do_ext, v_ext)).astype(BF)
        p_ref[slot, rows, kcols] = prob.astype(BF)

    def grads(index, qhalf, khalf, h, slot, diagonal):
        for k0, kn, q0 in ((0, 256, 0), (256, 256, 256)) if diagonal else ((0, HALF, 0),):
            span = slice(q0, HALF)
            cols = slice(k0, k0 + kn)
            sum_refs[index][1, khalf, :, cols] += dot(dot_ref[qhalf, h, :, span], p_ref[slot, span, cols])
            sum_refs[index][0, khalf, :, cols] += dot(qt_ref[qhalf, h, :, span], ds_ref[slot, span, cols])
        for q0, qn, kn in ((0, 256, 256), (256, 256, 512)) if diagonal else ((0, HALF, HALF),):
            span = slice(q0, q0 + qn)
            dqt_ref[qhalf, h, :, span] += dot(kv_ref[index, 0, khalf, :, :kn], ds_ref[slot, span, :kn], NT)

    def tile(index, qhalf, khalf, diagonal):
        for h in range(count):
            for k0 in range(0, HALF, BN):
                for q0 in range(0, HALF, BM):
                    if diagonal and q0 + BM <= k0:
                        if q0 >= k0 // 256 * 256:
                            ds_ref[h % 2, q0 : q0 + BM, k0 : k0 + BN] = jnp.zeros((BM, BN), BF)
                            p_ref[h % 2, q0 : q0 + BM, k0 : k0 + BN] = jnp.zeros((BM, BN), BF)
                        continue
                    scores(index, qhalf, khalf, h, h % 2, q0, k0, BM, BN, diagonal and q0 < k0 + BN)
            if PIPE and h > 0:
                grads(index, qhalf, khalf, h - 1, (h - 1) % 2, diagonal)
            if not PIPE:
                grads(index, qhalf, khalf, h, h % 2, diagonal)
        if PIPE:
            grads(index, qhalf, khalf, count - 1, (count - 1) % 2, diagonal)

    for index, step in enumerate(steps):
        if step == 0:

            def diagonal(half, carry, index=index):
                if index == 0:
                    turn_rows(half)
                tile(index, half, half, True)
                return carry

            lax.fori_loop(0, 2, diagonal, 0)
            tile(index, 1, 0, False)
        else:

            def both(turn, carry, index=index, step=step):
                second = second_ref[step]
                if index == 0:
                    turn_rows(1 - turn)
                tile(index, jnp.where(turn == 0, 1, second), jnp.where(turn == 0, 0, second), False)
                return carry

            lax.fori_loop(0, 2, both, 0)

    if last_dq:
        for half in range(2):
            for h in range(count):
                for i in range(4):
                    piece = dqt_ref[half, h, :, i * TOK : (i + 1) * TOK]
                    dq_ref[half * 4 + i, h] = (piece * SCALE).astype(BF).T
    if last_dkv:
        for total_ref, sum_ref in zip(dkv_refs, sum_refs):
            total_ref[0] = (sum_ref[0] * SCALE).astype(total_ref.dtype)
            total_ref[1] = sum_ref[1].astype(total_ref.dtype)


def attend(steps, chunk, second, qd, stats, kvs, kdoc, dkv, dq, last_dq, dkv_type, afters=()):
    first_head, count = sum(CHUNKS[:chunk]), CHUNKS[chunk]
    operands = [second, qd, stats]
    kvs = [kvs[step] for step in steps]
    for sources in kvs:
        operands += sources
    operands.append(kdoc)
    operands += [] if dkv is None else [dkv[step] for step in steps]
    operands += [] if dq is None else [dq]
    vmem = pl.BlockSpec(memory_space=pltpu.VMEM)
    stat_index = stats.shape[1] - 1
    stat_spec = pl.BlockSpec((8, 1, TOK, HD), lambda i: (0, stat_index, 0, 0))
    tiles = sum(2.5 if step == 0 else 2 for step in steps)
    flops = int(tiles * 5 * 2 * HALF * HALF * HD * count)
    partial_dq = (2, count, HD, HALF)
    sums = (2, 2, HD, HALF)
    kernel = functools.partial(
        attend_kernel,
        steps,
        count,
        first_head,
        [len(sources) for sources in kvs],
        dkv is not None,
        dq is not None,
        len(afters),
        last_dq,
        dkv_type is not None,
    )
    dq, *dkv = pl.pallas_call(
        kernel,
        grid=(1,),
        in_specs=[pl.BlockSpec(memory_space=pltpu.SMEM), vmem, stat_spec]
        + [vmem] * (len(operands) - 3)
        + [pl.BlockSpec(memory_space=pl.ANY)] * len(afters),
        out_specs=[vmem] * (1 + len(steps)),
        out_shape=[
            jax.ShapeDtypeStruct((8, count, TOK, HD) if last_dq else partial_dq, BF if last_dq else F32),
        ]
        + [jax.ShapeDtypeStruct(sums, dkv_type or F32)] * len(steps),
        scratch_shapes=[
            pltpu.VMEM((2, count, HD, HALF), BF),
            pltpu.VMEM((2, count, HD, HALF), BF),
            pltpu.VMEM((2 * count, 48, HALF), BF),
            pltpu.VMEM((len(steps), 2, 2, HD, HALF), BF),
            pltpu.VMEM((2, HALF, HALF), BF),
            pltpu.VMEM((2, HALF, HALF), BF),
        ]
        + ([pltpu.VMEM(partial_dq, F32)] if last_dq else [])
        + ([pltpu.VMEM(sums, F32)] * len(steps) if dkv_type is not None else []),
        compiler_params=pltpu.CompilerParams(vmem_limit_bytes=VMEM_LIMIT),
        cost_estimate=pl.CostEstimate(
            flops=2 * flops, bytes_accessed=8 << 20, transcendentals=int(tiles) * HALF * HALF * count
        ),
        name="attend",
    )(*operands, *afters)
    return dq, dict(zip(steps, dkv))


def join_kernel(one_ref, two_ref, inner_two_ref, inner_three_ref, to_one_ref, to_two_ref):
    to_one_ref[...] = (one_ref[...].astype(F32) + inner_two_ref[...].astype(F32)).astype(BF)
    to_two_ref[...] = (two_ref[...].astype(F32) + inner_three_ref[...].astype(F32)).astype(BF)


def join(*parts):
    shape = jax.ShapeDtypeStruct((2, 2, HD, HALF), BF)
    return pl.pallas_call(
        join_kernel,
        out_shape=[shape, shape],
        compiler_params=pltpu.CompilerParams(vmem_limit_bytes=VMEM_LIMIT),
        cost_estimate=pl.CostEstimate(flops=0, bytes_accessed=3 << 20, transcendentals=0),
        name="join",
    )(*parts)


def total_kernel(own_ref, *refs):
    *part_refs, out_ref = refs
    for pair in range(2):
        for half in range(2):
            total = own_ref[pair, half]
            for ref in part_refs:
                total += ref[pair, half].astype(F32)
            for i in range(4):
                out_ref[half * 4 + i, pair] = total[:, i * TOK : (i + 1) * TOK].astype(BF).T


def total(*parts):
    return pl.pallas_call(
        total_kernel,
        out_shape=jax.ShapeDtypeStruct((8, 2, TOK, HD), BF),
        compiler_params=pltpu.CompilerParams(vmem_limit_bytes=VMEM_LIMIT),
        cost_estimate=pl.CostEstimate(flops=0, bytes_accessed=4 << 20, transcendentals=0),
        name="total",
    )(*parts)


def unpack_q_kernel(per, *refs):
    out_ref = refs[-1]
    for u in range(per):
        h = u * HEADS_DEV
        for ref in refs[:-1]:
            for i in range(ref.shape[1]):
                out_ref[:, h * HD : (h + 1) * HD] = ref[u, i]
                h += 1


def unpack_q(parts):
    per = PACK_PER
    return pl.pallas_call(
        functools.partial(unpack_q_kernel, per),
        grid=(8 // per,),
        in_specs=[pl.BlockSpec((per,) + p.shape[1:], lambda u: (u, 0, 0, 0)) for p in parts],
        out_specs=pl.BlockSpec((TOK, per * HEADS_DEV * HD), lambda u: (0, u)),
        out_shape=jax.ShapeDtypeStruct((TOK, 8 * HEADS_DEV * HD), BF),
        compiler_params=pltpu.CompilerParams(vmem_limit_bytes=VMEM_LIMIT),
        cost_estimate=pl.CostEstimate(flops=0, bytes_accessed=4 << 20, transcendentals=0),
        name="unpack_q",
    )(*parts)


def unpack_kv_kernel(pair_ref, k_ref, v_ref):
    for u in range(8):
        k_ref[:, u * HD : (u + 1) * HD] = pair_ref[u, 0]
        v_ref[:, u * HD : (u + 1) * HD] = pair_ref[u, 1]


def unpack_kv(pair):
    shape = jax.ShapeDtypeStruct((TOK, 8 * HD), BF)
    return pl.pallas_call(
        unpack_kv_kernel,
        out_shape=[shape, shape],
        compiler_params=pltpu.CompilerParams(vmem_limit_bytes=VMEM_LIMIT),
        name="unpack_kv",
    )(pair)


def move(value, pairs):
    return lax.ppermute(value, "blk", pairs)


def exchange(value):
    return lax.all_to_all(value, "uly", split_axis=0, concat_axis=0, tiled=True)


def local(queries, key_rows, value_rows, grad_out, attn_out, log_norm, doc_ids):
    groups = lax.axis_size("blk")
    group = lax.axis_index("blk")
    member = lax.axis_index("uly")

    first = jnp.where(
        member < 4, group * HALF + member * TOK, (2 * groups - 1 - group) * HALF + (member - 4) * TOK
    )
    my_docs = lax.dynamic_slice_in_dim(doc_ids, first, TOK)
    lane = jnp.arange(128, dtype=jnp.int32)[None, :]
    doc_block = jnp.where(
        (lane >= 48) & (lane < 48 + DOCS) & (my_docs[:, None] != lane - 48), FAR, 0.0
    ).astype(BF)

    kdocs = []
    for step in range(STEPS):
        owner = (group - step) % groups
        low = lax.dynamic_slice_in_dim(doc_ids, owner * HALF, HALF)
        high = lax.dynamic_slice_in_dim(doc_ids, (2 * groups - 1 - owner) * HALF, HALF)
        kdocs.append(jnp.stack([low, high]))
    kdocs = jnp.stack(kdocs)
    kdoc = jnp.where(
        kdocs[:, :, None, :] == jnp.arange(16, dtype=jnp.int32)[None, None, :, None], -1.0, 0.0
    ).astype(BF)
    second = jnp.where(group >= jnp.arange(STEPS), 0, 1).astype(jnp.int32)

    chips = range(groups // 2)
    up = [(i, (i + 1) % groups) for i in range(groups)]
    inner_up = [(2 * m, 2 * m + 1) for m in chips]
    inner_down = [(2 * m + 1, 2 * m) for m in chips]
    down = [[(2 * m, (2 * m - step) % groups) for m in chips] for step in range(STEPS)]

    kv = exchange(pack_kv(key_rows, value_rows))
    one = move(kv, up)
    two, three = (move(kv, [(b, a) for a, b in down[step]]) for step in (2, 3))
    two_inner, three_inner = (move(part, inner_up) for part in (one, two))
    kvs = [[kv], [one], [two, two_inner], [three, three_inner]]

    qds = pack_q(queries, grad_out, attn_out, log_norm, doc_block, kv)
    first, *_ = lax.optimization_barrier((qds[0], one, two, three))
    first = exchange(first)
    last, *_ = lax.optimization_barrier((qds[1], first, two_inner, three_inner))
    qds = [first, exchange(last)]
    stats = qds[0]
    dkv = None
    dqs = []
    for chunk in range(len(CHUNKS) - 1):
        dq, dkv = attend(
            (0, 1, 2, 3), chunk, second, qds[chunk], stats, kvs, kdoc, dkv, None, True, None
        )
        dqs.append(exchange(dq))
    args = (len(CHUNKS) - 1, second, qds[-1], stats, kvs, kdoc, dkv)
    dq, far = attend((2, 3), *args, None, False, BF)
    inner_two, inner_three = (move(far[step], inner_down) for step in (2, 3))
    from_three = move(far[3], down[3])
    dq, near = attend((1,), *args, dq, False, BF, dqs[:1])
    inner_one = move(near[1], inner_down)
    to_one, to_two = join(near[1], far[2], inner_two, inner_three)
    from_one, from_two = move(to_one, down[1]), move(to_two, down[2])
    dq, own = attend((0,), *args, dq, True, F32, (to_one,))
    parts = (inner_one, from_one, from_two, from_three)
    dq, *parts = lax.optimization_barrier((dq, *parts))
    dqs.append(exchange(dq))
    pair, *_ = lax.optimization_barrier((total(own[0], *parts), dqs[-1]))
    pair = exchange(pair)
    grad_keys, grad_values = unpack_kv(pair)
    return unpack_q(dqs), grad_keys, grad_values


def solution(mesh):
    rows = P(("blk", "uly"), None)
    return jax.shard_map(
        local,
        mesh=mesh,
        in_specs=(rows, rows, rows, rows, rows, rows, P()),
        out_specs=(rows, rows, rows),
        check_vma=False,
    )
```

```python
import functools
import math

import jax
import jax.numpy as jnp
from jax import lax
from jax.experimental import pallas as pl
from jax.experimental.pallas import tpu as pltpu
from jax.sharding import PartitionSpec as P

HD = 128
STEPS = 4
DOCS = 8
TOK = 128
HEADS_DEV = 8
HALF = 512
CHUNKS = (3, 3, 2)
PARTS = 3
FAR = 32768.0
SCALE = HD ** (-0.5)
EXP2_SCALE = SCALE * math.log2(math.e)
NORM_SCALE = HD ** 0.5
BF = jnp.bfloat16
F32 = jnp.float32
BM, BN, PIPE = 256, 256, True
BM, BN = 256, 256
PACK_PER = 4
VMEM_LIMIT = 60 * 1024 * 1024

NN = (((1,), (0,)), ((), ()))
NT = (((1,), (1,)), ((), ()))


def dot(a, b, dims=NN):
    return lax.dot_general(a, b, dims, preferred_element_type=F32)


def parts_of(x):
    high = x.astype(BF)
    rest = x - high.astype(F32)
    mid = rest.astype(BF)
    low = (rest - mid.astype(F32)).astype(BF)
    return high, mid, low


def pack_kv_kernel(k_ref, v_ref, kv_ref):
    for u in range(8):
        kv_ref[u, 0] = k_ref[:, u * HD : (u + 1) * HD].T
        kv_ref[u, 1] = v_ref[:, u * HD : (u + 1) * HD].T


def pack_kv(key_rows, value_rows):
    return pl.pallas_call(
        pack_kv_kernel,
        out_shape=jax.ShapeDtypeStruct((8, 2, HD, TOK), BF),
        compiler_params=pltpu.CompilerParams(vmem_limit_bytes=VMEM_LIMIT),
        cost_estimate=pl.CostEstimate(flops=0, bytes_accessed=1 << 20, transcendentals=0),
        name="pack_kv",
    )(key_rows, value_rows)


def pack_q_kernel(per, q_ref, do_ref, o_ref, ln_ref, doc_ref, *refs):
    *qd_refs, pick_ref = refs
    step = pl.program_id(0)
    heads = ln_ref.shape[1]
    width = HEADS_DEV * HD

    @pl.when(step == 0)
    def _():
        head = lax.broadcasted_iota(jnp.int32, pick_ref.shape, 0) // HD
        col = lax.broadcasted_iota(jnp.int32, pick_ref.shape, 1)
        pick = (col >= 24) & (col < 48) & (head == col % HEADS_DEV)
        pick_ref[...] = jnp.where(pick, 1.0, 0.0).astype(BF)

    head = lax.broadcasted_iota(jnp.int32, (heads, 128), 0)
    col = lax.broadcasted_iota(jnp.int32, (heads, 128), 1)
    lane = lax.broadcasted_iota(jnp.int32, (TOK, 128), 1)
    norm_parts = parts_of(ln_ref[...] * NORM_SCALE)
    for i in range(per):
        first = i * width
        norm = jnp.zeros((TOK, 128), F32)
        for j, part in enumerate(norm_parts):
            mine = head == (step * per + i) * HEADS_DEV + col % HEADS_DEV
            pick = (col // HEADS_DEV == j) & mine
            norm += dot(part, jnp.where(pick, 1.0, 0.0).astype(BF))
        cols = slice(first, first + width)
        high, low, _ = parts_of(do_ref[:, cols].astype(F32) * o_ref[:, cols].astype(F32))
        delta = dot(high, pick_ref[...]) + dot(low, pick_ref[...])
        high, mid, low = parts_of(delta)
        delta = jnp.where(lane < 32, high, jnp.where(lane < 40, mid, low))
        stats = jnp.where(lane < 24, norm.astype(BF), jnp.where(lane < 48, delta, doc_ref[...]))
        h = 0
        for index, ref in enumerate(qd_refs):
            count = ref.shape[1] // 2
            for c in range(count):
                cols = slice(first + h * HD, first + (h + 1) * HD)
                ref[i, c] = q_ref[:, cols]
                ref[i, count + c] = do_ref[:, cols]
                h += 1
            if index == 0:
                ref[i, 2 * count] = stats


def pack_q(queries, grad_out, attn_out, log_norm, doc_block):
    per = PACK_PER
    wide = pl.BlockSpec((TOK, per * HEADS_DEV * HD), lambda u: (0, u))
    shapes = [(8, 2 * c + (i == 0), TOK, HD) for i, c in enumerate(CHUNKS)]
    return pl.pallas_call(
        functools.partial(pack_q_kernel, per),
        grid=(8 // per,),
        in_specs=[
            wide,
            wide,
            wide,
            pl.BlockSpec(log_norm.shape, lambda u: (0, 0)),
            pl.BlockSpec(doc_block.shape, lambda u: (0, 0)),
        ],
        out_specs=[pl.BlockSpec((per,) + s[1:], lambda u: (u, 0, 0, 0)) for s in shapes],
        out_shape=[jax.ShapeDtypeStruct(s, BF) for s in shapes],
        scratch_shapes=[pltpu.VMEM((HEADS_DEV * HD, 128), BF)],
        compiler_params=pltpu.CompilerParams(vmem_limit_bytes=VMEM_LIMIT),
        cost_estimate=pl.CostEstimate(flops=0, bytes_accessed=11 << 20, transcendentals=0),
        name="pack_q",
    )(queries, grad_out, attn_out, log_norm, doc_block)


def attend_kernel(count, first_head, kv_counts, has_dkv, has_dq, last, *refs):
    refs = list(refs)

    def take(n):
        head = refs[:n]
        del refs[:n]
        return head

    second_ref, qd_ref, stat_ref = take(3)
    kv_refs = [take(n) for n in kv_counts]
    (kdoc_ref,) = take(1)
    (dkv_in,) = take(1) if has_dkv else (None,)
    (dq_in,) = take(1) if has_dq else (None,)
    (dq_ref,) = take(1)
    dkv_refs = take(3 if last else 1)
    qt_ref, dot_ref, sel_ref, kv_ref, p_ref, ds_ref, dqt_ref = take(7)
    (sum_ref,) = take(1) if last else dkv_refs

    row = lax.broadcasted_iota(jnp.int32, (48, HALF), 0)
    for h in range(count):
        mine = row % HEADS_DEV == first_head + h
        sel_ref[h] = jnp.where(mine & (row < 24), -1.0, 0.0).astype(BF)
        sel_ref[count + h] = jnp.where(mine & (row >= 24), -1.0, 0.0).astype(BF)
    for half in range(2):
        for i in range(4):
            cols = slice(i * TOK, (i + 1) * TOK)
            for index, sources in enumerate(kv_refs):
                for pair in range(2):
                    block = sources[0][half * 4 + i, pair]
                    for other in sources[1:]:
                        block = block + other[half * 4 + i, pair]
                    kv_ref[index, pair, half, :, cols] = block
    dqt_ref[...] = jnp.zeros_like(dqt_ref)
    if has_dkv:
        sum_ref[...] = dkv_in[...]
    else:
        sum_ref[...] = jnp.zeros_like(sum_ref)

    def turn_rows(half):
        for i in range(4):
            cols = slice(i * TOK, (i + 1) * TOK)
            for h in range(count):
                qt_ref[half, h, :, cols] = qd_ref[half * 4 + i, h].T
                dot_ref[half, h, :, cols] = qd_ref[half * 4 + i, count + h].T

    def rows_of(qhalf, index, q0, qn):
        block = qd_ref[pl.ds(qhalf * 4 + q0 // TOK, qn // TOK), index]
        return block.reshape(qn, HD)

    def scores(index, qhalf, khalf, h, slot, q0, k0, bm, bn, diagonal):
        kcols = slice(k0, k0 + bn)
        k_ext = jnp.concatenate(
            [
                kv_ref[index, 0, khalf, :, kcols],
                sel_ref[h, :, kcols],
                kdoc_ref[index, khalf, :, kcols],
                jnp.zeros((64, bn), BF),
            ],
            axis=0,
        )
        v_ext = jnp.concatenate(
            [kv_ref[index, 1, khalf, :, kcols], sel_ref[count + h, :, kcols], jnp.zeros((80, bn), BF)],
            axis=0,
        )
        stats = stat_ref[pl.ds(qhalf * 4 + q0 // TOK, bm // TOK), 0].reshape(bm, HD)
        q_ext = jnp.concatenate([rows_of(qhalf, h, q0, bm), stats], axis=1)
        do_ext = jnp.concatenate([rows_of(qhalf, count + h, q0, bm), stats], axis=1)
        prob = jnp.exp2(dot(q_ext, k_ext) * EXP2_SCALE)
        if diagonal:
            qi = lax.broadcasted_iota(jnp.int32, (bm, bn), 0) + q0
            ki = lax.broadcasted_iota(jnp.int32, (bm, bn), 1) + k0
            prob = jnp.where(qi >= ki, prob, 0.0)
        rows = slice(q0, q0 + bm)
        ds_ref[slot, rows, kcols] = (prob * dot(do_ext, v_ext)).astype(BF)
        p_ref[slot, rows, kcols] = prob.astype(BF)

    def grads(index, qhalf, khalf, h, slot, diagonal):
        for k0, kn, q0 in ((0, 256, 0), (256, 256, 256)) if diagonal else ((0, HALF, 0),):
            span = slice(q0, HALF)
            cols = slice(k0, k0 + kn)
            sum_ref[index, 1, khalf, :, cols] += dot(dot_ref[qhalf, h, :, span], p_ref[slot, span, cols])
            sum_ref[index, 0, khalf, :, cols] += dot(qt_ref[qhalf, h, :, span], ds_ref[slot, span, cols])
        for q0, qn, kn in ((0, 256, 256), (256, 256, 512)) if diagonal else ((0, HALF, HALF),):
            span = slice(q0, q0 + qn)
            dqt_ref[qhalf, h, :, span] += dot(kv_ref[index, 0, khalf, :, :kn], ds_ref[slot, span, :kn], NT)

    def tile(index, qhalf, khalf, diagonal):
        for h in range(count):
            for k0 in range(0, HALF, BN):
                for q0 in range(0, HALF, BM):
                    if diagonal and q0 + BM <= k0:
                        if q0 >= k0 // 256 * 256:
                            ds_ref[h % 2, q0 : q0 + BM, k0 : k0 + BN] = jnp.zeros((BM, BN), BF)
                            p_ref[h % 2, q0 : q0 + BM, k0 : k0 + BN] = jnp.zeros((BM, BN), BF)
                        continue
                    scores(index, qhalf, khalf, h, h % 2, q0, k0, BM, BN, diagonal and q0 < k0 + BN)
            if PIPE and h > 0:
                grads(index, qhalf, khalf, h - 1, (h - 1) % 2, diagonal)
            if not PIPE:
                grads(index, qhalf, khalf, h, h % 2, diagonal)
        if PIPE:
            grads(index, qhalf, khalf, count - 1, (count - 1) % 2, diagonal)

    def diagonal(half, carry):
        turn_rows(half)
        tile(0, half, half, True)
        return carry

    lax.fori_loop(0, 2, diagonal, 0)
    tile(0, 1, 0, False)
    for step in range(1, STEPS):

        def both(turn, carry, step=step):
            second = second_ref[step]
            tile(step, jnp.where(turn == 0, 1, second), jnp.where(turn == 0, 0, second), False)
            return carry

        lax.fori_loop(0, 2, both, 0)

    ahead = dq_ref.shape[1] - count
    if has_dq:
        dq_ref[:, :ahead] = dq_in[...]
    for half in range(2):
        for h in range(count):
            for i in range(4):
                piece = dqt_ref[half, h, :, i * TOK : (i + 1) * TOK]
                dq_ref[half * 4 + i, ahead + h] = (piece * SCALE).astype(BF).T
    if last:
        own_ref, others_ref, three_ref = dkv_refs
        for pair, scale in ((0, SCALE), (1, 1.0)):
            own_ref[pair] = sum_ref[0, pair] * scale
            for step in range(1, STEPS):
                others_ref[step - 1, pair] = (sum_ref[step, pair] * scale).astype(BF)
            three_ref[pair] = others_ref[STEPS - 2, pair]


def attend(chunk, second, qd, stats, kvs, kdoc, dkv, dq, last):
    first_head, count = sum(CHUNKS[:chunk]), CHUNKS[chunk]
    operands = [second, qd, stats]
    for sources in kvs:
        operands += sources
    operands.append(kdoc)
    operands += [] if dkv is None else [dkv]
    operands += [] if dq is None else [dq]
    vmem = pl.BlockSpec(memory_space=pltpu.VMEM)
    stat_index = stats.shape[1] - 1
    stat_spec = pl.BlockSpec((8, 1, TOK, HD), lambda i: (0, stat_index, 0, 0))
    flops = int(8.5 * 5 * 2 * HALF * HALF * HD * count)
    out_heads = count + (0 if dq is None else dq.shape[1])
    sums = (STEPS, 2, 2, HD, HALF)
    shapes = [((8, out_heads, TOK, HD), BF)]
    shapes += [(sums[1:], F32), ((3,) + sums[1:], BF), (sums[1:], BF)] if last else [(sums, F32)]
    kernel = functools.partial(
        attend_kernel,
        count,
        first_head,
        [len(sources) for sources in kvs],
        dkv is not None,
        dq is not None,
        last,
    )
    return pl.pallas_call(
        kernel,
        grid=(1,),
        in_specs=[pl.BlockSpec(memory_space=pltpu.SMEM), vmem, stat_spec]
        + [vmem] * (len(operands) - 3),
        out_specs=[vmem] * len(shapes),
        out_shape=[jax.ShapeDtypeStruct(*shape) for shape in shapes],
        scratch_shapes=[
            pltpu.VMEM((2, count, HD, HALF), BF),
            pltpu.VMEM((2, count, HD, HALF), BF),
            pltpu.VMEM((2 * count, 48, HALF), BF),
            pltpu.VMEM(sums, BF),
            pltpu.VMEM((2, HALF, HALF), BF),
            pltpu.VMEM((2, HALF, HALF), BF),
            pltpu.VMEM((2, count, HD, HALF), F32),
        ]
        + ([pltpu.VMEM(sums, F32)] if last else []),
        compiler_params=pltpu.CompilerParams(vmem_limit_bytes=VMEM_LIMIT),
        cost_estimate=pl.CostEstimate(
            flops=2 * flops, bytes_accessed=8 << 20, transcendentals=8 * HALF * HALF * count
        ),
        name="attend",
    )(*operands)


def join_kernel(mine_ref, theirs_ref, to_one_ref, to_two_ref):
    for ref, step in ((to_one_ref, 0), (to_two_ref, 1)):
        ref[...] = (mine_ref[step].astype(F32) + theirs_ref[step + 1].astype(F32)).astype(BF)


def join(mine, theirs):
    shape = jax.ShapeDtypeStruct(mine.shape[1:], BF)
    return pl.pallas_call(
        join_kernel,
        out_shape=[shape, shape],
        compiler_params=pltpu.CompilerParams(vmem_limit_bytes=VMEM_LIMIT),
        cost_estimate=pl.CostEstimate(flops=0, bytes_accessed=3 << 20, transcendentals=0),
        name="join",
    )(mine, theirs)


def total_kernel(own_ref, theirs_ref, *refs):
    *part_refs, out_ref = refs
    for pair in range(2):
        for half in range(2):
            total = own_ref[pair, half] + theirs_ref[0, pair, half].astype(F32)
            for ref in part_refs:
                total += ref[pair, half].astype(F32)
            for i in range(4):
                out_ref[half * 4 + i, pair] = total[:, i * TOK : (i + 1) * TOK].astype(BF).T


def total(*parts):
    return pl.pallas_call(
        total_kernel,
        out_shape=jax.ShapeDtypeStruct((8, 2, TOK, HD), BF),
        compiler_params=pltpu.CompilerParams(vmem_limit_bytes=VMEM_LIMIT),
        cost_estimate=pl.CostEstimate(flops=0, bytes_accessed=4 << 20, transcendentals=0),
        name="total",
    )(*parts)


def unpack_q_kernel(per, *refs):
    out_ref = refs[-1]
    for u in range(per):
        h = u * HEADS_DEV
        for ref in refs[:-1]:
            for i in range(ref.shape[1]):
                out_ref[:, h * HD : (h + 1) * HD] = ref[u, i]
                h += 1


def unpack_q(parts):
    per = PACK_PER
    return pl.pallas_call(
        functools.partial(unpack_q_kernel, per),
        grid=(8 // per,),
        in_specs=[pl.BlockSpec((per,) + p.shape[1:], lambda u: (u, 0, 0, 0)) for p in parts],
        out_specs=pl.BlockSpec((TOK, per * HEADS_DEV * HD), lambda u: (0, u)),
        out_shape=jax.ShapeDtypeStruct((TOK, 8 * HEADS_DEV * HD), BF),
        compiler_params=pltpu.CompilerParams(vmem_limit_bytes=VMEM_LIMIT),
        cost_estimate=pl.CostEstimate(flops=0, bytes_accessed=4 << 20, transcendentals=0),
        name="unpack_q",
    )(*parts)


def unpack_kv_kernel(pair_ref, k_ref, v_ref):
    for u in range(8):
        k_ref[:, u * HD : (u + 1) * HD] = pair_ref[u, 0]
        v_ref[:, u * HD : (u + 1) * HD] = pair_ref[u, 1]


def unpack_kv(pair):
    shape = jax.ShapeDtypeStruct((TOK, 8 * HD), BF)
    return pl.pallas_call(
        unpack_kv_kernel,
        out_shape=[shape, shape],
        compiler_params=pltpu.CompilerParams(vmem_limit_bytes=VMEM_LIMIT),
        name="unpack_kv",
    )(pair)


def move(value, pairs):
    return lax.ppermute(value, "blk", pairs)


def exchange(value):
    return lax.all_to_all(value, "uly", split_axis=0, concat_axis=0, tiled=True)


def local(queries, key_rows, value_rows, grad_out, attn_out, log_norm, doc_ids):
    groups = lax.axis_size("blk")
    group = lax.axis_index("blk")
    member = lax.axis_index("uly")

    first = jnp.where(
        member < 4, group * HALF + member * TOK, (2 * groups - 1 - group) * HALF + (member - 4) * TOK
    )
    my_docs = lax.dynamic_slice_in_dim(doc_ids, first, TOK)
    lane = jnp.arange(128, dtype=jnp.int32)[None, :]
    doc_block = jnp.where(
        (lane >= 48) & (lane < 48 + DOCS) & (my_docs[:, None] != lane - 48), FAR, 0.0
    ).astype(BF)

    kdocs = []
    for step in range(STEPS):
        owner = (group - step) % groups
        low = lax.dynamic_slice_in_dim(doc_ids, owner * HALF, HALF)
        high = lax.dynamic_slice_in_dim(doc_ids, (2 * groups - 1 - owner) * HALF, HALF)
        kdocs.append(jnp.stack([low, high]))
    kdocs = jnp.stack(kdocs)
    kdoc = jnp.where(
        kdocs[:, :, None, :] == jnp.arange(16, dtype=jnp.int32)[None, None, :, None], -1.0, 0.0
    ).astype(BF)
    second = jnp.where(group >= jnp.arange(STEPS), 0, 1).astype(jnp.int32)

    chips = range(groups // 2)
    up = [(i, (i + 1) % groups) for i in range(groups)]
    inner_up = [(2 * m, 2 * m + 1) for m in chips]
    inner_down = [(2 * m + 1, 2 * m) for m in chips]
    down = [[(2 * m, (2 * m - step) % groups) for m in chips] for step in range(STEPS)]

    kv = exchange(pack_kv(key_rows, value_rows))
    one = move(kv, up)
    two, three = (move(kv, [(b, a) for a, b in down[step]]) for step in (2, 3))
    two_inner, three_inner = (move(part, inner_up) for part in (one, two))
    kvs = [[kv], [one], [two, two_inner], [three, three_inner]]

    packed = pack_q(queries, grad_out, attn_out, log_norm, doc_block)
    last = len(CHUNKS) - 1
    qds, dkv, dq = [exchange(packed[0])], None, None
    dqs = []
    for chunk in range(last + 1):
        if chunk < last:
            before = (two_inner, three_inner) if dq is None else (dq,)
            ahead, *_ = lax.optimization_barrier((packed[chunk + 1], qds[chunk], *before))
            qds.append(exchange(ahead))
        ready = dq if chunk == last else None
        dq, *dkvs = attend(
            chunk, second, qds[chunk], qds[0], kvs, kdoc, dkv, ready, chunk == last
        )
        dkv = dkvs[0]
        if chunk != last - 1:
            dqs.append(dq)
    own, others, three = dkvs
    early, *_ = lax.optimization_barrier((dqs[0], qds[last]))
    dqs = [exchange(early), exchange(dqs[1])]
    others, sent = lax.optimization_barrier((others, dqs[0]))
    dqs = [sent, *dqs[1:]]
    theirs = move(others, inner_down)
    from_three = move(three, down[3])
    to_one, to_two = join(others, theirs)
    from_one, from_two = move(to_one, down[1]), move(to_two, down[2])
    pair = total(own, theirs, from_one, from_two, from_three)
    pair, *_ = lax.optimization_barrier((pair, dqs[-1]))
    grad_keys, grad_values = unpack_kv(exchange(pair))
    return unpack_q(dqs), grad_keys, grad_values


def solution(mesh):
    rows = P(("blk", "uly"), None)
    return jax.shard_map(
        local,
        mesh=mesh,
        in_specs=(rows, rows, rows, rows, rows, rows, P()),
        out_specs=(rows, rows, rows),
        check_vma=False,
    )
```

```python
import functools
import math

import jax
import jax.numpy as jnp
from jax import lax
from jax.experimental import pallas as pl
from jax.experimental.pallas import tpu as pltpu
from jax.sharding import PartitionSpec as P

HD = 128
STEPS = 4
DOCS = 8
TOK = 128
HEADS_DEV = 8
HALF = 512
CHUNKS = (4, 4)
PARTS = 3
FAR = 32768.0
SCALE = HD ** (-0.5)
EXP2_SCALE = SCALE * math.log2(math.e)
NORM_SCALE = HD ** 0.5
BF = jnp.bfloat16
F32 = jnp.float32
BM, BN, PIPE = 256, 256, True
BM, BN = 256, 256
PACK_PER = 4
VMEM_LIMIT = 60 * 1024 * 1024

NN = (((1,), (0,)), ((), ()))
NT = (((1,), (1,)), ((), ()))


def dot(a, b, dims=NN):
    return lax.dot_general(a, b, dims, preferred_element_type=F32)


def parts_of(x):
    high = x.astype(BF)
    rest = x - high.astype(F32)
    mid = rest.astype(BF)
    low = (rest - mid.astype(F32)).astype(BF)
    return high, mid, low


def pack_kv_kernel(k_ref, v_ref, kv_ref):
    for u in range(8):
        kv_ref[u, 0] = k_ref[:, u * HD : (u + 1) * HD].T
        kv_ref[u, 1] = v_ref[:, u * HD : (u + 1) * HD].T


def pack_kv(key_rows, value_rows):
    return pl.pallas_call(
        pack_kv_kernel,
        out_shape=jax.ShapeDtypeStruct((8, 2, HD, TOK), BF),
        compiler_params=pltpu.CompilerParams(vmem_limit_bytes=VMEM_LIMIT),
        cost_estimate=pl.CostEstimate(flops=0, bytes_accessed=1 << 20, transcendentals=0),
        name="pack_kv",
    )(key_rows, value_rows)


def pack_q_kernel(per, q_ref, do_ref, o_ref, ln_ref, doc_ref, *refs):
    *qd_refs, pick_ref = refs
    step = pl.program_id(0)
    heads = ln_ref.shape[1]
    width = HEADS_DEV * HD

    @pl.when(step == 0)
    def _():
        head = lax.broadcasted_iota(jnp.int32, pick_ref.shape, 0) // HD
        col = lax.broadcasted_iota(jnp.int32, pick_ref.shape, 1)
        pick = (col >= 24) & (col < 48) & (head == col % HEADS_DEV)
        pick_ref[...] = jnp.where(pick, 1.0, 0.0).astype(BF)

    head = lax.broadcasted_iota(jnp.int32, (heads, 128), 0)
    col = lax.broadcasted_iota(jnp.int32, (heads, 128), 1)
    lane = lax.broadcasted_iota(jnp.int32, (TOK, 128), 1)
    norm_parts = parts_of(ln_ref[...] * NORM_SCALE)
    for i in range(per):
        first = i * width
        norm = jnp.zeros((TOK, 128), F32)
        for j, part in enumerate(norm_parts):
            mine = head == (step * per + i) * HEADS_DEV + col % HEADS_DEV
            pick = (col // HEADS_DEV == j) & mine
            norm += dot(part, jnp.where(pick, 1.0, 0.0).astype(BF))
        cols = slice(first, first + width)
        high, low, _ = parts_of(do_ref[:, cols].astype(F32) * o_ref[:, cols].astype(F32))
        delta = dot(high, pick_ref[...]) + dot(low, pick_ref[...])
        high, mid, low = parts_of(delta)
        delta = jnp.where(lane < 32, high, jnp.where(lane < 40, mid, low))
        stats = jnp.where(lane < 24, norm.astype(BF), jnp.where(lane < 48, delta, doc_ref[...]))
        h = 0
        for index, ref in enumerate(qd_refs):
            count = ref.shape[1] // 2
            for c in range(count):
                cols = slice(first + h * HD, first + (h + 1) * HD)
                ref[i, c] = q_ref[:, cols]
                ref[i, count + c] = do_ref[:, cols]
                h += 1
            if index == 0:
                ref[i, 2 * count] = stats


def pack_q(queries, grad_out, attn_out, log_norm, doc_block):
    per = PACK_PER
    wide = pl.BlockSpec((TOK, per * HEADS_DEV * HD), lambda u: (0, u))
    shapes = [(8, 2 * c + (i == 0), TOK, HD) for i, c in enumerate(CHUNKS)]
    return pl.pallas_call(
        functools.partial(pack_q_kernel, per),
        grid=(8 // per,),
        in_specs=[
            wide,
            wide,
            wide,
            pl.BlockSpec(log_norm.shape, lambda u: (0, 0)),
            pl.BlockSpec(doc_block.shape, lambda u: (0, 0)),
        ],
        out_specs=[pl.BlockSpec((per,) + s[1:], lambda u: (u, 0, 0, 0)) for s in shapes],
        out_shape=[jax.ShapeDtypeStruct(s, BF) for s in shapes],
        scratch_shapes=[pltpu.VMEM((HEADS_DEV * HD, 128), BF)],
        compiler_params=pltpu.CompilerParams(vmem_limit_bytes=VMEM_LIMIT),
        cost_estimate=pl.CostEstimate(flops=0, bytes_accessed=11 << 20, transcendentals=0),
        name="pack_q",
    )(queries, grad_out, attn_out, log_norm, doc_block)


def attend_kernel(count, first_head, kv_counts, has_dkv, has_dq, last, *refs):
    refs = list(refs)

    def take(n):
        head = refs[:n]
        del refs[:n]
        return head

    second_ref, qd_hbm, stat_hbm = take(3)
    kv_hbm = [take(n) for n in kv_counts]
    (kdoc_ref,) = take(1)
    (dkv_in,) = take(1) if has_dkv else (None,)
    (dq_in,) = take(1) if has_dq else (None,)
    (dq_ref,) = take(1)
    dkv_out = take(3 if last else 1)
    qt_ref, dot_ref, sel_ref, kv_ref, p_ref, ds_ref, dqt_ref = take(7)
    qd_ref, stat_ref, raw_ref, sum_ref, sems = take(5)
    (others_ref,) = take(1) if last else (None,)
    ahead = dq_ref.shape[1] - count

    def qd_copy(half):
        rows = pl.ds(half * 4, 4)
        return pltpu.make_async_copy(
            qd_hbm.at[rows, 0 : 2 * count], qd_ref.at[rows], sems.at[half]
        )

    stat_copy = pltpu.make_async_copy(
        stat_hbm.at[:, stat_hbm.shape[1] - 1], stat_ref, sems.at[2]
    )
    loads = []
    slot = 0
    for step, sources in enumerate(kv_hbm):
        loads.append([])
        for source in sources:
            loads[-1].append(pltpu.make_async_copy(source, raw_ref.at[slot], sems.at[3 + slot]))
            slot += 1
        if has_dkv:
            loads[-1].append(
                pltpu.make_async_copy(dkv_in.at[step], sum_ref.at[step], sems.at[9 + step])
            )
    stores = []
    if last:
        own_out, others_out, three_out = dkv_out
        stores.append(pltpu.make_async_copy(sum_ref.at[0], own_out, sems.at[13]))
        for step in range(1, STEPS):
            stores.append(
                pltpu.make_async_copy(
                    others_ref.at[step - 1], others_out.at[step - 1], sems.at[13 + step]
                )
            )
        three_store = pltpu.make_async_copy(others_ref.at[STEPS - 2], three_out, sems.at[17])
    else:
        for step in range(STEPS):
            stores.append(
                pltpu.make_async_copy(sum_ref.at[step], dkv_out[0].at[step], sems.at[13 + step])
            )
    if has_dq:
        dq_copy = pltpu.make_async_copy(dq_in, dq_ref.at[:, 0:ahead], sems.at[18])

    qd_copy(0).start()
    stat_copy.start()
    for copy in loads[0]:
        copy.start()
    qd_copy(1).start()
    for step_loads in loads[1:]:
        for copy in step_loads:
            copy.start()
    if has_dq:
        dq_copy.start()

    row = lax.broadcasted_iota(jnp.int32, (48, HALF), 0)
    for h in range(count):
        mine = row % HEADS_DEV == first_head + h
        sel_ref[h] = jnp.where(mine & (row < 24), -1.0, 0.0).astype(BF)
        sel_ref[count + h] = jnp.where(mine & (row >= 24), -1.0, 0.0).astype(BF)
    dqt_ref[...] = jnp.zeros_like(dqt_ref)
    if not has_dkv:
        sum_ref[...] = jnp.zeros_like(sum_ref)

    def begin(step):
        for copy in loads[step]:
            copy.wait()
        first = sum(kv_counts[:step])
        for half in range(2):
            for i in range(4):
                for pair in range(2):
                    block = raw_ref[first, half * 4 + i, pair]
                    for other in range(first + 1, first + kv_counts[step]):
                        block = block + raw_ref[other, half * 4 + i, pair]
                    kv_ref[step, pair, half, :, i * TOK : (i + 1) * TOK] = block

    def end(step):
        if last and step == 0:
            sum_ref[0, 0] = sum_ref[0, 0] * SCALE
        elif last:
            others_ref[step - 1, 0] = (sum_ref[step, 0] * SCALE).astype(BF)
            others_ref[step - 1, 1] = sum_ref[step, 1].astype(BF)
        stores[step].start()
        if last and step == STEPS - 1:
            three_store.start()

    def turn_rows(half):
        for i in range(4):
            cols = slice(i * TOK, (i + 1) * TOK)
            for h in range(count):
                qt_ref[half, h, :, cols] = qd_ref[half * 4 + i, h].T
                dot_ref[half, h, :, cols] = qd_ref[half * 4 + i, count + h].T

    def rows_of(qhalf, index, q0, qn):
        block = qd_ref[pl.ds(qhalf * 4 + q0 // TOK, qn // TOK), index]
        return block.reshape(qn, HD)

    def scores(index, qhalf, khalf, h, slot, q0, k0, bm, bn, diagonal):
        kcols = slice(k0, k0 + bn)
        k_ext = jnp.concatenate(
            [
                kv_ref[index, 0, khalf, :, kcols],
                sel_ref[h, :, kcols],
                kdoc_ref[index, khalf, :, kcols],
                jnp.zeros((64, bn), BF),
            ],
            axis=0,
        )
        v_ext = jnp.concatenate(
            [kv_ref[index, 1, khalf, :, kcols], sel_ref[count + h, :, kcols], jnp.zeros((80, bn), BF)],
            axis=0,
        )
        stats = stat_ref[pl.ds(qhalf * 4 + q0 // TOK, bm // TOK)].reshape(bm, HD)
        q_ext = jnp.concatenate([rows_of(qhalf, h, q0, bm), stats], axis=1)
        do_ext = jnp.concatenate([rows_of(qhalf, count + h, q0, bm), stats], axis=1)
        prob = jnp.exp2(dot(q_ext, k_ext) * EXP2_SCALE)
        if diagonal:
            qi = lax.broadcasted_iota(jnp.int32, (bm, bn), 0) + q0
            ki = lax.broadcasted_iota(jnp.int32, (bm, bn), 1) + k0
            prob = jnp.where(qi >= ki, prob, 0.0)
        rows = slice(q0, q0 + bm)
        ds_ref[slot, rows, kcols] = (prob * dot(do_ext, v_ext)).astype(BF)
        p_ref[slot, rows, kcols] = prob.astype(BF)

    def grads(index, qhalf, khalf, h, slot, diagonal):
        for k0, kn, q0 in ((0, 256, 0), (256, 256, 256)) if diagonal else ((0, HALF, 0),):
            span = slice(q0, HALF)
            cols = slice(k0, k0 + kn)
            sum_ref[index, 1, khalf, :, cols] += dot(dot_ref[qhalf, h, :, span], p_ref[slot, span, cols])
            sum_ref[index, 0, khalf, :, cols] += dot(qt_ref[qhalf, h, :, span], ds_ref[slot, span, cols])
        for q0, qn, kn in ((0, 256, 256), (256, 256, 512)) if diagonal else ((0, HALF, HALF),):
            span = slice(q0, q0 + qn)
            dqt_ref[qhalf, h, :, span] += dot(kv_ref[index, 0, khalf, :, :kn], ds_ref[slot, span, :kn], NT)

    def tile(index, qhalf, khalf, diagonal):
        for h in range(count):
            for k0 in range(0, HALF, BN):
                for q0 in range(0, HALF, BM):
                    if diagonal and q0 + BM <= k0:
                        if q0 >= k0 // 256 * 256:
                            ds_ref[h % 2, q0 : q0 + BM, k0 : k0 + BN] = jnp.zeros((BM, BN), BF)
                            p_ref[h % 2, q0 : q0 + BM, k0 : k0 + BN] = jnp.zeros((BM, BN), BF)
                        continue
                    scores(index, qhalf, khalf, h, h % 2, q0, k0, BM, BN, diagonal and q0 < k0 + BN)
            if PIPE and h > 0:
                grads(index, qhalf, khalf, h - 1, (h - 1) % 2, diagonal)
            if not PIPE:
                grads(index, qhalf, khalf, h, h % 2, diagonal)
        if PIPE:
            grads(index, qhalf, khalf, count - 1, (count - 1) % 2, diagonal)

    stat_copy.wait()
    begin(0)

    def diagonal(half, carry):
        qd_copy(half).wait()
        turn_rows(half)
        tile(0, half, half, True)
        return carry

    lax.fori_loop(0, 2, diagonal, 0)
    tile(0, 1, 0, False)
    end(0)
    for step in range(1, STEPS):
        begin(step)

        def both(turn, carry, step=step):
            second = second_ref[step]
            tile(step, jnp.where(turn == 0, 1, second), jnp.where(turn == 0, 0, second), False)
            return carry

        lax.fori_loop(0, 2, both, 0)
        end(step)

    for half in range(2):
        for h in range(count):
            for i in range(4):
                piece = dqt_ref[half, h, :, i * TOK : (i + 1) * TOK]
                dq_ref[half * 4 + i, ahead + h] = (piece * SCALE).astype(BF).T
    if has_dq:
        dq_copy.wait()
    for copy in stores:
        copy.wait()
    if last:
        three_store.wait()


def attend(chunk, second, qd, stats, kvs, kdoc, dkv, dq, last):
    first_head, count = sum(CHUNKS[:chunk]), CHUNKS[chunk]
    operands = [second, qd, stats]
    for sources in kvs:
        operands += sources
    operands.append(kdoc)
    operands += [] if dkv is None else [dkv]
    operands += [] if dq is None else [dq]
    vmem = pl.BlockSpec(memory_space=pltpu.VMEM)
    anywhere = pl.BlockSpec(memory_space=pl.ANY)
    flops = int(8.5 * 5 * 2 * HALF * HALF * HD * count)
    out_heads = count + (0 if dq is None else dq.shape[1])
    sums = (STEPS, 2, 2, HD, HALF)
    shapes = [((8, out_heads, TOK, HD), BF)]
    shapes += [(sums[1:], F32), ((3,) + sums[1:], BF), (sums[1:], BF)] if last else [(sums, F32)]
    kernel = functools.partial(
        attend_kernel,
        count,
        first_head,
        [len(sources) for sources in kvs],
        dkv is not None,
        dq is not None,
        last,
    )
    return pl.pallas_call(
        kernel,
        in_specs=[
            pl.BlockSpec(memory_space=pltpu.SMEM),
            *[anywhere] * (2 + sum(len(sources) for sources in kvs)),
            vmem,
            *[anywhere] * ((dkv is not None) + (dq is not None)),
        ],
        out_specs=[vmem] + [anywhere] * (len(shapes) - 1),
        out_shape=[jax.ShapeDtypeStruct(*shape) for shape in shapes],
        scratch_shapes=[
            pltpu.VMEM((2, count, HD, HALF), BF),
            pltpu.VMEM((2, count, HD, HALF), BF),
            pltpu.VMEM((2 * count, 48, HALF), BF),
            pltpu.VMEM(sums, BF),
            pltpu.VMEM((2, HALF, HALF), BF),
            pltpu.VMEM((2, HALF, HALF), BF),
            pltpu.VMEM((2, count, HD, HALF), F32),
            pltpu.VMEM((8, 2 * count, TOK, HD), BF),
            pltpu.VMEM((8, TOK, HD), BF),
            pltpu.VMEM((sum(len(sources) for sources in kvs), 8, 2, HD, TOK), BF),
            pltpu.VMEM(sums, F32),
            pltpu.SemaphoreType.DMA((19,)),
        ]
        + ([pltpu.VMEM((3,) + sums[1:], BF)] if last else []),
        compiler_params=pltpu.CompilerParams(vmem_limit_bytes=VMEM_LIMIT),
        cost_estimate=pl.CostEstimate(
            flops=2 * flops, bytes_accessed=8 << 20, transcendentals=8 * HALF * HALF * count
        ),
        name="attend",
    )(*operands)


def join_kernel(mine_ref, inner_two_ref, inner_three_ref, to_one_ref, to_two_ref):
    to_one_ref[...] = (mine_ref[0].astype(F32) + inner_two_ref[0].astype(F32)).astype(BF)
    to_two_ref[...] = (mine_ref[1].astype(F32) + inner_three_ref[0].astype(F32)).astype(BF)


def join(mine, theirs):
    def block(steps, first):
        return pl.BlockSpec((steps, 1, 2, HD, HALF), lambda pair: (first, pair, 0, 0, 0))

    out = pl.BlockSpec((1, 2, HD, HALF), lambda pair: (pair, 0, 0, 0))
    shape = jax.ShapeDtypeStruct(mine.shape[1:], BF)
    return pl.pallas_call(
        join_kernel,
        grid=(2,),
        in_specs=[block(2, 0), block(1, 1), block(1, 2)],
        out_specs=[out, out],
        out_shape=[shape, shape],
        compiler_params=pltpu.CompilerParams(vmem_limit_bytes=VMEM_LIMIT),
        cost_estimate=pl.CostEstimate(flops=0, bytes_accessed=3 << 20, transcendentals=0),
        name="join",
    )(mine, theirs, theirs)


def total_kernel(own_ref, theirs_ref, *refs):
    *part_refs, out_ref = refs
    for half in range(2):
        total = own_ref[0, half] + theirs_ref[0, 0, half].astype(F32)
        for ref in part_refs:
            total += ref[0, half].astype(F32)
        for i in range(4):
            out_ref[half * 4 + i, 0] = total[:, i * TOK : (i + 1) * TOK].astype(BF).T


def total(own, theirs, *parts):
    part = pl.BlockSpec((1, 2, HD, HALF), lambda pair: (pair, 0, 0, 0))
    return pl.pallas_call(
        total_kernel,
        grid=(2,),
        in_specs=[
            part,
            pl.BlockSpec((1, 1, 2, HD, HALF), lambda pair: (0, pair, 0, 0, 0)),
            *[part] * len(parts),
        ],
        out_specs=pl.BlockSpec((8, 1, TOK, HD), lambda pair: (0, pair, 0, 0)),
        out_shape=jax.ShapeDtypeStruct((8, 2, TOK, HD), BF),
        compiler_params=pltpu.CompilerParams(vmem_limit_bytes=VMEM_LIMIT),
        cost_estimate=pl.CostEstimate(flops=0, bytes_accessed=4 << 20, transcendentals=0),
        name="total",
    )(own, theirs, *parts)


def unpack_q_kernel(per, *refs):
    out_ref = refs[-1]
    for u in range(per):
        h = u * HEADS_DEV
        for ref in refs[:-1]:
            for i in range(ref.shape[1]):
                out_ref[:, h * HD : (h + 1) * HD] = ref[u, i]
                h += 1


def unpack_q(parts):
    per = PACK_PER
    return pl.pallas_call(
        functools.partial(unpack_q_kernel, per),
        grid=(8 // per,),
        in_specs=[pl.BlockSpec((per,) + p.shape[1:], lambda u: (u, 0, 0, 0)) for p in parts],
        out_specs=pl.BlockSpec((TOK, per * HEADS_DEV * HD), lambda u: (0, u)),
        out_shape=jax.ShapeDtypeStruct((TOK, 8 * HEADS_DEV * HD), BF),
        compiler_params=pltpu.CompilerParams(vmem_limit_bytes=VMEM_LIMIT),
        cost_estimate=pl.CostEstimate(flops=0, bytes_accessed=4 << 20, transcendentals=0),
        name="unpack_q",
    )(*parts)


def unpack_kv_kernel(pair_ref, k_ref, v_ref):
    for u in range(8):
        k_ref[:, u * HD : (u + 1) * HD] = pair_ref[u, 0]
        v_ref[:, u * HD : (u + 1) * HD] = pair_ref[u, 1]


def unpack_kv(pair):
    shape = jax.ShapeDtypeStruct((TOK, 8 * HD), BF)
    return pl.pallas_call(
        unpack_kv_kernel,
        out_shape=[shape, shape],
        compiler_params=pltpu.CompilerParams(vmem_limit_bytes=VMEM_LIMIT),
        name="unpack_kv",
    )(pair)


def move(value, pairs):
    return lax.ppermute(value, "blk", pairs)


def exchange(value):
    return lax.all_to_all(value, "uly", split_axis=0, concat_axis=0, tiled=True)


def local(queries, key_rows, value_rows, grad_out, attn_out, log_norm, doc_ids):
    groups = lax.axis_size("blk")
    group = lax.axis_index("blk")
    member = lax.axis_index("uly")

    first = jnp.where(
        member < 4, group * HALF + member * TOK, (2 * groups - 1 - group) * HALF + (member - 4) * TOK
    )
    my_docs = lax.dynamic_slice_in_dim(doc_ids, first, TOK)
    lane = jnp.arange(128, dtype=jnp.int32)[None, :]
    doc_block = jnp.where(
        (lane >= 48) & (lane < 48 + DOCS) & (my_docs[:, None] != lane - 48), FAR, 0.0
    ).astype(BF)

    kdocs = []
    for step in range(STEPS):
        owner = (group - step) % groups
        low = lax.dynamic_slice_in_dim(doc_ids, owner * HALF, HALF)
        high = lax.dynamic_slice_in_dim(doc_ids, (2 * groups - 1 - owner) * HALF, HALF)
        kdocs.append(jnp.stack([low, high]))
    kdocs = jnp.stack(kdocs)
    kdoc = jnp.where(
        kdocs[:, :, None, :] == jnp.arange(16, dtype=jnp.int32)[None, None, :, None], -1.0, 0.0
    ).astype(BF)
    second = jnp.where(group >= jnp.arange(STEPS), 0, 1).astype(jnp.int32)

    chips = range(groups // 2)
    up = [(i, (i + 1) % groups) for i in range(groups)]
    inner_up = [(2 * m, 2 * m + 1) for m in chips]
    inner_down = [(2 * m + 1, 2 * m) for m in chips]
    down = [[(2 * m, (2 * m - step) % groups) for m in chips] for step in range(STEPS)]

    kv = exchange(pack_kv(key_rows, value_rows))
    one = move(kv, up)
    two, three = (move(kv, [(b, a) for a, b in down[step]]) for step in (2, 3))
    two_inner, three_inner = (move(part, inner_up) for part in (one, two))
    kvs = [[kv], [one], [two, two_inner], [three, three_inner]]

    packed = pack_q(queries, grad_out, attn_out, log_norm, doc_block)
    early = exchange(packed[0])
    late, *_ = lax.optimization_barrier((packed[1], early, two_inner, three_inner))
    late = exchange(late)
    dq, dkv = attend(0, second, early, early, kvs, kdoc, None, None, False)
    dq, own, others, three = attend(1, second, late, early, kvs, kdoc, dkv, dq, True)

    theirs = move(others, inner_down)
    dq = exchange(dq)
    from_three = move(three, down[3])
    to_one, to_two = join(others, theirs)
    from_one, from_two = move(to_one, down[1]), move(to_two, down[2])
    pair = total(own, theirs, from_one, from_two, from_three)
    pair, *_ = lax.optimization_barrier((pair, dq))
    grad_keys, grad_values = unpack_kv(exchange(pair))
    return unpack_q([dq]), grad_keys, grad_values


def solution(mesh):
    rows = P(("blk", "uly"), None)
    return jax.shard_map(
        local,
        mesh=mesh,
        in_specs=(rows, rows, rows, rows, rows, rows, P()),
        out_specs=(rows, rows, rows),
        check_vma=False,
    )
```

```python
import functools
import math

import jax
import jax.numpy as jnp
from jax import lax
from jax.experimental import pallas as pl
from jax.experimental.pallas import tpu as pltpu
from jax.sharding import PartitionSpec as P

HD = 128
STEPS = 4
DOCS = 8
TOK = 128
HEADS_DEV = 8
HALF = 512
CHUNKS = (4, 4)
PARTS = 3
FAR = 32768.0
SCALE = HD ** (-0.5)
EXP2_SCALE = SCALE * math.log2(math.e)
NORM_SCALE = HD ** 0.5
BF = jnp.bfloat16
F32 = jnp.float32
BM, BN, PIPE = 256, 256, True
BM, BN = 256, 256
PACK_PER = 4
VMEM_LIMIT = 60 * 1024 * 1024

NN = (((1,), (0,)), ((), ()))
NT = (((1,), (1,)), ((), ()))


def dot(a, b, dims=NN):
    return lax.dot_general(a, b, dims, preferred_element_type=F32)


def parts_of(x):
    high = x.astype(BF)
    rest = x - high.astype(F32)
    mid = rest.astype(BF)
    low = (rest - mid.astype(F32)).astype(BF)
    return high, mid, low


def pack_kv_kernel(k_ref, v_ref, kv_ref):
    for u in range(8):
        kv_ref[u, 0] = k_ref[:, u * HD : (u + 1) * HD].T
        kv_ref[u, 1] = v_ref[:, u * HD : (u + 1) * HD].T


def pack_kv(key_rows, value_rows):
    return pl.pallas_call(
        pack_kv_kernel,
        out_shape=jax.ShapeDtypeStruct((8, 2, HD, TOK), BF),
        compiler_params=pltpu.CompilerParams(vmem_limit_bytes=VMEM_LIMIT),
        cost_estimate=pl.CostEstimate(flops=0, bytes_accessed=1 << 20, transcendentals=0),
        name="pack_kv",
    )(key_rows, value_rows)


def pack_q_kernel(per, q_ref, do_ref, o_ref, ln_ref, doc_ref, *refs):
    *qd_refs, pick_ref = refs
    step = pl.program_id(0)
    heads = ln_ref.shape[1]
    width = HEADS_DEV * HD

    @pl.when(step == 0)
    def _():
        head = lax.broadcasted_iota(jnp.int32, pick_ref.shape, 0) // HD
        col = lax.broadcasted_iota(jnp.int32, pick_ref.shape, 1)
        pick = (col >= 24) & (col < 48) & (head == col % HEADS_DEV)
        pick_ref[...] = jnp.where(pick, 1.0, 0.0).astype(BF)

    head = lax.broadcasted_iota(jnp.int32, (heads, 128), 0)
    col = lax.broadcasted_iota(jnp.int32, (heads, 128), 1)
    lane = lax.broadcasted_iota(jnp.int32, (TOK, 128), 1)
    norm_parts = parts_of(ln_ref[...] * NORM_SCALE)
    for i in range(per):
        first = i * width
        norm = jnp.zeros((TOK, 128), F32)
        for j, part in enumerate(norm_parts):
            mine = head == (step * per + i) * HEADS_DEV + col % HEADS_DEV
            pick = (col // HEADS_DEV == j) & mine
            norm += dot(part, jnp.where(pick, 1.0, 0.0).astype(BF))
        cols = slice(first, first + width)
        high, low, _ = parts_of(do_ref[:, cols].astype(F32) * o_ref[:, cols].astype(F32))
        delta = dot(high, pick_ref[...]) + dot(low, pick_ref[...])
        high, mid, low = parts_of(delta)
        delta = jnp.where(lane < 32, high, jnp.where(lane < 40, mid, low))
        stats = jnp.where(lane < 24, norm.astype(BF), jnp.where(lane < 48, delta, doc_ref[...]))
        h = 0
        for index, ref in enumerate(qd_refs):
            count = ref.shape[1] // 2
            for c in range(count):
                cols = slice(first + h * HD, first + (h + 1) * HD)
                ref[i, c] = q_ref[:, cols]
                ref[i, count + c] = do_ref[:, cols]
                h += 1
            if index == 0:
                ref[i, 2 * count] = stats


def pack_q(queries, grad_out, attn_out, log_norm, doc_block):
    per = PACK_PER
    wide = pl.BlockSpec((TOK, per * HEADS_DEV * HD), lambda u: (0, u))
    shapes = [(8, 2 * c + (i == 0), TOK, HD) for i, c in enumerate(CHUNKS)]
    return pl.pallas_call(
        functools.partial(pack_q_kernel, per),
        grid=(8 // per,),
        in_specs=[
            wide,
            wide,
            wide,
            pl.BlockSpec(log_norm.shape, lambda u: (0, 0)),
            pl.BlockSpec(doc_block.shape, lambda u: (0, 0)),
        ],
        out_specs=[pl.BlockSpec((per,) + s[1:], lambda u: (u, 0, 0, 0)) for s in shapes],
        out_shape=[jax.ShapeDtypeStruct(s, BF) for s in shapes],
        scratch_shapes=[pltpu.VMEM((HEADS_DEV * HD, 128), BF)],
        compiler_params=pltpu.CompilerParams(vmem_limit_bytes=VMEM_LIMIT),
        cost_estimate=pl.CostEstimate(flops=0, bytes_accessed=11 << 20, transcendentals=0),
        name="pack_q",
    )(queries, grad_out, attn_out, log_norm, doc_block)


def attend_kernel(count, first_head, kv_counts, has_dkv, last, *refs):
    refs = list(refs)

    def take(n):
        head = refs[:n]
        del refs[:n]
        return head

    second_ref, qd_hbm, stat_hbm = take(3)
    kv_hbm = [take(n) for n in kv_counts]
    (kdoc_ref,) = take(1)
    (dkv_in,) = take(1) if has_dkv else (None,)
    (dq_ref,) = take(1)
    dkv_out = take(3 if last else 1)
    qt_ref, dot_ref, sel_ref, kv_ref, p_ref, ds_ref, dqt_ref = take(7)
    qd_ref, stat_ref, raw_ref, sum_ref, sems = take(5)
    (others_ref,) = take(1) if last else (None,)

    def qd_copy(half):
        rows = pl.ds(half * 4, 4)
        return pltpu.make_async_copy(
            qd_hbm.at[rows, 0 : 2 * count], qd_ref.at[rows], sems.at[half]
        )

    stat_copy = pltpu.make_async_copy(
        stat_hbm.at[:, stat_hbm.shape[1] - 1], stat_ref, sems.at[2]
    )
    loads = []
    slot = 0
    for step, sources in enumerate(kv_hbm):
        loads.append([])
        for source in sources:
            loads[-1].append(pltpu.make_async_copy(source, raw_ref.at[slot], sems.at[3 + slot]))
            slot += 1
        if has_dkv:
            loads[-1].append(
                pltpu.make_async_copy(dkv_in.at[step], sum_ref.at[step], sems.at[9 + step])
            )
    stores = []
    if last:
        own_out, others_out, three_out = dkv_out
        stores.append(pltpu.make_async_copy(sum_ref.at[0], own_out, sems.at[13]))
        for step in range(1, STEPS):
            stores.append(
                pltpu.make_async_copy(
                    others_ref.at[step - 1], others_out.at[step - 1], sems.at[13 + step]
                )
            )
        three_store = pltpu.make_async_copy(others_ref.at[STEPS - 2], three_out, sems.at[17])
    else:
        for step in range(STEPS):
            stores.append(
                pltpu.make_async_copy(sum_ref.at[step], dkv_out[0].at[step], sems.at[13 + step])
            )

    qd_copy(0).start()
    stat_copy.start()
    for copy in loads[0]:
        copy.start()
    qd_copy(1).start()
    for step_loads in loads[1:]:
        for copy in step_loads:
            copy.start()

    row = lax.broadcasted_iota(jnp.int32, (48, HALF), 0)
    for h in range(count):
        mine = row % HEADS_DEV == first_head + h
        sel_ref[h] = jnp.where(mine & (row < 24), -1.0, 0.0).astype(BF)
        sel_ref[count + h] = jnp.where(mine & (row >= 24), -1.0, 0.0).astype(BF)
    dqt_ref[...] = jnp.zeros_like(dqt_ref)
    if not has_dkv:
        sum_ref[...] = jnp.zeros_like(sum_ref)

    def begin(step):
        for copy in loads[step]:
            copy.wait()
        first = sum(kv_counts[:step])
        for half in range(2):
            for i in range(4):
                for pair in range(2):
                    block = raw_ref[first, half * 4 + i, pair]
                    for other in range(first + 1, first + kv_counts[step]):
                        block = block + raw_ref[other, half * 4 + i, pair]
                    kv_ref[step, pair, half, :, i * TOK : (i + 1) * TOK] = block

    def end(step):
        if last and step == 0:
            sum_ref[0, 0] = sum_ref[0, 0] * SCALE
        elif last:
            others_ref[step - 1, 0] = (sum_ref[step, 0] * SCALE).astype(BF)
            others_ref[step - 1, 1] = sum_ref[step, 1].astype(BF)
        stores[step].start()
        if last and step == STEPS - 1:
            three_store.start()

    def turn_rows(half):
        for i in range(4):
            cols = slice(i * TOK, (i + 1) * TOK)
            for h in range(count):
                qt_ref[half, h, :, cols] = qd_ref[half * 4 + i, h].T
                dot_ref[half, h, :, cols] = qd_ref[half * 4 + i, count + h].T

    def rows_of(qhalf, index, q0, qn):
        block = qd_ref[pl.ds(qhalf * 4 + q0 // TOK, qn // TOK), index]
        return block.reshape(qn, HD)

    def scores(index, qhalf, khalf, h, slot, q0, k0, bm, bn, diagonal):
        kcols = slice(k0, k0 + bn)
        k_ext = jnp.concatenate(
            [
                kv_ref[index, 0, khalf, :, kcols],
                sel_ref[h, :, kcols],
                kdoc_ref[index, khalf, :, kcols],
                jnp.zeros((64, bn), BF),
            ],
            axis=0,
        )
        v_ext = jnp.concatenate(
            [kv_ref[index, 1, khalf, :, kcols], sel_ref[count + h, :, kcols], jnp.zeros((80, bn), BF)],
            axis=0,
        )
        stats = stat_ref[pl.ds(qhalf * 4 + q0 // TOK, bm // TOK)].reshape(bm, HD)
        q_ext = jnp.concatenate([rows_of(qhalf, h, q0, bm), stats], axis=1)
        do_ext = jnp.concatenate([rows_of(qhalf, count + h, q0, bm), stats], axis=1)
        prob = jnp.exp2(dot(q_ext, k_ext) * EXP2_SCALE)
        if diagonal:
            qi = lax.broadcasted_iota(jnp.int32, (bm, bn), 0) + q0
            ki = lax.broadcasted_iota(jnp.int32, (bm, bn), 1) + k0
            prob = jnp.where(qi >= ki, prob, 0.0)
        rows = slice(q0, q0 + bm)
        ds_ref[slot, rows, kcols] = (prob * dot(do_ext, v_ext)).astype(BF)
        p_ref[slot, rows, kcols] = prob.astype(BF)

    def grads(index, qhalf, khalf, h, slot, diagonal):
        for k0, kn, q0 in ((0, 256, 0), (256, 256, 256)) if diagonal else ((0, HALF, 0),):
            span = slice(q0, HALF)
            cols = slice(k0, k0 + kn)
            sum_ref[index, 1, khalf, :, cols] += dot(dot_ref[qhalf, h, :, span], p_ref[slot, span, cols])
            sum_ref[index, 0, khalf, :, cols] += dot(qt_ref[qhalf, h, :, span], ds_ref[slot, span, cols])
        for q0, qn, kn in ((0, 256, 256), (256, 256, 512)) if diagonal else ((0, HALF, HALF),):
            span = slice(q0, q0 + qn)
            dqt_ref[qhalf, h, :, span] += dot(kv_ref[index, 0, khalf, :, :kn], ds_ref[slot, span, :kn], NT)

    def tile(index, qhalf, khalf, diagonal):
        for h in range(count):
            for k0 in range(0, HALF, BN):
                for q0 in range(0, HALF, BM):
                    if diagonal and q0 + BM <= k0:
                        if q0 >= k0 // 256 * 256:
                            ds_ref[h % 2, q0 : q0 + BM, k0 : k0 + BN] = jnp.zeros((BM, BN), BF)
                            p_ref[h % 2, q0 : q0 + BM, k0 : k0 + BN] = jnp.zeros((BM, BN), BF)
                        continue
                    scores(index, qhalf, khalf, h, h % 2, q0, k0, BM, BN, diagonal and q0 < k0 + BN)
            if PIPE and h > 0:
                grads(index, qhalf, khalf, h - 1, (h - 1) % 2, diagonal)
            if not PIPE:
                grads(index, qhalf, khalf, h, h % 2, diagonal)
        if PIPE:
            grads(index, qhalf, khalf, count - 1, (count - 1) % 2, diagonal)

    stat_copy.wait()
    begin(0)

    def diagonal(half, carry):
        qd_copy(half).wait()
        turn_rows(half)
        tile(0, half, half, True)
        return carry

    lax.fori_loop(0, 2, diagonal, 0)
    tile(0, 1, 0, False)
    end(0)
    for step in range(1, STEPS):
        begin(step)

        def both(turn, carry, step=step):
            second = second_ref[step]
            tile(step, jnp.where(turn == 0, 1, second), jnp.where(turn == 0, 0, second), False)
            return carry

        lax.fori_loop(0, 2, both, 0)
        end(step)

    for half in range(2):
        for h in range(count):
            for i in range(4):
                piece = dqt_ref[half, h, :, i * TOK : (i + 1) * TOK]
                dq_ref[half * 4 + i, h] = (piece * SCALE).astype(BF).T
    for copy in stores:
        copy.wait()
    if last:
        three_store.wait()


def attend(chunk, second, qd, stats, kvs, kdoc, dkv, last):
    first_head, count = sum(CHUNKS[:chunk]), CHUNKS[chunk]
    operands = [second, qd, stats]
    for sources in kvs:
        operands += sources
    operands.append(kdoc)
    operands += [] if dkv is None else [dkv]
    vmem = pl.BlockSpec(memory_space=pltpu.VMEM)
    anywhere = pl.BlockSpec(memory_space=pl.ANY)
    flops = int(8.5 * 5 * 2 * HALF * HALF * HD * count)
    sums = (STEPS, 2, 2, HD, HALF)
    shapes = [((8, count, TOK, HD), BF)]
    shapes += [(sums[1:], F32), ((3,) + sums[1:], BF), (sums[1:], BF)] if last else [(sums, F32)]
    kernel = functools.partial(
        attend_kernel,
        count,
        first_head,
        [len(sources) for sources in kvs],
        dkv is not None,
        last,
    )
    return pl.pallas_call(
        kernel,
        in_specs=[
            pl.BlockSpec(memory_space=pltpu.SMEM),
            *[anywhere] * (2 + sum(len(sources) for sources in kvs)),
            vmem,
            *[anywhere] * (dkv is not None),
        ],
        out_specs=[vmem] + [anywhere] * (len(shapes) - 1),
        out_shape=[jax.ShapeDtypeStruct(*shape) for shape in shapes],
        scratch_shapes=[
            pltpu.VMEM((2, count, HD, HALF), BF),
            pltpu.VMEM((2, count, HD, HALF), BF),
            pltpu.VMEM((2 * count, 48, HALF), BF),
            pltpu.VMEM(sums, BF),
            pltpu.VMEM((2, HALF, HALF), BF),
            pltpu.VMEM((2, HALF, HALF), BF),
            pltpu.VMEM((2, count, HD, HALF), F32),
            pltpu.VMEM((8, 2 * count, TOK, HD), BF),
            pltpu.VMEM((8, TOK, HD), BF),
            pltpu.VMEM((sum(len(sources) for sources in kvs), 8, 2, HD, TOK), BF),
            pltpu.VMEM(sums, F32),
            pltpu.SemaphoreType.DMA((18,)),
        ]
        + ([pltpu.VMEM((3,) + sums[1:], BF)] if last else []),
        compiler_params=pltpu.CompilerParams(vmem_limit_bytes=VMEM_LIMIT),
        cost_estimate=pl.CostEstimate(
            flops=2 * flops, bytes_accessed=8 << 20, transcendentals=8 * HALF * HALF * count
        ),
        name="attend",
    )(*operands)


def join_kernel(mine_ref, inner_two_ref, inner_three_ref, to_one_ref, to_two_ref):
    to_one_ref[...] = (mine_ref[0].astype(F32) + inner_two_ref[0].astype(F32)).astype(BF)
    to_two_ref[...] = (mine_ref[1].astype(F32) + inner_three_ref[0].astype(F32)).astype(BF)


def join(mine, theirs):
    def block(steps, first):
        return pl.BlockSpec((steps, 1, 2, HD, HALF), lambda pair: (first, pair, 0, 0, 0))

    out = pl.BlockSpec((1, 2, HD, HALF), lambda pair: (pair, 0, 0, 0))
    shape = jax.ShapeDtypeStruct(mine.shape[1:], BF)
    return pl.pallas_call(
        join_kernel,
        grid=(2,),
        in_specs=[block(2, 0), block(1, 1), block(1, 2)],
        out_specs=[out, out],
        out_shape=[shape, shape],
        compiler_params=pltpu.CompilerParams(vmem_limit_bytes=VMEM_LIMIT),
        cost_estimate=pl.CostEstimate(flops=0, bytes_accessed=3 << 20, transcendentals=0),
        name="join",
    )(mine, theirs, theirs)


def total_kernel(own_ref, theirs_ref, *refs):
    *part_refs, out_ref = refs
    for half in range(2):
        total = own_ref[0, half] + theirs_ref[0, 0, half].astype(F32)
        for ref in part_refs:
            total += ref[0, half].astype(F32)
        for i in range(4):
            out_ref[half * 4 + i, 0] = total[:, i * TOK : (i + 1) * TOK].astype(BF).T


def total(own, theirs, *parts):
    part = pl.BlockSpec((1, 2, HD, HALF), lambda pair: (pair, 0, 0, 0))
    return pl.pallas_call(
        total_kernel,
        grid=(2,),
        in_specs=[
            part,
            pl.BlockSpec((1, 1, 2, HD, HALF), lambda pair: (0, pair, 0, 0, 0)),
            *[part] * len(parts),
        ],
        out_specs=pl.BlockSpec((8, 1, TOK, HD), lambda pair: (0, pair, 0, 0)),
        out_shape=jax.ShapeDtypeStruct((8, 2, TOK, HD), BF),
        compiler_params=pltpu.CompilerParams(vmem_limit_bytes=VMEM_LIMIT),
        cost_estimate=pl.CostEstimate(flops=0, bytes_accessed=4 << 20, transcendentals=0),
        name="total",
    )(own, theirs, *parts)


def unpack_q_kernel(per, *refs):
    out_ref = refs[-1]
    for u in range(per):
        h = u * HEADS_DEV
        for ref in refs[:-1]:
            for i in range(ref.shape[1]):
                out_ref[:, h * HD : (h + 1) * HD] = ref[u, i]
                h += 1


def unpack_q(parts):
    per = PACK_PER
    return pl.pallas_call(
        functools.partial(unpack_q_kernel, per),
        grid=(8 // per,),
        in_specs=[pl.BlockSpec((per,) + p.shape[1:], lambda u: (u, 0, 0, 0)) for p in parts],
        out_specs=pl.BlockSpec((TOK, per * HEADS_DEV * HD), lambda u: (0, u)),
        out_shape=jax.ShapeDtypeStruct((TOK, 8 * HEADS_DEV * HD), BF),
        compiler_params=pltpu.CompilerParams(vmem_limit_bytes=VMEM_LIMIT),
        cost_estimate=pl.CostEstimate(flops=0, bytes_accessed=4 << 20, transcendentals=0),
        name="unpack_q",
    )(*parts)


def unpack_kv_kernel(pair_ref, k_ref, v_ref):
    for u in range(8):
        k_ref[:, u * HD : (u + 1) * HD] = pair_ref[u, 0]
        v_ref[:, u * HD : (u + 1) * HD] = pair_ref[u, 1]


def unpack_kv(pair):
    shape = jax.ShapeDtypeStruct((TOK, 8 * HD), BF)
    return pl.pallas_call(
        unpack_kv_kernel,
        out_shape=[shape, shape],
        compiler_params=pltpu.CompilerParams(vmem_limit_bytes=VMEM_LIMIT),
        name="unpack_kv",
    )(pair)


def move(value, pairs):
    return lax.ppermute(value, "blk", pairs)


def exchange(value):
    return lax.all_to_all(value, "uly", split_axis=0, concat_axis=0, tiled=True)


def local(queries, key_rows, value_rows, grad_out, attn_out, log_norm, doc_ids):
    groups = lax.axis_size("blk")
    group = lax.axis_index("blk")
    member = lax.axis_index("uly")

    first = jnp.where(
        member < 4, group * HALF + member * TOK, (2 * groups - 1 - group) * HALF + (member - 4) * TOK
    )
    my_docs = lax.dynamic_slice_in_dim(doc_ids, first, TOK)
    lane = jnp.arange(128, dtype=jnp.int32)[None, :]
    doc_block = jnp.where(
        (lane >= 48) & (lane < 48 + DOCS) & (my_docs[:, None] != lane - 48), FAR, 0.0
    ).astype(BF)

    kdocs = []
    for step in range(STEPS):
        owner = (group - step) % groups
        low = lax.dynamic_slice_in_dim(doc_ids, owner * HALF, HALF)
        high = lax.dynamic_slice_in_dim(doc_ids, (2 * groups - 1 - owner) * HALF, HALF)
        kdocs.append(jnp.stack([low, high]))
    kdocs = jnp.stack(kdocs)
    kdoc = jnp.where(
        kdocs[:, :, None, :] == jnp.arange(16, dtype=jnp.int32)[None, None, :, None], -1.0, 0.0
    ).astype(BF)
    second = jnp.where(group >= jnp.arange(STEPS), 0, 1).astype(jnp.int32)

    chips = range(groups // 2)
    up = [(i, (i + 1) % groups) for i in range(groups)]
    inner_up = [(2 * m, 2 * m + 1) for m in chips]
    inner_down = [(2 * m + 1, 2 * m) for m in chips]
    down = [[(2 * m, (2 * m - step) % groups) for m in chips] for step in range(STEPS)]

    kv = exchange(pack_kv(key_rows, value_rows))
    one = move(kv, up)
    two, three = (move(kv, [(b, a) for a, b in down[step]]) for step in (2, 3))
    two_inner, three_inner = (move(part, inner_up) for part in (one, two))
    kvs = [[kv], [one], [two, two_inner], [three, three_inner]]

    packed = pack_q(queries, grad_out, attn_out, log_norm, doc_block)
    early = exchange(packed[0])
    late, *_ = lax.optimization_barrier((packed[1], early))
    late = exchange(late)
    dq_early, dkv = attend(0, second, early, early, kvs, kdoc, None, False)
    dq_early, *_ = lax.optimization_barrier((dq_early, late))
    dq_early = exchange(dq_early)
    dq_late, own, others, far = attend(1, second, late, early, kvs, kdoc, dkv, True)

    others, dq_early = lax.optimization_barrier((others, dq_early))
    theirs = move(others, inner_down)
    dq_late = exchange(dq_late)
    from_three = move(far, down[3])
    to_one, to_two = join(others, theirs)
    from_one, from_two = move(to_one, down[1]), move(to_two, down[2])
    pair = total(own, theirs, from_one, from_two, from_three)
    pair, *_ = lax.optimization_barrier((pair, dq_late))
    grad_keys, grad_values = unpack_kv(exchange(pair))
    return unpack_q([dq_early, dq_late]), grad_keys, grad_values


def solution(mesh):
    rows = P(("blk", "uly"), None)
    return jax.shard_map(
        local,
        mesh=mesh,
        in_specs=(rows, rows, rows, rows, rows, rows, P()),
        out_specs=(rows, rows, rows),
        check_vma=False,
    )
```

```python
import functools
import math

import jax
import jax.numpy as jnp
from jax import lax
from jax.experimental import pallas as pl
from jax.experimental.pallas import tpu as pltpu
from jax.sharding import PartitionSpec as P

HD = 128
STEPS = 4
DOCS = 8
TOK = 128
HEADS_DEV = 8
HALF = 512
CHUNKS = (4, 4)
PARTS = 3
FAR = 32768.0
SCALE = HD ** (-0.5)
EXP2_SCALE = SCALE * math.log2(math.e)
NORM_SCALE = HD ** 0.5
BF = jnp.bfloat16
F32 = jnp.float32
BM, BN, PIPE = 256, 256, True
BM, BN = 256, 256
GROUP = 4
PACK_PER = 4
VMEM_LIMIT = 60 * 1024 * 1024

NN = (((1,), (0,)), ((), ()))
NT = (((1,), (1,)), ((), ()))
TN = (((0,), (0,)), ((), ()))


def dot(a, b, dims=NN):
    return lax.dot_general(a, b, dims, preferred_element_type=F32)


def parts_of(x):
    high = x.astype(BF)
    rest = x - high.astype(F32)
    mid = rest.astype(BF)
    low = (rest - mid.astype(F32)).astype(BF)
    return high, mid, low


def pack_kv_kernel(k_ref, v_ref, kv_ref):
    for u in range(8):
        kv_ref[u, 0] = k_ref[:, u * HD : (u + 1) * HD].T
        kv_ref[u, 1] = v_ref[:, u * HD : (u + 1) * HD].T


def pack_kv(key_rows, value_rows):
    return pl.pallas_call(
        pack_kv_kernel,
        out_shape=jax.ShapeDtypeStruct((8, 2, HD, TOK), BF),
        compiler_params=pltpu.CompilerParams(vmem_limit_bytes=VMEM_LIMIT),
        cost_estimate=pl.CostEstimate(flops=0, bytes_accessed=1 << 20, transcendentals=0),
        name="pack_kv",
    )(key_rows, value_rows)


def pack_q_kernel(per, q_ref, do_ref, o_ref, ln_ref, doc_ref, *refs):
    *qd_refs, pick_ref = refs
    step = pl.program_id(0)
    group, member = lax.axis_index("blk"), lax.axis_index("uly")
    groups = lax.axis_size("blk")
    heads = ln_ref.shape[0]
    width = HEADS_DEV * HD

    @pl.when(step == 0)
    def _():
        head = lax.broadcasted_iota(jnp.int32, pick_ref.shape, 0) // HD
        col = lax.broadcasted_iota(jnp.int32, pick_ref.shape, 1)
        pick = (col >= 24) & (col < 48) & (head == col % HEADS_DEV)
        pick_ref[...] = jnp.where(pick, 1.0, 0.0).astype(BF)

    head = lax.broadcasted_iota(jnp.int32, (heads, 128), 0)
    col = lax.broadcasted_iota(jnp.int32, (heads, 128), 1)
    lane = lax.broadcasted_iota(jnp.int32, (TOK, 128), 1)
    quarters = HALF // TOK
    low = group * quarters + member
    high = (2 * groups - 1 - group) * quarters + member - quarters
    spot = jnp.where(member < quarters, low, high)
    docs = doc_ref[pl.ds(spot, 1), :].astype(F32)
    row = lax.broadcasted_iota(jnp.int32, (TOK, 128), 0)
    docs = jnp.where(row == lane, jnp.broadcast_to(docs, (TOK, 128)), 0.0).astype(BF)
    docs = dot(docs, jnp.ones((128, 128), BF))
    other = (lane < 48 + DOCS) & (docs != (lane - 48).astype(F32))
    doc_block = jnp.where(other, FAR, 0.0).astype(BF)
    norm_parts = parts_of(ln_ref[...] * NORM_SCALE)
    for i in range(per):
        first = i * width
        norm = jnp.zeros((TOK, 128), F32)
        for j, part in enumerate(norm_parts):
            mine = head == (step * per + i) * HEADS_DEV + col % HEADS_DEV
            pick = (col // HEADS_DEV == j) & mine
            norm += dot(part, jnp.where(pick, 1.0, 0.0).astype(BF), TN)
        cols = slice(first, first + width)
        high, low, _ = parts_of(do_ref[:, cols].astype(F32) * o_ref[:, cols].astype(F32))
        delta = dot(high, pick_ref[...]) + dot(low, pick_ref[...])
        high, mid, low = parts_of(delta)
        delta = jnp.where(lane < 32, high, jnp.where(lane < 40, mid, low))
        stats = jnp.where(lane < 24, norm.astype(BF), jnp.where(lane < 48, delta, doc_block))
        h = 0
        for index, ref in enumerate(qd_refs):
            count = ref.shape[1] // 2
            for c in range(count):
                cols = slice(first + h * HD, first + (h + 1) * HD)
                ref[i, c] = q_ref[:, cols]
                ref[i, count + c] = do_ref[:, cols]
                h += 1
            if index == 0:
                ref[i, 2 * count] = stats


def pack_q(queries, grad_out, attn_out, log_norm, doc_block):
    per = PACK_PER
    wide = pl.BlockSpec((TOK, per * HEADS_DEV * HD), lambda u: (0, u))
    shapes = [(8, 2 * c + (i == 0), TOK, HD) for i, c in enumerate(CHUNKS)]
    return pl.pallas_call(
        functools.partial(pack_q_kernel, per),
        grid=(8 // per,),
        in_specs=[
            wide,
            wide,
            wide,
            pl.BlockSpec(log_norm.shape, lambda u: (0, 0)),
            pl.BlockSpec(doc_block.shape, lambda u: (0, 0)),
        ],
        out_specs=[pl.BlockSpec((per,) + s[1:], lambda u: (u, 0, 0, 0)) for s in shapes],
        out_shape=[jax.ShapeDtypeStruct(s, BF) for s in shapes],
        scratch_shapes=[pltpu.VMEM((HEADS_DEV * HD, 128), BF)],
        compiler_params=pltpu.CompilerParams(vmem_limit_bytes=VMEM_LIMIT),
        cost_estimate=pl.CostEstimate(flops=0, bytes_accessed=11 << 20, transcendentals=0),
        name="pack_q",
    )(queries, grad_out, attn_out, log_norm, doc_block)


def attend_kernel(count, first_head, kv_counts, has_dkv, last, *refs):
    refs = list(refs)

    def take(n):
        head = refs[:n]
        del refs[:n]
        return head

    second_ref, qd_hbm, stat_hbm = take(3)
    kv_hbm = [take(n) for n in kv_counts]
    (kdoc_ref,) = take(1)
    (dkv_in,) = take(1) if has_dkv else (None,)
    (dq_ref,) = take(1)
    dkv_out = take(3 if last else 1)
    qt_ref, dot_ref, sel_ref, kv_ref, p_ref, ds_ref, dqt_ref, dst_ref = take(8)
    qd_ref, stat_ref, raw_ref, sum_ref, sems = take(5)
    (others_ref,) = take(1) if last else (None,)

    def qd_copy(half):
        rows = pl.ds(half * 4, 4)
        return pltpu.make_async_copy(
            qd_hbm.at[rows, 0 : 2 * count], qd_ref.at[rows], sems.at[half]
        )

    stat_copy = pltpu.make_async_copy(
        stat_hbm.at[:, stat_hbm.shape[1] - 1], stat_ref, sems.at[2]
    )
    loads = []
    slot = 0
    for step, sources in enumerate(kv_hbm):
        loads.append([])
        for source in sources:
            loads[-1].append(pltpu.make_async_copy(source, raw_ref.at[slot], sems.at[3 + slot]))
            slot += 1
        if has_dkv:
            loads[-1].append(
                pltpu.make_async_copy(dkv_in.at[step], sum_ref.at[step], sems.at[9 + step])
            )
    stores = []
    if last:
        own_out, others_out, three_out = dkv_out
        stores.append(pltpu.make_async_copy(sum_ref.at[0], own_out, sems.at[13]))
        for step in range(1, STEPS):
            stores.append(
                pltpu.make_async_copy(
                    others_ref.at[step - 1], others_out.at[step - 1], sems.at[13 + step]
                )
            )
        three_store = pltpu.make_async_copy(others_ref.at[STEPS - 2], three_out, sems.at[17])
    else:
        for step in range(STEPS):
            stores.append(
                pltpu.make_async_copy(sum_ref.at[step], dkv_out[0].at[step], sems.at[13 + step])
            )

    qd_copy(0).start()
    stat_copy.start()
    for copy in loads[0]:
        copy.start()
    qd_copy(1).start()
    for step_loads in loads[1:]:
        for copy in step_loads:
            copy.start()

    row = lax.broadcasted_iota(jnp.int32, (48, HALF), 0)
    for h in range(count):
        mine = row % HEADS_DEV == first_head + h
        sel_ref[h] = jnp.where(mine & (row < 24), -1.0, 0.0).astype(BF)
        sel_ref[count + h] = jnp.where(mine & (row >= 24), -1.0, 0.0).astype(BF)
    dqt_ref[...] = jnp.zeros_like(dqt_ref)
    if not has_dkv:
        sum_ref[...] = jnp.zeros_like(sum_ref)

    def begin(step):
        for copy in loads[step]:
            copy.wait()
        first = sum(kv_counts[:step])
        for half in range(2):
            for i in range(4):
                for pair in range(2):
                    block = raw_ref[first, half * 4 + i, pair]
                    for other in range(first + 1, first + kv_counts[step]):
                        block = block + raw_ref[other, half * 4 + i, pair]
                    kv_ref[step, pair, half, :, i * TOK : (i + 1) * TOK] = block

    def end(step):
        if last and step == 0:
            sum_ref[0, 0] = sum_ref[0, 0] * SCALE
        elif last:
            others_ref[step - 1, 0] = (sum_ref[step, 0] * SCALE).astype(BF)
            others_ref[step - 1, 1] = sum_ref[step, 1].astype(BF)
        stores[step].start()
        if last and step == STEPS - 1:
            three_store.start()

    def turn_rows(half):
        for i in range(4):
            cols = slice(i * TOK, (i + 1) * TOK)
            for h in range(count):
                qt_ref[half, h, :, cols] = qd_ref[half * 4 + i, h].T
                dot_ref[half, h, :, cols] = qd_ref[half * 4 + i, count + h].T

    def rows_of(qhalf, index, q0, qn):
        block = qd_ref[pl.ds(qhalf * 4 + q0 // TOK, qn // TOK), index]
        return block.reshape(qn, HD)

    def scores(index, qhalf, khalf, h, slot, q0, k0, bm, bn, diagonal):
        kcols = slice(k0, k0 + bn)
        k_ext = jnp.concatenate(
            [
                kv_ref[index, 0, khalf, :, kcols],
                sel_ref[h, :, kcols],
                kdoc_ref[index, khalf, :, kcols],
                jnp.zeros((64, bn), BF),
            ],
            axis=0,
        )
        v_ext = jnp.concatenate(
            [kv_ref[index, 1, khalf, :, kcols], sel_ref[count + h, :, kcols], jnp.zeros((80, bn), BF)],
            axis=0,
        )
        stats = stat_ref[pl.ds(qhalf * 4 + q0 // TOK, bm // TOK)].reshape(bm, HD)
        q_ext = jnp.concatenate([rows_of(qhalf, h, q0, bm), stats], axis=1)
        do_ext = jnp.concatenate([rows_of(qhalf, count + h, q0, bm), stats], axis=1)
        prob = jnp.exp2(dot(q_ext, k_ext) * EXP2_SCALE)
        if diagonal:
            qi = lax.broadcasted_iota(jnp.int32, (bm, bn), 0) + q0
            ki = lax.broadcasted_iota(jnp.int32, (bm, bn), 1) + k0
            prob = jnp.where(qi >= ki, prob, 0.0)
        rows = slice(q0, q0 + bm)
        dscore = (prob * dot(do_ext, v_ext)).astype(BF)
        ds_ref[slot, rows, kcols] = dscore
        dst_ref[slot, kcols, rows] = dscore.T
        p_ref[slot, rows, kcols] = prob.astype(BF)

    def grads(index, qhalf, khalf, heads, diagonal):
        for k0, kn, q0 in ((0, 256, 0), (256, 256, 256)) if diagonal else ((0, HALF, 0),):
            span = slice(q0, HALF)
            cols = slice(k0, k0 + kn)
            for pair, left_ref, right_ref in ((1, dot_ref, p_ref), (0, qt_ref, ds_ref)):
                left = jnp.concatenate([left_ref[qhalf, h, :, span] for h in heads], axis=1)
                right = jnp.concatenate([right_ref[h, span, cols] for h in heads], axis=0)
                sum_ref[index, pair, khalf, :, cols] += dot(left, right)
        for q0, qn, kn in ((0, 256, 256), (256, 256, 512)) if diagonal else ((0, HALF, HALF),):
            span = slice(q0, q0 + qn)
            for h in heads:
                dqt_ref[qhalf, h, :, span] += dot(
                    kv_ref[index, 0, khalf, :, :kn], dst_ref[h, :kn, span]
                )

    def tile(index, qhalf, khalf, diagonal):
        groups = [range(h, min(h + GROUP, count)) for h in range(0, count, GROUP)]
        for turn, heads in enumerate(groups):
            for h in heads:
                for k0 in range(0, HALF, BN):
                    for q0 in range(0, HALF, BM):
                        if diagonal and q0 + BM <= k0:
                            continue
                        scores(index, qhalf, khalf, h, h, q0, k0, BM, BN, diagonal and q0 < k0 + BN)
            if turn:
                grads(index, qhalf, khalf, groups[turn - 1], diagonal)
        grads(index, qhalf, khalf, groups[-1], diagonal)

    stat_copy.wait()
    begin(0)

    def diagonal(half, carry):
        qd_copy(half).wait()
        turn_rows(half)
        tile(0, half, half, True)
        return carry

    lax.fori_loop(0, 2, diagonal, 0)
    tile(0, 1, 0, False)
    end(0)
    for step in range(1, STEPS):
        begin(step)

        def both(turn, carry, step=step):
            second = second_ref[step]
            tile(step, jnp.where(turn == 0, 1, second), jnp.where(turn == 0, 0, second), False)
            return carry

        lax.fori_loop(0, 2, both, 0)
        end(step)

    for half in range(2):
        for h in range(count):
            for i in range(4):
                piece = dqt_ref[half, h, :, i * TOK : (i + 1) * TOK]
                dq_ref[half * 4 + i, h] = (piece * SCALE).astype(BF).T
    for copy in stores:
        copy.wait()
    if last:
        three_store.wait()


def attend(chunk, second, qd, stats, kvs, kdoc, dkv, last):
    first_head, count = sum(CHUNKS[:chunk]), CHUNKS[chunk]
    operands = [second, qd, stats]
    for sources in kvs:
        operands += sources
    operands.append(kdoc)
    operands += [] if dkv is None else [dkv]
    vmem = pl.BlockSpec(memory_space=pltpu.VMEM)
    anywhere = pl.BlockSpec(memory_space=pl.ANY)
    flops = int(8.5 * 5 * 2 * HALF * HALF * HD * count)
    sums = (STEPS, 2, 2, HD, HALF)
    shapes = [((8, count, TOK, HD), BF)]
    shapes += [(sums[1:], F32), ((3,) + sums[1:], BF), (sums[1:], BF)] if last else [(sums, F32)]
    kernel = functools.partial(
        attend_kernel,
        count,
        first_head,
        [len(sources) for sources in kvs],
        dkv is not None,
        last,
    )
    return pl.pallas_call(
        kernel,
        in_specs=[
            pl.BlockSpec(memory_space=pltpu.SMEM),
            *[anywhere] * (2 + sum(len(sources) for sources in kvs)),
            vmem,
            *[anywhere] * (dkv is not None),
        ],
        out_specs=[vmem] + [anywhere] * (len(shapes) - 1),
        out_shape=[jax.ShapeDtypeStruct(*shape) for shape in shapes],
        scratch_shapes=[
            pltpu.VMEM((2, count, HD, HALF), BF),
            pltpu.VMEM((2, count, HD, HALF), BF),
            pltpu.VMEM((2 * count, 48, HALF), BF),
            pltpu.VMEM(sums, BF),
            pltpu.VMEM((count, HALF, HALF), BF),
            pltpu.VMEM((count, HALF, HALF), BF),
            pltpu.VMEM((2, count, HD, HALF), F32),
            pltpu.VMEM((count, HALF, HALF), BF),
            pltpu.VMEM((8, 2 * count, TOK, HD), BF),
            pltpu.VMEM((8, TOK, HD), BF),
            pltpu.VMEM((sum(len(sources) for sources in kvs), 8, 2, HD, TOK), BF),
            pltpu.VMEM(sums, F32),
            pltpu.SemaphoreType.DMA((18,)),
        ]
        + ([pltpu.VMEM((3,) + sums[1:], BF)] if last else []),
        compiler_params=pltpu.CompilerParams(vmem_limit_bytes=VMEM_LIMIT),
        cost_estimate=pl.CostEstimate(
            flops=2 * flops, bytes_accessed=8 << 20, transcendentals=8 * HALF * HALF * count
        ),
        name="attend",
    )(*operands)


def join_kernel(mine_ref, inner_two_ref, inner_three_ref, to_one_ref, to_two_ref):
    to_one_ref[...] = (mine_ref[0].astype(F32) + inner_two_ref[0].astype(F32)).astype(BF)
    to_two_ref[...] = (mine_ref[1].astype(F32) + inner_three_ref[0].astype(F32)).astype(BF)


def join(mine, theirs):
    def block(steps, first):
        return pl.BlockSpec((steps, 1, 2, HD, HALF), lambda pair: (first, pair, 0, 0, 0))

    out = pl.BlockSpec((1, 2, HD, HALF), lambda pair: (pair, 0, 0, 0))
    shape = jax.ShapeDtypeStruct(mine.shape[1:], BF)
    return pl.pallas_call(
        join_kernel,
        grid=(2,),
        in_specs=[block(2, 0), block(1, 1), block(1, 2)],
        out_specs=[out, out],
        out_shape=[shape, shape],
        compiler_params=pltpu.CompilerParams(vmem_limit_bytes=VMEM_LIMIT),
        cost_estimate=pl.CostEstimate(flops=0, bytes_accessed=3 << 20, transcendentals=0),
        name="join",
    )(mine, theirs, theirs)


def total_kernel(own_ref, theirs_ref, *refs):
    *part_refs, out_ref = refs
    for half in range(2):
        total = own_ref[0, half] + theirs_ref[0, 0, half].astype(F32)
        for ref in part_refs:
            total += ref[0, half].astype(F32)
        for i in range(4):
            out_ref[half * 4 + i, 0] = total[:, i * TOK : (i + 1) * TOK].astype(BF).T


def total(own, theirs, *parts):
    part = pl.BlockSpec((1, 2, HD, HALF), lambda pair: (pair, 0, 0, 0))
    return pl.pallas_call(
        total_kernel,
        grid=(2,),
        in_specs=[
            part,
            pl.BlockSpec((1, 1, 2, HD, HALF), lambda pair: (0, pair, 0, 0, 0)),
            *[part] * len(parts),
        ],
        out_specs=pl.BlockSpec((8, 1, TOK, HD), lambda pair: (0, pair, 0, 0)),
        out_shape=jax.ShapeDtypeStruct((8, 2, TOK, HD), BF),
        compiler_params=pltpu.CompilerParams(vmem_limit_bytes=VMEM_LIMIT),
        cost_estimate=pl.CostEstimate(flops=0, bytes_accessed=4 << 20, transcendentals=0),
        name="total",
    )(own, theirs, *parts)


def unpack_q_kernel(per, *refs):
    out_ref = refs[-1]
    for u in range(per):
        h = u * HEADS_DEV
        for ref in refs[:-1]:
            for i in range(ref.shape[1]):
                out_ref[:, h * HD : (h + 1) * HD] = ref[u, i]
                h += 1


def unpack_q(parts):
    per = PACK_PER
    return pl.pallas_call(
        functools.partial(unpack_q_kernel, per),
        grid=(8 // per,),
        in_specs=[pl.BlockSpec((per,) + p.shape[1:], lambda u: (u, 0, 0, 0)) for p in parts],
        out_specs=pl.BlockSpec((TOK, per * HEADS_DEV * HD), lambda u: (0, u)),
        out_shape=jax.ShapeDtypeStruct((TOK, 8 * HEADS_DEV * HD), BF),
        compiler_params=pltpu.CompilerParams(vmem_limit_bytes=VMEM_LIMIT),
        cost_estimate=pl.CostEstimate(flops=0, bytes_accessed=4 << 20, transcendentals=0),
        name="unpack_q",
    )(*parts)


def unpack_kv_kernel(pair_ref, k_ref, v_ref, sems):
    copies = []
    for u in range(8):
        for i, ref in enumerate((k_ref, v_ref)):
            target = ref.at[:, u * HD : (u + 1) * HD]
            copies.append(pltpu.make_async_copy(pair_ref.at[u, i], target, sems.at[u, i]))
    for copy in copies:
        copy.start()
    for copy in copies:
        copy.wait()


def unpack_kv(pair):
    shape = jax.ShapeDtypeStruct((TOK, 8 * HD), BF)
    anywhere = pl.BlockSpec(memory_space=pl.ANY)
    return pl.pallas_call(
        unpack_kv_kernel,
        in_specs=[anywhere],
        out_specs=[anywhere, anywhere],
        out_shape=[shape, shape],
        scratch_shapes=[pltpu.SemaphoreType.DMA((8, 2))],
        compiler_params=pltpu.CompilerParams(vmem_limit_bytes=VMEM_LIMIT),
        name="unpack_kv",
    )(pair)


def move(value, pairs):
    return lax.ppermute(value, "blk", pairs)


def exchange(value):
    return lax.all_to_all(value, "uly", split_axis=0, concat_axis=0, tiled=True)


def local(queries, key_rows, value_rows, grad_out, attn_out, log_norm, doc_ids):
    groups = lax.axis_size("blk")
    group = lax.axis_index("blk")
    kdocs = []
    for step in range(STEPS):
        owner = (group - step) % groups
        low = lax.dynamic_slice_in_dim(doc_ids, owner * HALF, HALF)
        high = lax.dynamic_slice_in_dim(doc_ids, (2 * groups - 1 - owner) * HALF, HALF)
        kdocs.append(jnp.stack([low, high]))
    kdocs = jnp.stack(kdocs)
    kdoc = jnp.where(
        kdocs[:, :, None, :] == jnp.arange(16, dtype=jnp.int32)[None, None, :, None], -1.0, 0.0
    ).astype(BF)
    second = jnp.where(group >= jnp.arange(STEPS), 0, 1).astype(jnp.int32)

    chips = range(groups // 2)
    up = [(i, (i + 1) % groups) for i in range(groups)]
    inner_up = [(2 * m, 2 * m + 1) for m in chips]
    inner_down = [(2 * m + 1, 2 * m) for m in chips]
    down = [[(2 * m, (2 * m - step) % groups) for m in chips] for step in range(STEPS)]

    kv = exchange(pack_kv(key_rows, value_rows))
    one = move(kv, up)
    two, three = (move(kv, [(b, a) for a, b in down[step]]) for step in (2, 3))
    two_inner, three_inner = (move(part, inner_up) for part in (one, two))
    kvs = [[kv], [one], [two, two_inner], [three, three_inner]]

    packed = pack_q(queries, grad_out, attn_out, log_norm.T, doc_ids.reshape(-1, TOK))
    early = exchange(packed[0])
    late, *_ = lax.optimization_barrier((packed[1], early))
    late = exchange(late)
    dq_early, dkv = attend(0, second, early, early, kvs, kdoc, None, False)
    dq_early, *_ = lax.optimization_barrier((dq_early, late))
    dq_early = exchange(dq_early)
    dq_late, own, others, far = attend(1, second, late, early, kvs, kdoc, dkv, True)

    others, dq_early = lax.optimization_barrier((others, dq_early))
    theirs = move(others, inner_down)
    dq_late = exchange(dq_late)
    from_three = move(far, down[3])
    to_one, to_two = join(others, theirs)
    from_one, from_two = move(to_one, down[1]), move(to_two, down[2])
    pair = total(own, theirs, from_one, from_two, from_three)
    pair, *_ = lax.optimization_barrier((pair, dq_late))
    grad_keys, grad_values = unpack_kv(exchange(pair))
    return unpack_q([dq_early, dq_late]), grad_keys, grad_values


def solution(mesh):
    rows = P(("blk", "uly"), None)
    return jax.shard_map(
        local,
        mesh=mesh,
        in_specs=(rows, rows, rows, rows, rows, rows, P()),
        out_specs=(rows, rows, rows),
        check_vma=False,
    )
```

```python
import functools
import math

import jax
import jax.numpy as jnp
from jax import lax
from jax.experimental import pallas as pl
from jax.experimental.pallas import tpu as pltpu
from jax.sharding import PartitionSpec as P

HD = 128
STEPS = 4
DOCS = 8
TOK = 128
HEADS_DEV = 8
HALF = 512
CHUNKS = (4, 4)
PARTS = 3
FAR = 32768.0
SCALE = HD ** (-0.5)
EXP2_SCALE = SCALE * math.log2(math.e)
NORM_SCALE = HD ** 0.5
BF = jnp.bfloat16
F32 = jnp.float32
BM, BN, PIPE = 256, 256, True
BM, BN = 256, 256
GROUP = 4
PACK_PER = 4
VMEM_LIMIT = 60 * 1024 * 1024

NN = (((1,), (0,)), ((), ()))
NT = (((1,), (1,)), ((), ()))
TN = (((0,), (0,)), ((), ()))


def dot(a, b, dims=NN):
    return lax.dot_general(a, b, dims, preferred_element_type=F32)


def parts_of(x):
    high = x.astype(BF)
    rest = x - high.astype(F32)
    mid = rest.astype(BF)
    low = (rest - mid.astype(F32)).astype(BF)
    return high, mid, low


def pack_kv_kernel(k_ref, v_ref, kv_ref):
    for u in range(8):
        kv_ref[u, 0] = k_ref[:, u * HD : (u + 1) * HD].T
        kv_ref[u, 1] = v_ref[:, u * HD : (u + 1) * HD].T


def pack_kv(key_rows, value_rows):
    return pl.pallas_call(
        pack_kv_kernel,
        out_shape=jax.ShapeDtypeStruct((8, 2, HD, TOK), BF),
        compiler_params=pltpu.CompilerParams(vmem_limit_bytes=VMEM_LIMIT),
        cost_estimate=pl.CostEstimate(flops=0, bytes_accessed=1 << 20, transcendentals=0),
        name="pack_kv",
    )(key_rows, value_rows)


def pack_q_kernel(per, q_ref, do_ref, o_ref, ln_ref, doc_ref, *refs):
    *qd_refs, pick_ref = refs
    step = pl.program_id(0)
    group, member = lax.axis_index("blk"), lax.axis_index("uly")
    groups = lax.axis_size("blk")
    heads = ln_ref.shape[0]
    width = HEADS_DEV * HD

    @pl.when(step == 0)
    def _():
        head = lax.broadcasted_iota(jnp.int32, pick_ref.shape, 0) // HD
        col = lax.broadcasted_iota(jnp.int32, pick_ref.shape, 1)
        pick = (col >= 24) & (col < 48) & (head == col % HEADS_DEV)
        pick_ref[...] = jnp.where(pick, 1.0, 0.0).astype(BF)

    head = lax.broadcasted_iota(jnp.int32, (heads, 128), 0)
    col = lax.broadcasted_iota(jnp.int32, (heads, 128), 1)
    lane = lax.broadcasted_iota(jnp.int32, (TOK, 128), 1)
    quarters = HALF // TOK
    low = group * quarters + member
    high = (2 * groups - 1 - group) * quarters + member - quarters
    spot = jnp.where(member < quarters, low, high)
    docs = doc_ref[pl.ds(spot, 1), :].astype(F32)
    row = lax.broadcasted_iota(jnp.int32, (TOK, 128), 0)
    docs = jnp.where(row == lane, jnp.broadcast_to(docs, (TOK, 128)), 0.0).astype(BF)
    docs = dot(docs, jnp.ones((128, 128), BF))
    other = (lane < 48 + DOCS) & (docs != (lane - 48).astype(F32))
    doc_block = jnp.where(other, FAR, 0.0).astype(BF)
    norm_parts = parts_of(ln_ref[...] * NORM_SCALE)
    for i in range(per):
        first = i * width
        norm = jnp.zeros((TOK, 128), F32)
        for j, part in enumerate(norm_parts):
            mine = head == (step * per + i) * HEADS_DEV + col % HEADS_DEV
            pick = (col // HEADS_DEV == j) & mine
            norm += dot(part, jnp.where(pick, 1.0, 0.0).astype(BF), TN)
        cols = slice(first, first + width)
        high, low, _ = parts_of(do_ref[:, cols].astype(F32) * o_ref[:, cols].astype(F32))
        delta = dot(high, pick_ref[...]) + dot(low, pick_ref[...])
        high, mid, low = parts_of(delta)
        delta = jnp.where(lane < 32, high, jnp.where(lane < 40, mid, low))
        stats = jnp.where(lane < 24, norm.astype(BF), jnp.where(lane < 48, delta, doc_block))
        h = 0
        for index, ref in enumerate(qd_refs):
            count = ref.shape[1] // 2
            for c in range(count):
                cols = slice(first + h * HD, first + (h + 1) * HD)
                ref[i, c] = q_ref[:, cols]
                ref[i, count + c] = do_ref[:, cols]
                h += 1
            if index == 0:
                ref[i, 2 * count] = stats


def pack_q(queries, grad_out, attn_out, log_norm, doc_block):
    per = PACK_PER
    wide = pl.BlockSpec((TOK, per * HEADS_DEV * HD), lambda u: (0, u))
    shapes = [(8, 2 * c + (i == 0), TOK, HD) for i, c in enumerate(CHUNKS)]
    return pl.pallas_call(
        functools.partial(pack_q_kernel, per),
        grid=(8 // per,),
        in_specs=[
            wide,
            wide,
            wide,
            pl.BlockSpec(log_norm.shape, lambda u: (0, 0)),
            pl.BlockSpec(doc_block.shape, lambda u: (0, 0)),
        ],
        out_specs=[pl.BlockSpec((per,) + s[1:], lambda u: (u, 0, 0, 0)) for s in shapes],
        out_shape=[jax.ShapeDtypeStruct(s, BF) for s in shapes],
        scratch_shapes=[pltpu.VMEM((HEADS_DEV * HD, 128), BF)],
        compiler_params=pltpu.CompilerParams(vmem_limit_bytes=VMEM_LIMIT),
        cost_estimate=pl.CostEstimate(flops=0, bytes_accessed=11 << 20, transcendentals=0),
        name="pack_q",
    )(queries, grad_out, attn_out, log_norm, doc_block)


def attend_kernel(count, first_head, kv_counts, has_dkv, last, *refs):
    refs = list(refs)

    def take(n):
        head = refs[:n]
        del refs[:n]
        return head

    second_ref, qd_hbm, stat_hbm = take(3)
    kv_hbm = [take(n) for n in kv_counts]
    (kdoc_ref,) = take(1)
    (dkv_in,) = take(1) if has_dkv else (None,)
    (dq_ref,) = take(1)
    dkv_out = take(3 if last else 1)
    qt_ref, dot_ref, sel_ref, kv_ref, p_ref, ds_ref, dqt_ref, dst_ref = take(8)
    qd_ref, stat_ref, raw_ref, sum_ref, sems = take(5)
    (others_ref,) = take(1) if last else (None,)

    def qd_copy(half):
        rows = pl.ds(half * 4, 4)
        return pltpu.make_async_copy(
            qd_hbm.at[rows, 0 : 2 * count], qd_ref.at[rows], sems.at[half]
        )

    stat_copy = pltpu.make_async_copy(
        stat_hbm.at[:, stat_hbm.shape[1] - 1], stat_ref, sems.at[2]
    )
    loads = []
    slot = 0
    for step, sources in enumerate(kv_hbm):
        loads.append([])
        for source in sources:
            loads[-1].append(pltpu.make_async_copy(source, raw_ref.at[slot], sems.at[3 + slot]))
            slot += 1
        if has_dkv:
            loads[-1].append(
                pltpu.make_async_copy(dkv_in.at[step], sum_ref.at[step], sems.at[9 + step])
            )
    stores = []
    if last:
        own_out, others_out, three_out = dkv_out
        stores.append(pltpu.make_async_copy(sum_ref.at[0], own_out, sems.at[13]))
        for step in range(1, STEPS):
            stores.append(
                pltpu.make_async_copy(
                    others_ref.at[step - 1], others_out.at[step - 1], sems.at[13 + step]
                )
            )
        three_store = pltpu.make_async_copy(others_ref.at[STEPS - 2], three_out, sems.at[17])
    else:
        for step in range(STEPS):
            stores.append(
                pltpu.make_async_copy(sum_ref.at[step], dkv_out[0].at[step], sems.at[13 + step])
            )

    qd_copy(0).start()
    stat_copy.start()
    for copy in loads[0]:
        copy.start()
    qd_copy(1).start()
    for step_loads in loads[1:]:
        for copy in step_loads:
            copy.start()

    row = lax.broadcasted_iota(jnp.int32, (48, HALF), 0)
    for h in range(count):
        mine = row % HEADS_DEV == first_head + h
        sel_ref[h] = jnp.where(mine & (row < 24), -1.0, 0.0).astype(BF)
        sel_ref[count + h] = jnp.where(mine & (row >= 24), -1.0, 0.0).astype(BF)
    dqt_ref[...] = jnp.zeros_like(dqt_ref)
    if not has_dkv:
        sum_ref[...] = jnp.zeros_like(sum_ref)

    def begin(step):
        for copy in loads[step]:
            copy.wait()
        first = sum(kv_counts[:step])
        for half in range(2):
            for i in range(4):
                for pair in range(2):
                    block = raw_ref[first, half * 4 + i, pair]
                    for other in range(first + 1, first + kv_counts[step]):
                        block = block + raw_ref[other, half * 4 + i, pair]
                    kv_ref[step, pair, half, :, i * TOK : (i + 1) * TOK] = block

    def end(step):
        if last and step == 0:
            sum_ref[0, 0] = sum_ref[0, 0] * SCALE
        elif last:
            others_ref[step - 1, 0] = (sum_ref[step, 0] * SCALE).astype(BF)
            others_ref[step - 1, 1] = sum_ref[step, 1].astype(BF)
        stores[step].start()
        if last and step == STEPS - 1:
            three_store.start()

    def turn_rows(half):
        for i in range(4):
            cols = slice(i * TOK, (i + 1) * TOK)
            for h in range(count):
                qt_ref[half, h, :, cols] = qd_ref[half * 4 + i, h].T
                dot_ref[half, h, :, cols] = qd_ref[half * 4 + i, count + h].T

    def rows_of(qhalf, index, q0, qn):
        block = qd_ref[pl.ds(qhalf * 4 + q0 // TOK, qn // TOK), index]
        return block.reshape(qn, HD)

    def scores(index, qhalf, khalf, h, slot, q0, k0, bm, bn, diagonal):
        kcols = slice(k0, k0 + bn)
        k_ext = jnp.concatenate(
            [
                kv_ref[index, 0, khalf, :, kcols],
                sel_ref[h, :, kcols],
                kdoc_ref[index, khalf, :, kcols],
                jnp.zeros((64, bn), BF),
            ],
            axis=0,
        )
        v_ext = jnp.concatenate(
            [kv_ref[index, 1, khalf, :, kcols], sel_ref[count + h, :, kcols], jnp.zeros((80, bn), BF)],
            axis=0,
        )
        stats = stat_ref[pl.ds(qhalf * 4 + q0 // TOK, bm // TOK)].reshape(bm, HD)
        q_ext = jnp.concatenate([rows_of(qhalf, h, q0, bm), stats], axis=1)
        do_ext = jnp.concatenate([rows_of(qhalf, count + h, q0, bm), stats], axis=1)
        prob = jnp.exp2(dot(q_ext, k_ext) * EXP2_SCALE)
        if diagonal:
            qi = lax.broadcasted_iota(jnp.int32, (bm, bn), 0) + q0
            ki = lax.broadcasted_iota(jnp.int32, (bm, bn), 1) + k0
            prob = jnp.where(qi >= ki, prob, 0.0)
        rows = slice(q0, q0 + bm)
        dscore = (prob * dot(do_ext, v_ext)).astype(BF)
        ds_ref[slot, rows, kcols] = dscore
        dst_ref[slot, kcols, rows] = dscore.T
        p_ref[slot, rows, kcols] = prob.astype(BF)

    def grads(index, qhalf, khalf, heads, diagonal):
        for k0, kn, q0 in ((0, 256, 0), (256, 256, 256)) if diagonal else ((0, HALF, 0),):
            span = slice(q0, HALF)
            cols = slice(k0, k0 + kn)
            for pair, left_ref, right_ref in ((1, dot_ref, p_ref), (0, qt_ref, ds_ref)):
                left = jnp.concatenate([left_ref[qhalf, h, :, span] for h in heads], axis=1)
                right = jnp.concatenate([right_ref[h, span, cols] for h in heads], axis=0)
                sum_ref[index, pair, khalf, :, cols] += dot(left, right)
        for q0, qn, kn in ((0, 256, 256), (256, 256, 512)) if diagonal else ((0, HALF, HALF),):
            span = slice(q0, q0 + qn)
            for h in heads:
                dqt_ref[qhalf, h, :, span] += dot(
                    kv_ref[index, 0, khalf, :, :kn], dst_ref[h, :kn, span]
                )

    def tile(index, qhalf, khalf, diagonal):
        groups = [range(h, min(h + GROUP, count)) for h in range(0, count, GROUP)]
        for turn, heads in enumerate(groups):
            for h in heads:
                for k0 in range(0, HALF, BN):
                    for q0 in range(0, HALF, BM):
                        if diagonal and q0 + BM <= k0:
                            continue
                        scores(index, qhalf, khalf, h, h, q0, k0, BM, BN, diagonal and q0 < k0 + BN)
            if turn:
                grads(index, qhalf, khalf, groups[turn - 1], diagonal)
        grads(index, qhalf, khalf, groups[-1], diagonal)

    stat_copy.wait()
    begin(0)

    def diagonal(half, carry):
        qd_copy(half).wait()
        turn_rows(half)
        tile(0, half, half, True)
        return carry

    lax.fori_loop(0, 2, diagonal, 0)
    tile(0, 1, 0, False)
    end(0)
    for step in range(1, STEPS):
        begin(step)

        def both(turn, carry, step=step):
            second = second_ref[step]
            tile(step, jnp.where(turn == 0, 1, second), jnp.where(turn == 0, 0, second), False)
            return carry

        lax.fori_loop(0, 2, both, 0)
        end(step)

    for half in range(2):
        for h in range(count):
            for i in range(4):
                piece = dqt_ref[half, h, :, i * TOK : (i + 1) * TOK]
                dq_ref[half * 4 + i, h] = (piece * SCALE).astype(BF).T
    for copy in stores:
        copy.wait()
    if last:
        three_store.wait()


def attend(chunk, second, qd, stats, kvs, kdoc, dkv, last):
    first_head, count = sum(CHUNKS[:chunk]), CHUNKS[chunk]
    operands = [second, qd, stats]
    for sources in kvs:
        operands += sources
    operands.append(kdoc)
    operands += [] if dkv is None else [dkv]
    vmem = pl.BlockSpec(memory_space=pltpu.VMEM)
    anywhere = pl.BlockSpec(memory_space=pl.ANY)
    flops = int(8.5 * 5 * 2 * HALF * HALF * HD * count)
    sums = (STEPS, 2, 2, HD, HALF)
    shapes = [((8, count, TOK, HD), BF)]
    shapes += [(sums[1:], F32), ((3,) + sums[1:], BF), (sums[1:], BF)] if last else [(sums, F32)]
    kernel = functools.partial(
        attend_kernel,
        count,
        first_head,
        [len(sources) for sources in kvs],
        dkv is not None,
        last,
    )
    return pl.pallas_call(
        kernel,
        in_specs=[
            pl.BlockSpec(memory_space=pltpu.SMEM),
            *[anywhere] * (2 + sum(len(sources) for sources in kvs)),
            vmem,
            *[anywhere] * (dkv is not None),
        ],
        out_specs=[vmem] + [anywhere] * (len(shapes) - 1),
        out_shape=[jax.ShapeDtypeStruct(*shape) for shape in shapes],
        scratch_shapes=[
            pltpu.VMEM((2, count, HD, HALF), BF),
            pltpu.VMEM((2, count, HD, HALF), BF),
            pltpu.VMEM((2 * count, 48, HALF), BF),
            pltpu.VMEM(sums, BF),
            pltpu.VMEM((count, HALF, HALF), BF),
            pltpu.VMEM((count, HALF, HALF), BF),
            pltpu.VMEM((2, count, HD, HALF), F32),
            pltpu.VMEM((count, HALF, HALF), BF),
            pltpu.VMEM((8, 2 * count, TOK, HD), BF),
            pltpu.VMEM((8, TOK, HD), BF),
            pltpu.VMEM((sum(len(sources) for sources in kvs), 8, 2, HD, TOK), BF),
            pltpu.VMEM(sums, F32),
            pltpu.SemaphoreType.DMA((18,)),
        ]
        + ([pltpu.VMEM((3,) + sums[1:], BF)] if last else []),
        compiler_params=pltpu.CompilerParams(vmem_limit_bytes=VMEM_LIMIT),
        cost_estimate=pl.CostEstimate(
            flops=2 * flops, bytes_accessed=8 << 20, transcendentals=8 * HALF * HALF * count
        ),
        name="attend",
    )(*operands)


def join_kernel(mine_ref, inner_two_ref, inner_three_ref, to_one_ref, to_two_ref):
    to_one_ref[...] = (mine_ref[0].astype(F32) + inner_two_ref[0].astype(F32)).astype(BF)
    to_two_ref[...] = (mine_ref[1].astype(F32) + inner_three_ref[0].astype(F32)).astype(BF)


def join(mine, theirs):
    def block(steps, first):
        return pl.BlockSpec((steps, 1, 2, HD, HALF), lambda pair: (first, pair, 0, 0, 0))

    out = pl.BlockSpec((1, 2, HD, HALF), lambda pair: (pair, 0, 0, 0))
    shape = jax.ShapeDtypeStruct(mine.shape[1:], BF)
    return pl.pallas_call(
        join_kernel,
        grid=(2,),
        in_specs=[block(2, 0), block(1, 1), block(1, 2)],
        out_specs=[out, out],
        out_shape=[shape, shape],
        compiler_params=pltpu.CompilerParams(vmem_limit_bytes=VMEM_LIMIT),
        cost_estimate=pl.CostEstimate(flops=0, bytes_accessed=3 << 20, transcendentals=0),
        name="join",
    )(mine, theirs, theirs)


def total_kernel(own_ref, theirs_ref, *refs):
    *part_refs, out_ref = refs
    for half in range(2):
        total = own_ref[0, half] + theirs_ref[0, 0, half].astype(F32)
        for ref in part_refs:
            total += ref[0, half].astype(F32)
        for i in range(4):
            out_ref[half * 4 + i, 0] = total[:, i * TOK : (i + 1) * TOK].astype(BF).T


def total(own, theirs, *parts):
    part = pl.BlockSpec((1, 2, HD, HALF), lambda pair: (pair, 0, 0, 0))
    return pl.pallas_call(
        total_kernel,
        grid=(2,),
        in_specs=[
            part,
            pl.BlockSpec((1, 1, 2, HD, HALF), lambda pair: (0, pair, 0, 0, 0)),
            *[part] * len(parts),
        ],
        out_specs=pl.BlockSpec((8, 1, TOK, HD), lambda pair: (0, pair, 0, 0)),
        out_shape=jax.ShapeDtypeStruct((8, 2, TOK, HD), BF),
        compiler_params=pltpu.CompilerParams(vmem_limit_bytes=VMEM_LIMIT),
        cost_estimate=pl.CostEstimate(flops=0, bytes_accessed=4 << 20, transcendentals=0),
        name="total",
    )(own, theirs, *parts)


def unpack_q_kernel(per, *refs):
    out_ref = refs[-1]
    for u in range(per):
        h = u * HEADS_DEV
        for ref in refs[:-1]:
            for i in range(ref.shape[1]):
                out_ref[:, h * HD : (h + 1) * HD] = ref[u, i]
                h += 1


def unpack_q(parts):
    per = PACK_PER
    return pl.pallas_call(
        functools.partial(unpack_q_kernel, per),
        grid=(8 // per,),
        in_specs=[pl.BlockSpec((per,) + p.shape[1:], lambda u: (u, 0, 0, 0)) for p in parts],
        out_specs=pl.BlockSpec((TOK, per * HEADS_DEV * HD), lambda u: (0, u)),
        out_shape=jax.ShapeDtypeStruct((TOK, 8 * HEADS_DEV * HD), BF),
        compiler_params=pltpu.CompilerParams(vmem_limit_bytes=VMEM_LIMIT),
        cost_estimate=pl.CostEstimate(flops=0, bytes_accessed=4 << 20, transcendentals=0),
        name="unpack_q",
    )(*parts)


def unpack_kv_kernel(pair_ref, k_ref, v_ref):
    for u in range(8):
        k_ref[:, u * HD : (u + 1) * HD] = pair_ref[u, 0]
        v_ref[:, u * HD : (u + 1) * HD] = pair_ref[u, 1]


def unpack_kv(pair):
    shape = jax.ShapeDtypeStruct((TOK, 8 * HD), BF)
    return pl.pallas_call(
        unpack_kv_kernel,
        out_shape=[shape, shape],
        compiler_params=pltpu.CompilerParams(vmem_limit_bytes=VMEM_LIMIT),
        name="unpack_kv",
    )(pair)


def move(value, pairs):
    return lax.ppermute(value, "blk", pairs)


def exchange(value):
    return lax.all_to_all(value, "uly", split_axis=0, concat_axis=0, tiled=True)


def local(queries, key_rows, value_rows, grad_out, attn_out, log_norm, doc_ids):
    groups = lax.axis_size("blk")
    group = lax.axis_index("blk")
    kdocs = []
    for step in range(STEPS):
        owner = (group - step) % groups
        low = lax.dynamic_slice_in_dim(doc_ids, owner * HALF, HALF)
        high = lax.dynamic_slice_in_dim(doc_ids, (2 * groups - 1 - owner) * HALF, HALF)
        kdocs.append(jnp.stack([low, high]))
    kdocs = jnp.stack(kdocs)
    kdoc = jnp.where(
        kdocs[:, :, None, :] == jnp.arange(16, dtype=jnp.int32)[None, None, :, None], -1.0, 0.0
    ).astype(BF)
    second = jnp.where(group >= jnp.arange(STEPS), 0, 1).astype(jnp.int32)

    chips = range(groups // 2)
    up = [(i, (i + 1) % groups) for i in range(groups)]
    inner_up = [(2 * m, 2 * m + 1) for m in chips]
    inner_down = [(2 * m + 1, 2 * m) for m in chips]
    down = [[(2 * m, (2 * m - step) % groups) for m in chips] for step in range(STEPS)]

    kv = exchange(pack_kv(key_rows, value_rows))
    one = move(kv, up)
    two, three = (move(kv, [(b, a) for a, b in down[step]]) for step in (2, 3))
    two_inner, three_inner = (move(part, inner_up) for part in (one, two))
    kvs = [[kv], [one], [two, two_inner], [three, three_inner]]

    packed = pack_q(queries, grad_out, attn_out, log_norm.T, doc_ids.reshape(-1, TOK))
    early = exchange(packed[0])
    late, *_ = lax.optimization_barrier((packed[1], early))
    late = exchange(late)
    dq_early, dkv = attend(0, second, early, early, kvs, kdoc, None, False)
    dq_early, *_ = lax.optimization_barrier((dq_early, late))
    dq_early = exchange(dq_early)
    dq_late, own, others, far = attend(1, second, late, early, kvs, kdoc, dkv, True)

    others, dq_early = lax.optimization_barrier((others, dq_early))
    theirs = move(others, inner_down)
    dq_late = exchange(dq_late)
    from_three = move(far, down[3])
    to_one, to_two = join(others, theirs)
    from_one, from_two = move(to_one, down[1]), move(to_two, down[2])
    pair = total(own, theirs, from_one, from_two, from_three)
    pair, *_ = lax.optimization_barrier((pair, dq_late))
    grad_keys, grad_values = unpack_kv(exchange(pair))
    return unpack_q([dq_early, dq_late]), grad_keys, grad_values


def solution(mesh):
    rows = P(("blk", "uly"), None)
    return jax.shard_map(
        local,
        mesh=mesh,
        in_specs=(rows, rows, rows, rows, rows, rows, P()),
        out_specs=(rows, rows, rows),
        check_vma=False,
    )
```

```python
import functools
import math

import jax
import jax.numpy as jnp
from jax import lax
from jax.experimental import pallas as pl
from jax.experimental.pallas import tpu as pltpu
from jax.sharding import PartitionSpec as P

HD = 128
STEPS = 4
DOCS = 8
TOK = 128
HEADS_DEV = 8
HALF = 512
CHUNKS = (4, 4)
PARTS = 3
FAR = 32768.0
SCALE = HD ** (-0.5)
EXP2_SCALE = SCALE * math.log2(math.e)
NORM_SCALE = HD ** 0.5
BF = jnp.bfloat16
F32 = jnp.float32
BM, BN, PIPE = 256, 256, True
BM, BN = 256, 256
GROUP = 4
PACK_PER = 4
VMEM_LIMIT = 60 * 1024 * 1024

NN = (((1,), (0,)), ((), ()))
NT = (((1,), (1,)), ((), ()))
TN = (((0,), (0,)), ((), ()))


def dot(a, b, dims=NN):
    return lax.dot_general(a, b, dims, preferred_element_type=F32)


def parts_of(x):
    high = x.astype(BF)
    rest = x - high.astype(F32)
    mid = rest.astype(BF)
    low = (rest - mid.astype(F32)).astype(BF)
    return high, mid, low


def pack_kv_kernel(k_ref, v_ref, kv_ref):
    for u in range(8):
        kv_ref[u, 0] = k_ref[:, u * HD : (u + 1) * HD].T
        kv_ref[u, 1] = v_ref[:, u * HD : (u + 1) * HD].T


def pack_kv(key_rows, value_rows):
    return pl.pallas_call(
        pack_kv_kernel,
        out_shape=jax.ShapeDtypeStruct((8, 2, HD, TOK), BF),
        compiler_params=pltpu.CompilerParams(vmem_limit_bytes=VMEM_LIMIT),
        cost_estimate=pl.CostEstimate(flops=0, bytes_accessed=1 << 20, transcendentals=0),
        name="pack_kv",
    )(key_rows, value_rows)


def pack_q_kernel(per, q_ref, do_ref, o_ref, ln_ref, doc_ref, *refs):
    *qd_refs, pick_ref = refs
    step = pl.program_id(0)
    group, member = lax.axis_index("blk"), lax.axis_index("uly")
    groups = lax.axis_size("blk")
    heads = ln_ref.shape[0]
    width = HEADS_DEV * HD

    @pl.when(step == 0)
    def _():
        head = lax.broadcasted_iota(jnp.int32, pick_ref.shape, 0) // HD
        col = lax.broadcasted_iota(jnp.int32, pick_ref.shape, 1)
        pick = (col >= 24) & (col < 48) & (head == col % HEADS_DEV)
        pick_ref[...] = jnp.where(pick, 1.0, 0.0).astype(BF)

    head = lax.broadcasted_iota(jnp.int32, (heads, 128), 0)
    col = lax.broadcasted_iota(jnp.int32, (heads, 128), 1)
    lane = lax.broadcasted_iota(jnp.int32, (TOK, 128), 1)
    quarters = HALF // TOK
    low = group * quarters + member
    high = (2 * groups - 1 - group) * quarters + member - quarters
    spot = jnp.where(member < quarters, low, high)
    docs = doc_ref[pl.ds(spot, 1), :].astype(F32)
    row = lax.broadcasted_iota(jnp.int32, (TOK, 128), 0)
    docs = jnp.where(row == lane, jnp.broadcast_to(docs, (TOK, 128)), 0.0).astype(BF)
    docs = dot(docs, jnp.ones((128, 128), BF))
    other = (lane < 48 + DOCS) & (docs != (lane - 48).astype(F32))
    doc_block = jnp.where(other, FAR, 0.0).astype(BF)
    norm_parts = parts_of(ln_ref[...] * NORM_SCALE)
    for i in range(per):
        first = i * width
        norm = jnp.zeros((TOK, 128), F32)
        for j, part in enumerate(norm_parts):
            mine = head == (step * per + i) * HEADS_DEV + col % HEADS_DEV
            pick = (col // HEADS_DEV == j) & mine
            norm += dot(part, jnp.where(pick, 1.0, 0.0).astype(BF), TN)
        cols = slice(first, first + width)
        high, low, _ = parts_of(do_ref[:, cols].astype(F32) * o_ref[:, cols].astype(F32))
        delta = dot(high, pick_ref[...]) + dot(low, pick_ref[...])
        high, mid, low = parts_of(delta)
        delta = jnp.where(lane < 32, high, jnp.where(lane < 40, mid, low))
        stats = jnp.where(lane < 24, norm.astype(BF), jnp.where(lane < 48, delta, doc_block))
        h = 0
        for index, ref in enumerate(qd_refs):
            count = ref.shape[1] // 2
            for c in range(count):
                cols = slice(first + h * HD, first + (h + 1) * HD)
                ref[i, c] = q_ref[:, cols]
                ref[i, count + c] = do_ref[:, cols]
                h += 1
            if index == 0:
                ref[i, 2 * count] = stats


def pack_q(queries, grad_out, attn_out, log_norm, doc_block):
    per = PACK_PER
    wide = pl.BlockSpec((TOK, per * HEADS_DEV * HD), lambda u: (0, u))
    shapes = [(8, 2 * c + (i == 0), TOK, HD) for i, c in enumerate(CHUNKS)]
    return pl.pallas_call(
        functools.partial(pack_q_kernel, per),
        grid=(8 // per,),
        in_specs=[
            wide,
            wide,
            wide,
            pl.BlockSpec(log_norm.shape, lambda u: (0, 0)),
            pl.BlockSpec(doc_block.shape, lambda u: (0, 0)),
        ],
        out_specs=[pl.BlockSpec((per,) + s[1:], lambda u: (u, 0, 0, 0)) for s in shapes],
        out_shape=[jax.ShapeDtypeStruct(s, BF) for s in shapes],
        scratch_shapes=[pltpu.VMEM((HEADS_DEV * HD, 128), BF)],
        compiler_params=pltpu.CompilerParams(vmem_limit_bytes=VMEM_LIMIT),
        cost_estimate=pl.CostEstimate(flops=0, bytes_accessed=11 << 20, transcendentals=0),
        name="pack_q",
    )(queries, grad_out, attn_out, log_norm, doc_block)


def attend_kernel(count, first_head, kv_counts, has_dkv, last, *refs):
    refs = list(refs)

    def take(n):
        head = refs[:n]
        del refs[:n]
        return head

    second_ref, qd_hbm, stat_hbm = take(3)
    kv_hbm = [take(n) for n in kv_counts]
    (kdoc_ref,) = take(1)
    (dkv_in,) = take(1) if has_dkv else (None,)
    (dq_ref,) = take(1)
    dkv_out = take(3 if last else 1)
    qt_ref, dot_ref, sel_ref, kv_ref, p_ref, ds_ref, dqt_ref, dst_ref = take(8)
    qd_ref, stat_ref, raw_ref, sum_ref, sems = take(5)
    (others_ref,) = take(1) if last else (None,)

    def qd_copy(half):
        rows = pl.ds(half * 4, 4)
        return pltpu.make_async_copy(
            qd_hbm.at[rows, 0 : 2 * count], qd_ref.at[rows], sems.at[half]
        )

    stat_copy = pltpu.make_async_copy(
        stat_hbm.at[:, stat_hbm.shape[1] - 1], stat_ref, sems.at[2]
    )
    loads = []
    slot = 0
    for step, sources in enumerate(kv_hbm):
        loads.append([])
        for source in sources:
            loads[-1].append(pltpu.make_async_copy(source, raw_ref.at[slot], sems.at[3 + slot]))
            slot += 1
        if has_dkv:
            loads[-1].append(
                pltpu.make_async_copy(dkv_in.at[step], sum_ref.at[step], sems.at[9 + step])
            )
    stores = []
    if last:
        own_out, others_out, three_out = dkv_out
        stores.append(pltpu.make_async_copy(sum_ref.at[0], own_out, sems.at[13]))
        for step in range(1, STEPS):
            stores.append(
                pltpu.make_async_copy(
                    others_ref.at[step - 1], others_out.at[step - 1], sems.at[13 + step]
                )
            )
        three_store = pltpu.make_async_copy(others_ref.at[STEPS - 2], three_out, sems.at[17])
    else:
        for step in range(STEPS):
            stores.append(
                pltpu.make_async_copy(sum_ref.at[step], dkv_out[0].at[step], sems.at[13 + step])
            )

    qd_copy(0).start()
    stat_copy.start()
    for copy in loads[0]:
        copy.start()
    qd_copy(1).start()
    for step_loads in loads[1:]:
        for copy in step_loads:
            copy.start()

    row = lax.broadcasted_iota(jnp.int32, (48, HALF), 0)
    for h in range(count):
        mine = row % HEADS_DEV == first_head + h
        sel_ref[h] = jnp.where(mine & (row < 24), -1.0, 0.0).astype(BF)
        sel_ref[count + h] = jnp.where(mine & (row >= 24), -1.0, 0.0).astype(BF)
    dqt_ref[...] = jnp.zeros_like(dqt_ref)
    if not has_dkv:
        sum_ref[...] = jnp.zeros_like(sum_ref)

    def begin(step):
        for copy in loads[step]:
            copy.wait()
        first = sum(kv_counts[:step])
        for half in range(2):
            for i in range(4):
                for pair in range(2):
                    block = raw_ref[first, half * 4 + i, pair]
                    for other in range(first + 1, first + kv_counts[step]):
                        block = block + raw_ref[other, half * 4 + i, pair]
                    kv_ref[step, pair, half, :, i * TOK : (i + 1) * TOK] = block

    def end(step):
        if last and step == 0:
            sum_ref[0, 0] = sum_ref[0, 0] * SCALE
        elif last:
            others_ref[step - 1, 0] = (sum_ref[step, 0] * SCALE).astype(BF)
            others_ref[step - 1, 1] = sum_ref[step, 1].astype(BF)
        stores[step].start()
        if last and step == STEPS - 1:
            three_store.start()

    def turn_rows(half):
        for i in range(4):
            cols = slice(i * TOK, (i + 1) * TOK)
            for h in range(count):
                qt_ref[half, h, :, cols] = qd_ref[half * 4 + i, h].T
                dot_ref[half, h, :, cols] = qd_ref[half * 4 + i, count + h].T

    def rows_of(qhalf, index, q0, qn):
        block = qd_ref[pl.ds(qhalf * 4 + q0 // TOK, qn // TOK), index]
        return block.reshape(qn, HD)

    def scores(index, qhalf, khalf, h, slot, q0, k0, bm, bn, diagonal):
        kcols = slice(k0, k0 + bn)
        k_ext = jnp.concatenate(
            [
                kv_ref[index, 0, khalf, :, kcols],
                sel_ref[h, :, kcols],
                kdoc_ref[index, khalf, :, kcols],
                jnp.zeros((64, bn), BF),
            ],
            axis=0,
        )
        v_ext = jnp.concatenate(
            [kv_ref[index, 1, khalf, :, kcols], sel_ref[count + h, :, kcols], jnp.zeros((80, bn), BF)],
            axis=0,
        )
        stats = stat_ref[pl.ds(qhalf * 4 + q0 // TOK, bm // TOK)].reshape(bm, HD)
        q_ext = jnp.concatenate([rows_of(qhalf, h, q0, bm), stats], axis=1)
        do_ext = jnp.concatenate([rows_of(qhalf, count + h, q0, bm), stats], axis=1)
        prob = jnp.exp2(dot(q_ext, k_ext) * EXP2_SCALE)
        if diagonal:
            qi = lax.broadcasted_iota(jnp.int32, (bm, bn), 0) + q0
            ki = lax.broadcasted_iota(jnp.int32, (bm, bn), 1) + k0
            prob = jnp.where(qi >= ki, prob, 0.0)
        rows = slice(q0, q0 + bm)
        dscore = (prob * dot(do_ext, v_ext)).astype(BF)
        ds_ref[slot, rows, kcols] = dscore
        dst_ref[slot, kcols, rows] = dscore.T
        p_ref[slot, rows, kcols] = prob.astype(BF)

    def grads(index, qhalf, khalf, heads, diagonal):
        for k0, kn, q0 in ((0, 256, 0), (256, 256, 256)) if diagonal else ((0, HALF, 0),):
            span = slice(q0, HALF)
            cols = slice(k0, k0 + kn)
            for pair, left_ref, right_ref in ((1, dot_ref, p_ref), (0, qt_ref, ds_ref)):
                left = jnp.concatenate([left_ref[qhalf, h, :, span] for h in heads], axis=1)
                right = jnp.concatenate([right_ref[h, span, cols] for h in heads], axis=0)
                sum_ref[index, pair, khalf, :, cols] += dot(left, right)
        for q0, qn, kn in ((0, 256, 256), (256, 256, 512)) if diagonal else ((0, HALF, HALF),):
            span = slice(q0, q0 + qn)
            for h in heads:
                dqt_ref[qhalf, h, :, span] += dot(
                    kv_ref[index, 0, khalf, :, :kn], dst_ref[h, :kn, span]
                )

    def tile(index, qhalf, khalf, diagonal):
        groups = [range(h, min(h + GROUP, count)) for h in range(0, count, GROUP)]
        for turn, heads in enumerate(groups):
            for h in heads:
                for k0 in range(0, HALF, BN):
                    for q0 in range(0, HALF, BM):
                        if diagonal and q0 + BM <= k0:
                            continue
                        scores(index, qhalf, khalf, h, h, q0, k0, BM, BN, diagonal and q0 < k0 + BN)
            if turn:
                grads(index, qhalf, khalf, groups[turn - 1], diagonal)
        grads(index, qhalf, khalf, groups[-1], diagonal)

    stat_copy.wait()
    begin(0)

    def diagonal(half, carry):
        qd_copy(half).wait()
        turn_rows(half)
        tile(0, half, half, True)
        return carry

    lax.fori_loop(0, 2, diagonal, 0)
    tile(0, 1, 0, False)
    end(0)
    for step in range(1, STEPS):
        begin(step)

        def both(turn, carry, step=step):
            second = second_ref[step]
            tile(step, jnp.where(turn == 0, 1, second), jnp.where(turn == 0, 0, second), False)
            return carry

        lax.fori_loop(0, 2, both, 0)
        end(step)

    for half in range(2):
        for h in range(count):
            for i in range(4):
                piece = dqt_ref[half, h, :, i * TOK : (i + 1) * TOK]
                dq_ref[half * 4 + i, h] = (piece * SCALE).astype(BF).T
    for copy in stores:
        copy.wait()
    if last:
        three_store.wait()


def attend(chunk, second, qd, stats, kvs, kdoc, dkv, last):
    first_head, count = sum(CHUNKS[:chunk]), CHUNKS[chunk]
    operands = [second, qd, stats]
    for sources in kvs:
        operands += sources
    operands.append(kdoc)
    operands += [] if dkv is None else [dkv]
    vmem = pl.BlockSpec(memory_space=pltpu.VMEM)
    anywhere = pl.BlockSpec(memory_space=pl.ANY)
    flops = int(8.5 * 5 * 2 * HALF * HALF * HD * count)
    sums = (STEPS, 2, 2, HD, HALF)
    shapes = [((8, count, TOK, HD), BF)]
    shapes += [(sums[1:], F32), ((3,) + sums[1:], BF), (sums[1:], BF)] if last else [(sums, F32)]
    kernel = functools.partial(
        attend_kernel,
        count,
        first_head,
        [len(sources) for sources in kvs],
        dkv is not None,
        last,
    )
    return pl.pallas_call(
        kernel,
        in_specs=[
            pl.BlockSpec(memory_space=pltpu.SMEM),
            *[anywhere] * (2 + sum(len(sources) for sources in kvs)),
            vmem,
            *[anywhere] * (dkv is not None),
        ],
        out_specs=[vmem] + [anywhere] * (len(shapes) - 1),
        out_shape=[jax.ShapeDtypeStruct(*shape) for shape in shapes],
        scratch_shapes=[
            pltpu.VMEM((2, count, HD, HALF), BF),
            pltpu.VMEM((2, count, HD, HALF), BF),
            pltpu.VMEM((2 * count, 48, HALF), BF),
            pltpu.VMEM(sums, BF),
            pltpu.VMEM((count, HALF, HALF), BF),
            pltpu.VMEM((count, HALF, HALF), BF),
            pltpu.VMEM((2, count, HD, HALF), F32),
            pltpu.VMEM((count, HALF, HALF), BF),
            pltpu.VMEM((8, 2 * count, TOK, HD), BF),
            pltpu.VMEM((8, TOK, HD), BF),
            pltpu.VMEM((sum(len(sources) for sources in kvs), 8, 2, HD, TOK), BF),
            pltpu.VMEM(sums, F32),
            pltpu.SemaphoreType.DMA((18,)),
        ]
        + ([pltpu.VMEM((3,) + sums[1:], BF)] if last else []),
        compiler_params=pltpu.CompilerParams(vmem_limit_bytes=VMEM_LIMIT),
        cost_estimate=pl.CostEstimate(
            flops=2 * flops, bytes_accessed=8 << 20, transcendentals=8 * HALF * HALF * count
        ),
        name="attend",
    )(*operands)


def join_kernel(mine_ref, inner_two_ref, inner_three_ref, to_one_ref, to_two_ref):
    to_one_ref[...] = (mine_ref[0].astype(F32) + inner_two_ref[0].astype(F32)).astype(BF)
    to_two_ref[...] = (mine_ref[1].astype(F32) + inner_three_ref[0].astype(F32)).astype(BF)


def join(mine, theirs):
    def block(steps, first):
        return pl.BlockSpec((steps, 1, 2, HD, HALF), lambda pair: (first, pair, 0, 0, 0))

    out = pl.BlockSpec((1, 2, HD, HALF), lambda pair: (pair, 0, 0, 0))
    shape = jax.ShapeDtypeStruct(mine.shape[1:], BF)
    return pl.pallas_call(
        join_kernel,
        grid=(2,),
        in_specs=[block(2, 0), block(1, 1), block(1, 2)],
        out_specs=[out, out],
        out_shape=[shape, shape],
        compiler_params=pltpu.CompilerParams(vmem_limit_bytes=VMEM_LIMIT),
        cost_estimate=pl.CostEstimate(flops=0, bytes_accessed=3 << 20, transcendentals=0),
        name="join",
    )(mine, theirs, theirs)


def total_kernel(own_ref, theirs_ref, *refs):
    *part_refs, out_ref = refs
    for half in range(2):
        total = own_ref[0, half] + theirs_ref[0, 0, half].astype(F32)
        for ref in part_refs:
            total += ref[0, half].astype(F32)
        for i in range(4):
            out_ref[half * 4 + i, 0] = total[:, i * TOK : (i + 1) * TOK].astype(BF).T


def total(own, theirs, *parts):
    part = pl.BlockSpec((1, 2, HD, HALF), lambda pair: (pair, 0, 0, 0))
    return pl.pallas_call(
        total_kernel,
        grid=(2,),
        in_specs=[
            part,
            pl.BlockSpec((1, 1, 2, HD, HALF), lambda pair: (0, pair, 0, 0, 0)),
            *[part] * len(parts),
        ],
        out_specs=pl.BlockSpec((8, 1, TOK, HD), lambda pair: (0, pair, 0, 0)),
        out_shape=jax.ShapeDtypeStruct((8, 2, TOK, HD), BF),
        compiler_params=pltpu.CompilerParams(vmem_limit_bytes=VMEM_LIMIT),
        cost_estimate=pl.CostEstimate(flops=0, bytes_accessed=4 << 20, transcendentals=0),
        name="total",
    )(own, theirs, *parts)


def unpack_q_kernel(per, *refs):
    out_ref = refs[-1]
    for u in range(per):
        h = u * HEADS_DEV
        for ref in refs[:-1]:
            for i in range(ref.shape[1]):
                out_ref[:, h * HD : (h + 1) * HD] = ref[u, i]
                h += 1


def unpack_q(parts):
    per = PACK_PER
    return pl.pallas_call(
        functools.partial(unpack_q_kernel, per),
        grid=(8 // per,),
        in_specs=[pl.BlockSpec((per,) + p.shape[1:], lambda u: (u, 0, 0, 0)) for p in parts],
        out_specs=pl.BlockSpec((TOK, per * HEADS_DEV * HD), lambda u: (0, u)),
        out_shape=jax.ShapeDtypeStruct((TOK, 8 * HEADS_DEV * HD), BF),
        compiler_params=pltpu.CompilerParams(vmem_limit_bytes=VMEM_LIMIT),
        cost_estimate=pl.CostEstimate(flops=0, bytes_accessed=4 << 20, transcendentals=0),
        name="unpack_q",
    )(*parts)


def unpack_kv_kernel(pair_ref, k_ref, v_ref):
    for u in range(8):
        k_ref[:, u * HD : (u + 1) * HD] = pair_ref[u, 0]
        v_ref[:, u * HD : (u + 1) * HD] = pair_ref[u, 1]


def unpack_kv(pair):
    shape = jax.ShapeDtypeStruct((TOK, 8 * HD), BF)
    return pl.pallas_call(
        unpack_kv_kernel,
        out_shape=[shape, shape],
        compiler_params=pltpu.CompilerParams(vmem_limit_bytes=VMEM_LIMIT),
        name="unpack_kv",
    )(pair)


def move(value, pairs):
    return lax.ppermute(value, "blk", pairs)


def exchange(value):
    return lax.all_to_all(value, "uly", split_axis=0, concat_axis=0, tiled=True)


def local(queries, key_rows, value_rows, grad_out, attn_out, log_norm, doc_ids):
    groups = lax.axis_size("blk")
    group = lax.axis_index("blk")
    kdocs = []
    for step in range(STEPS):
        owner = (group - step) % groups
        low = lax.dynamic_slice_in_dim(doc_ids, owner * HALF, HALF)
        high = lax.dynamic_slice_in_dim(doc_ids, (2 * groups - 1 - owner) * HALF, HALF)
        kdocs.append(jnp.stack([low, high]))
    kdocs = jnp.stack(kdocs)
    kdoc = jnp.where(
        kdocs[:, :, None, :] == jnp.arange(16, dtype=jnp.int32)[None, None, :, None], -1.0, 0.0
    ).astype(BF)
    second = jnp.where(group >= jnp.arange(STEPS), 0, 1).astype(jnp.int32)

    chips = range(groups // 2)
    up = [(i, (i + 1) % groups) for i in range(groups)]
    inner_up = [(2 * m, 2 * m + 1) for m in chips]
    inner_down = [(2 * m + 1, 2 * m) for m in chips]
    down = [[(2 * m, (2 * m - step) % groups) for m in chips] for step in range(STEPS)]

    kv = exchange(pack_kv(key_rows, value_rows))
    one = move(kv, up)
    two, three = (move(kv, [(b, a) for a, b in down[step]]) for step in (2, 3))
    two_inner, three_inner = (move(part, inner_up) for part in (one, two))
    kvs = [[kv], [one], [two, two_inner], [three, three_inner]]

    packed = pack_q(queries, grad_out, attn_out, log_norm.T, doc_ids.reshape(-1, TOK))
    early = exchange(packed[0])
    late, *_ = lax.optimization_barrier((packed[1], early))
    late = exchange(late)
    dq_early, dkv = attend(0, second, early, early, kvs, kdoc, None, False)
    dq_early, *_ = lax.optimization_barrier((dq_early, late))
    dq_early = exchange(dq_early)
    dq_late, own, others, far = attend(1, second, late, early, kvs, kdoc, dkv, True)

    others, dq_early = lax.optimization_barrier((others, dq_early))
    theirs = move(others, inner_down)
    from_three = move(far, down[3])
    to_one, to_two = join(others, theirs)
    dq_late, to_one, to_two = lax.optimization_barrier((dq_late, to_one, to_two))
    dq_late = exchange(dq_late)
    from_one, from_two = move(to_one, down[1]), move(to_two, down[2])
    pair = total(own, theirs, from_one, from_two, from_three)
    pair, *_ = lax.optimization_barrier((pair, dq_late))
    grad_keys, grad_values = unpack_kv(exchange(pair))
    return unpack_q([dq_early, dq_late]), grad_keys, grad_values


def solution(mesh):
    rows = P(("blk", "uly"), None)
    return jax.shard_map(
        local,
        mesh=mesh,
        in_specs=(rows, rows, rows, rows, rows, rows, P()),
        out_specs=(rows, rows, rows),
        check_vma=False,
    )
```
